32 devices in a mesh: blk: 8 (over y, x, core), uly: 4 (over z).
Axes of the slice: x: 2, y: 2, z: 4, core: 2. Of those that a mesh axis runs over, the one named last changes fastest.
Arguments:
- inputs: bfloat16 [2, 2048, 768], P(None, ('blk', 'uly')), may hold values from -6 to 6
- doc_starts: int32 [2, 2048], P(None, ('blk', 'uly')), may hold values from 0 to 2046, as said below
- out_grad: bfloat16 [2, 2048, 768], P(None, ('blk', 'uly')), may hold values from -6 to 6
- first_gain: bfloat16 [768], P('blk'), may hold values from 0.099609375 to 1.8984375
- first_bias: bfloat16 [768], P('blk'), may hold values from -3 to 3
- query_key_value_weight: bfloat16 [768, 2304], P('blk', 'uly'), may hold values from -0.21875 to 0.21875
- attention_out_weight: bfloat16 [768, 768], P('blk', 'uly'), may hold values from -6 to 6
- second_gain: bfloat16 [768], P('blk'), may hold values from 0.099609375 to 1.8984375
- second_bias: bfloat16 [768], P('blk'), may hold values from -3 to 3
- up_weight: bfloat16 [768, 3072], P('blk', 'uly'), may hold values from -0.21875 to 0.21875
- down_weight: bfloat16 [3072, 768], P('blk', 'uly'), may hold values from -0.75 to 0.75
Outputs:
- output: bfloat16 [2, 2048, 768], P(None, ('blk', 'uly'))
- grad_inputs: float32 [2, 2048, 768], P(None, ('blk', 'uly'))
- grad_first_gain: float32 [768], P('blk')
- grad_first_bias: float32 [768], P('blk')
- grad_w_qkv: float32 [768, 2304], P('blk', 'uly')
- grad_w_attn_out: float32 [768, 768], P('blk', 'uly')
- grad_second_gain: float32 [768], P('blk')
- grad_second_bias: float32 [768], P('blk')
- grad_w_up: float32 [768, 3072], P('blk', 'uly')
- grad_w_down: float32 [3072, 768], P('blk', 'uly')
The draws below stay inside these ranges and needn't reach their ends.
Inputs may be any that keep to these rules, and one draw needn't show every extreme that they name: `doc_starts`: each entry is the position, within its sequence, of the first token of that token's document: it never exceeds the token's own position, and entries never fall along a sequence.
All inputs are finite; a program needn't handle non-finite values.
Results may differ from the reference program's by a relative error of at most 0.039.
Values may be sent and summed in bfloat16 or wider, within the bound.
No kernel may reach another device: no remote copies, remote signals or barrier semaphores. Data moves between devices by JAX's collectives and lax.ppermute only.
A program may use at most 192 MiB of HBM per device.

```python
import jax
import jax.numpy as jnp
from jax import lax

D = 768
HEADS = 12
HEAD_DIM = 64
FF = 3072
SEQS = 2
TOK_DEV = 64
SEQ_LEN = 2048


def heavy_row(key):
    length = SEQ_LEN
    top_exp = max(5, (length // 4).bit_length() - 1)
    first_key, second_key = jax.random.split(key)
    doc_count = length // 4
    exponents = jax.random.randint(first_key, (doc_count,), 3, top_exp + 1)
    limits = jnp.left_shift(jnp.ones((doc_count,), jnp.int32), exponents)
    doc_sizes = 4 + jax.random.randint(second_key, (doc_count,), 0, limits)
    doc_ends = jnp.cumsum(doc_sizes)
    begins = doc_ends - doc_sizes
    positions = jnp.arange(length, dtype=jnp.int32)
    doc_index = jnp.searchsorted(doc_ends, positions, side='right')
    starts = begins[doc_index]
    return jnp.where(positions >= length - 2, length - 2, starts).astype(jnp.int32)


def span_row(key):
    length = SEQ_LEN
    first_key, second_key = jax.random.split(key)
    head_len = jax.random.randint(first_key, (), 1, TOK_DEV + 1)
    tail_len = jax.random.randint(second_key, (), 3, TOK_DEV + 1)
    positions = jnp.arange(length, dtype=jnp.int32)
    inner = jnp.where(positions < length - 2, length - tail_len, length - 2)
    middle = jnp.where(positions < length - tail_len, head_len, inner)
    return jnp.where(positions < head_len, 0, middle).astype(jnp.int32)


def draw_doc_starts(key, part):
    row_keys = jax.random.split(jax.random.fold_in(key, 11), SEQS)
    heavy = jax.vmap(heavy_row)(row_keys)
    chosen = jax.random.randint(jax.random.fold_in(key, 12), (), 0, SEQS)
    spanning = span_row(jax.random.fold_in(key, 13))
    row_ids = jnp.arange(SEQS, dtype=jnp.int32)
    return jnp.where(row_ids[:, None] == chosen, spanning[None, :], heavy).astype(jnp.int32)


def block_levels(rng, dims, shards, low, high):
    gain = 1.0
    for axis_at, shards_of in shards:
        heights = jax.random.uniform(jax.random.fold_in(jax.random.fold_in(rng, 6), axis_at), (shards_of,), jnp.float32, low / len(shards), high / len(shards))
        gain = gain * jnp.repeat(jnp.exp(heights), dims[axis_at] // shards_of).reshape((-1,) + (1,) * (len(dims) - 1 - axis_at))
    return gain


def scatter_about(key, dims, deviation, limit, pieces=(), held_as=jnp.bfloat16):
    drawn = deviation * jax.random.normal(key, dims, jnp.float32)
    if pieces:
        drawn = drawn * block_levels(key, dims, pieces, -0.22, 0.18)
    return jnp.clip(drawn, -limit, limit).astype(held_as)


def setup_inputs(seed: int = 0) -> dict:
    key_of = jax.random.split(jax.random.key(seed), 12)
    inputs = scatter_about(key_of[0], (SEQS, SEQ_LEN, D), 1.0, 6.0, ((1, 32),))
    doc_starts = draw_doc_starts(jax.random.fold_in(key_of[11], 71), 0)
    out_grad = scatter_about(key_of[2], (SEQS, SEQ_LEN, D), 1.0, 6.0, ((1, 32),))
    first_gain = jnp.clip(1.0 + 0.18 * jax.random.normal(key_of[3], (D,), jnp.float32), 0.099609375, 1.8984375).astype(jnp.bfloat16)
    first_bias = scatter_about(key_of[4], (D,), 0.5, 3.0, ((0, 8),))
    query_key_value_weight = scatter_about(key_of[5], (D, 3 * D), D ** -0.5, 0.21875, ((0, 8), (1, 4)))
    attention_out_weight = scatter_about(key_of[6], (D, D), 1.0, 6.0, ((0, 8), (1, 4)))
    second_gain = jnp.clip(1.0 + 0.18 * jax.random.normal(key_of[7], (D,), jnp.float32), 0.099609375, 1.8984375).astype(jnp.bfloat16)
    second_bias = scatter_about(key_of[8], (D,), 0.5, 3.0, ((0, 8),))
    up_weight = scatter_about(key_of[9], (D, FF), D ** -0.5, 0.21875, ((0, 8), (1, 4)))
    down_weight = scatter_about(key_of[10], (FF, D), (FF // 48) ** -0.5, 0.75, ((0, 8), (1, 4)))
    return dict(inputs=inputs, doc_starts=doc_starts, out_grad=out_grad, first_gain=first_gain, first_bias=first_bias, query_key_value_weight=query_key_value_weight, attention_out_weight=attention_out_weight, second_gain=second_gain, second_bias=second_bias, up_weight=up_weight, down_weight=down_weight)


@jax.custom_vjp
def low(v):
    return lax.optimization_barrier(v.astype(jnp.bfloat16)).astype(jnp.float32)

@jax.custom_vjp
def low_back(v):
    return v

def low_keep(v):
    return (low(v), None)

def low_pass(kept, grad):
    return (grad,)

def back_keep(v):
    return (v, None)

def back_low(kept, grad):
    return (low(grad),)
low.defvjp(low_keep, low_pass)
low_back.defvjp(back_keep, back_low)
branch_scale = 48.0 ** (-0.5)
norm_epsilon = 1e-05
neg_large = -1e+30
exact_precision = lax.Precision.HIGHEST

def layer_norm(values, gain_vec, shift_vec):
    center = values - lax.optimization_barrier(jnp.mean(values, axis=-1, keepdims=True))
    spread = lax.optimization_barrier(jnp.mean(center * center, axis=-1, keepdims=True))
    return center * lax.rsqrt(spread + norm_epsilon) * gain_vec + shift_vec

def attend(queries, key_rows, value_rows, firsts):
    length = queries.shape[0]
    block_rows = min(512, length)
    block_count = length // block_rows
    score_scale = queries.shape[-1] ** (-0.5)
    key_pos = jnp.arange(length, dtype=jnp.int32)

    def one_block(inputs):
        block_query, block_first, first_row = inputs
        query_pos = first_row + jnp.arange(block_rows, dtype=jnp.int32)
        scores = jnp.einsum('qhd,khd->hqk', block_query, key_rows, precision=exact_precision) * score_scale
        scores = low_back(scores)
        allowed = (key_pos[None, :] <= query_pos[:, None]) & (key_pos[None, :] >= block_first[:, None])
        scores = jnp.where(allowed[None], scores, neg_large)
        highest = lax.optimization_barrier(jnp.max(scores, axis=-1, keepdims=True))
        weights = jnp.where(allowed[None], jnp.exp(scores - highest), 0.0)
        probs = weights / lax.optimization_barrier(jnp.sum(weights, axis=-1, keepdims=True))
        return jnp.einsum('hqk,khd->qhd', low(probs), value_rows, precision=exact_precision)
    blocks = lax.map(jax.checkpoint(one_block), (queries.reshape((block_count, block_rows) + queries.shape[1:]), firsts.reshape(block_count, block_rows).astype(jnp.int32), jnp.arange(block_count, dtype=jnp.int32) * block_rows))
    return blocks.reshape(length, -1)

def forward(inputs, first_gain, first_bias, query_key_value_weight, attention_out_weight, second_gain, second_bias, up_weight, down_weight, doc_starts):
    seq_count, length, model_width = inputs.shape
    first_normalized = low(layer_norm(inputs, first_gain, first_bias))
    query_key_value = low_back(low(jnp.einsum('cmz,zy->cmy', first_normalized, query_key_value_weight, precision=exact_precision)))
    query_key_value = query_key_value.reshape(seq_count, length, 3, HEADS, HEAD_DIM)
    attention_mixed = jnp.stack([attend(query_key_value[index, :, 0], query_key_value[index, :, 1], query_key_value[index, :, 2], doc_starts[index]) for index in range(seq_count)])
    attention_mixed = low_back(low(attention_mixed))
    attention_projected = low_back(jnp.einsum('cmz,zy->cmy', attention_mixed, attention_out_weight, precision=exact_precision))
    middle = inputs + branch_scale * attention_projected
    second_normalized = low(layer_norm(middle, second_gain, second_bias))
    before_activation = low_back(jnp.einsum('hwb,bp->hwp', second_normalized, up_weight, precision=exact_precision))
    activation_rows = low(jax.nn.gelu(before_activation, approximate=True))
    feedforward_output = low_back(jnp.einsum('xzt,tu->xzu', activation_rows, down_weight, precision=exact_precision))
    return middle + branch_scale * feedforward_output

def reference(inputs, doc_starts, out_grad, first_gain, first_bias, query_key_value_weight, attention_out_weight, second_gain, second_bias, up_weight, down_weight):
    floats = tuple((item.astype(jnp.float32) for item in (inputs, first_gain, first_bias, query_key_value_weight, attention_out_weight, second_gain, second_bias, up_weight, down_weight)))

    def closed(inputs_f, gain_one, bias_one, qkv_f, attn_f, gain_two, bias_two, up_f, down_f):
        return forward(inputs_f, gain_one, bias_one, qkv_f, attn_f, gain_two, bias_two, up_f, down_f, doc_starts)
    result, pullback = jax.vjp(closed, *floats)
    grads = pullback(out_grad.astype(jnp.float32))
    return (result.astype(jnp.bfloat16), grads[0], grads[1], grads[2], grads[3], grads[4], grads[5], grads[6], grads[7], grads[8])
```

```python
import functools
import math

import jax
import jax.numpy as jnp
from jax import lax
from jax.experimental import pallas as pl
from jax.experimental.pallas import tpu as pltpu
from jax.sharding import PartitionSpec as P

HEAD_DIM = 64


branch_scale = 48.0 ** (-0.5)
norm_epsilon = 1e-05
neg_large = -1e30


def layer_norm(values, gain_vec, shift_vec):
    center = values - jnp.mean(values, axis=-1, keepdims=True)
    spread = jnp.mean(center * center, axis=-1, keepdims=True)
    return center * lax.rsqrt(spread + norm_epsilon) * gain_vec + shift_vec


def smooth_gate(values):
    return jax.nn.gelu(values, approximate=True)


def project(left, right):
    return jnp.einsum("stk,kn->stn", left, right, preferred_element_type=jnp.float32)


def project_back(left, right):
    return jnp.einsum("stn,kn->stk", left, right, preferred_element_type=jnp.float32)


def weight_grad(left, right):
    return jnp.einsum("stk,stn->kn", left, right, preferred_element_type=jnp.float32)


def visible(query_pos, query_first, key_pos):
    return (key_pos[None, :] <= query_pos[:, None]) & (key_pos[None, :] >= query_first[:, None])


def live_pair(query_pos, query_first, key_pos):
    return (key_pos[0] <= query_pos[-1]) & (key_pos[-1] >= query_first[0])


def forward_pair(carried, queries, key_rows, value_rows, query_pos, query_first, key_pos):
    run_max, run_sum, run_acc = carried
    score_scale = queries.shape[-1] ** (-0.5)
    scores = (
        jnp.einsum("qhd,khd->hqk", queries, key_rows, preferred_element_type=jnp.float32)
        * score_scale
    )
    allowed = visible(query_pos, query_first, key_pos)[None]
    scores = jnp.where(allowed, scores, neg_large)
    new_max = jnp.maximum(run_max, jnp.max(scores, axis=-1))
    weights = jnp.where(allowed, jnp.exp(scores - new_max[..., None]), 0.0)
    factor = jnp.exp(run_max - new_max)
    new_sum = factor * run_sum + jnp.sum(weights, axis=-1)
    attention_mixed = jnp.einsum(
        "hqk,khd->hqd", weights.astype(jnp.bfloat16), value_rows, preferred_element_type=jnp.float32
    )
    return (new_max, new_sum, factor[..., None] * run_acc + attention_mixed)


def backward_pair(
    queries,
    grad_rows,
    log_sum,
    delta_rows,
    key_rows,
    value_rows,
    query_pos,
    query_first,
    key_pos,
    want_query,
    want_keys,
):
    score_scale = queries.shape[-1] ** (-0.5)
    scores = (
        jnp.einsum("qhd,khd->hqk", queries, key_rows, preferred_element_type=jnp.float32)
        * score_scale
    )
    allowed = visible(query_pos, query_first, key_pos)[None]
    probs = jnp.where(
        allowed, jnp.exp(jnp.where(allowed, scores, neg_large) - log_sum[..., None]), 0.0
    )
    grad_probs = jnp.einsum(
        "qhd,khd->hqk", grad_rows, value_rows, preferred_element_type=jnp.float32
    )
    grad_scores = (probs * (grad_probs - delta_rows[..., None])).astype(jnp.bfloat16)
    results = ()
    if want_query:
        results = results + (
            jnp.einsum("hqk,khd->qhd", grad_scores, key_rows, preferred_element_type=jnp.float32)
            * score_scale,
        )
    if want_keys:
        grad_key_rows = (
            jnp.einsum("hqk,qhd->khd", grad_scores, queries, preferred_element_type=jnp.float32)
            * score_scale
        )
        grad_value_rows = jnp.einsum(
            "hqk,qhd->khd",
            probs.astype(jnp.bfloat16),
            grad_rows,
            preferred_element_type=jnp.float32,
        )
        results = results + (grad_key_rows, grad_value_rows)
    return results


def each_block(update, carried, arrays, row_limit):
    total_rows = arrays[0].shape[1]
    span_rows = math.gcd(total_rows, row_limit)
    block_count = total_rows // span_rows
    split_arrays = tuple(
        (
            jnp.swapaxes(
                member.reshape((member.shape[0], block_count, span_rows) + member.shape[2:]), 0, 1
            )
            for member in arrays
        )
    )

    def advance(running, inputs):
        number, blocks = inputs
        return (update(running, blocks, number * span_rows), None)

    result, unused = lax.scan(
        advance, carried, (jnp.arange(block_count, dtype=jnp.int32), split_arrays)
    )
    return result


def local_general(
    inputs,
    doc_starts,
    out_grad,
    first_gain,
    first_bias,
    query_key_value_weight,
    attention_out_weight,
    second_gain,
    second_bias,
    up_weight,
    down_weight,
):
    groups = lax.axis_size("uly")
    cycle_place = lax.axis_index("blk")
    seq_count, tok_dev, model_width = inputs.shape
    block_rows = tok_dev * groups
    group_width = model_width // groups
    heads_here = group_width // HEAD_DIM
    qkv_cols, attn_cols, up_cols, down_cols = (
        lax.all_gather(query_key_value_weight, "uly", axis=1, tiled=True),
        lax.all_gather(attention_out_weight, "uly", axis=1, tiled=True),
        lax.all_gather(up_weight, "uly", axis=1, tiled=True),
        lax.all_gather(down_weight, "uly", axis=1, tiled=True),
    )
    gathered = (
        lax.all_gather(qkv_cols, "blk", axis=0, tiled=True),
        lax.all_gather(attn_cols, "blk", axis=0, tiled=True),
        lax.all_gather(up_cols, "blk", axis=0, tiled=True),
        lax.all_gather(down_cols, "blk", axis=0, tiled=True),
        lax.all_gather(first_gain, "blk", axis=0, tiled=True),
        lax.all_gather(first_bias, "blk", axis=0, tiled=True),
        lax.all_gather(second_gain, "blk", axis=0, tiled=True),
        lax.all_gather(second_bias, "blk", axis=0, tiled=True),
    )
    wide_qkv, wide_attn, wide_up, wide_down = (gathered[0], gathered[1], gathered[2], gathered[3])
    gain_one = gathered[4].astype(jnp.float32)
    bias_one = gathered[5].astype(jnp.float32)
    gain_two = gathered[6].astype(jnp.float32)
    bias_two = gathered[7].astype(jnp.float32)
    residual = inputs.astype(jnp.float32)
    first_normalized, norm_one_back = jax.vjp(layer_norm, residual, gain_one, bias_one)
    normed_low = first_normalized.astype(jnp.bfloat16)
    query_key_value = project(normed_low, wide_qkv).astype(jnp.bfloat16)
    packed = query_key_value.reshape(seq_count, tok_dev, 3, groups, group_width)
    spread = lax.all_to_all(packed, "uly", split_axis=3, concat_axis=1, tiled=True)
    query_flat = spread[:, :, 0, 0]
    key_flat = spread[:, :, 1, 0]
    value_flat = spread[:, :, 2, 0]
    queries = query_flat.reshape(seq_count, block_rows, heads_here, HEAD_DIM)
    key_heads = key_flat.reshape(seq_count, block_rows, heads_here, HEAD_DIM)
    value_heads = value_flat.reshape(seq_count, block_rows, heads_here, HEAD_DIM)
    firsts = lax.all_gather(doc_starts, "uly", axis=1, tiled=True)
    query_pos = cycle_place * block_rows + jnp.arange(block_rows, dtype=jnp.int32)

    def forward_update(carried, blocks, first_row):
        span_rows = blocks[0].shape[1]
        key_pos = first_row + jnp.arange(span_rows, dtype=jnp.int32)
        new_max, new_sum, new_acc = ([], [], [])
        for seq_index in range(seq_count):
            one_state = (carried[0][seq_index], carried[1][seq_index], carried[2][seq_index])
            key_one = blocks[0][seq_index].reshape(span_rows, heads_here, HEAD_DIM)
            value_one = blocks[1][seq_index].reshape(span_rows, heads_here, HEAD_DIM)

            def advance_state(state_in):
                return forward_pair(
                    state_in,
                    queries[seq_index],
                    key_one,
                    value_one,
                    query_pos,
                    firsts[seq_index],
                    key_pos,
                )

            def keep_state(state_in):
                return state_in

            updated = lax.cond(
                live_pair(query_pos, firsts[seq_index], key_pos),
                advance_state,
                keep_state,
                one_state,
            )
            new_max.append(updated[0])
            new_sum.append(updated[1])
            new_acc.append(updated[2])
        return (jnp.stack(new_max), jnp.stack(new_sum), jnp.stack(new_acc))

    start_state = (
        jnp.full((seq_count, heads_here, block_rows), neg_large, jnp.float32),
        jnp.zeros((seq_count, heads_here, block_rows), jnp.float32),
        jnp.zeros((seq_count, heads_here, block_rows, HEAD_DIM), jnp.float32),
    )
    run_max, run_sum, run_acc = each_block(
        forward_update,
        start_state,
        (
            lax.all_gather(key_flat, "blk", axis=1, tiled=True),
            lax.all_gather(value_flat, "blk", axis=1, tiled=True),
        ),
        block_rows,
    )
    attn_heads = jnp.swapaxes(run_acc / run_sum[..., None], 1, 2)
    log_sum = run_max + jnp.log(run_sum)
    attn_low = attn_heads.reshape(seq_count, block_rows, 1, group_width).astype(jnp.bfloat16)
    back_rows = lax.all_to_all(attn_low, "uly", split_axis=1, concat_axis=2, tiled=True).reshape(
        seq_count, tok_dev, model_width
    )
    attention_projected = project(back_rows, wide_attn)
    middle = residual + branch_scale * attention_projected
    second_normalized, norm_two_back = jax.vjp(layer_norm, middle, gain_two, bias_two)
    normed_two_low = second_normalized.astype(jnp.bfloat16)
    before_activation = project(normed_two_low, wide_up)
    act_value, gate_back = jax.vjp(smooth_gate, before_activation)
    act_low = act_value.astype(jnp.bfloat16)
    feedforward_output = project(act_low, wide_down)
    output = (middle + branch_scale * feedforward_output).astype(jnp.bfloat16)
    grad_res = out_grad.astype(jnp.float32)
    grad_branch = (branch_scale * grad_res).astype(jnp.bfloat16)
    grad_w_down = weight_grad(act_low, grad_branch)
    grad_act = project_back(grad_branch, wide_down)
    grad_pre = gate_back(grad_act)[0].astype(jnp.bfloat16)
    grad_w_up = weight_grad(normed_two_low, grad_pre)
    grad_norm_two = project_back(grad_pre, wide_up)
    grad_mid_part, grad_gain_two, grad_bias_two = norm_two_back(grad_norm_two)
    grad_middle = grad_res + grad_mid_part
    grad_attn = (branch_scale * grad_middle).astype(jnp.bfloat16)
    grad_w_attn = weight_grad(back_rows, grad_attn)
    grad_mixed = project_back(grad_attn, wide_attn).astype(jnp.bfloat16)
    grad_spread = lax.all_to_all(
        grad_mixed.reshape(seq_count, tok_dev, groups, group_width),
        "uly",
        split_axis=2,
        concat_axis=1,
        tiled=True,
    )
    grad_flat = grad_spread[:, :, 0]
    grad_heads = grad_flat.reshape(seq_count, block_rows, heads_here, HEAD_DIM)
    delta_rows = jnp.swapaxes(jnp.sum(attn_heads * grad_heads.astype(jnp.float32), axis=-1), 1, 2)

    def query_update(grad_query, blocks, first_row):
        span_rows = blocks[0].shape[1]
        key_pos = first_row + jnp.arange(span_rows, dtype=jnp.int32)
        new_terms = []
        for seq_index in range(seq_count):
            key_one = blocks[0][seq_index].reshape(span_rows, heads_here, HEAD_DIM)
            value_one = blocks[1][seq_index].reshape(span_rows, heads_here, HEAD_DIM)

            def query_compute_terms(unused):
                return backward_pair(
                    queries[seq_index],
                    grad_heads[seq_index],
                    log_sum[seq_index],
                    delta_rows[seq_index],
                    key_one,
                    value_one,
                    query_pos,
                    firsts[seq_index],
                    key_pos,
                    True,
                    False,
                )[0]

            def query_zero_terms(unused):
                return jnp.zeros((block_rows, heads_here, HEAD_DIM), jnp.float32)

            new_terms.append(
                grad_query[seq_index]
                + lax.cond(
                    live_pair(query_pos, firsts[seq_index], key_pos),
                    query_compute_terms,
                    query_zero_terms,
                    0,
                )
            )
        return jnp.stack(new_terms)

    grad_query = each_block(
        query_update,
        jnp.zeros((seq_count, block_rows, heads_here, HEAD_DIM), jnp.float32),
        (
            lax.all_gather(key_flat, "blk", axis=1, tiled=True),
            lax.all_gather(value_flat, "blk", axis=1, tiled=True),
        ),
        block_rows,
    )

    def key_update(carried, blocks, first_row):
        span_rows = blocks[0].shape[1]
        other_pos = first_row + jnp.arange(span_rows, dtype=jnp.int32)
        key_sums, value_sums = ([], [])
        for seq_index in range(seq_count):
            query_one = blocks[0][seq_index].reshape(span_rows, heads_here, HEAD_DIM)
            grad_one = blocks[1][seq_index].reshape(span_rows, heads_here, HEAD_DIM)
            lse_one = jnp.transpose(blocks[2][seq_index])
            delta_one = jnp.transpose(blocks[3][seq_index])
            first_one = blocks[4][seq_index]

            def key_compute_terms(unused):
                return backward_pair(
                    query_one,
                    grad_one,
                    lse_one,
                    delta_one,
                    key_heads[seq_index],
                    value_heads[seq_index],
                    other_pos,
                    first_one,
                    query_pos,
                    False,
                    True,
                )

            def key_zero_terms(unused):
                zero_rows = jnp.zeros((block_rows, heads_here, HEAD_DIM), jnp.float32)
                return (zero_rows, zero_rows)

            terms = lax.cond(
                live_pair(other_pos, first_one, query_pos), key_compute_terms, key_zero_terms, 0
            )
            key_sums.append(carried[0][seq_index] + terms[0])
            value_sums.append(carried[1][seq_index] + terms[1])
        return (jnp.stack(key_sums), jnp.stack(value_sums))

    zero_heads = jnp.zeros((seq_count, block_rows, heads_here, HEAD_DIM), jnp.float32)
    grad_keys, grad_values = each_block(
        key_update,
        (zero_heads, zero_heads),
        (
            lax.all_gather(query_flat, "blk", axis=1, tiled=True),
            lax.all_gather(grad_flat, "blk", axis=1, tiled=True),
            lax.all_gather(
                jnp.swapaxes(log_sum, 1, 2).astype(jnp.bfloat16), "blk", axis=1, tiled=True
            ).astype(jnp.float32),
            lax.all_gather(
                jnp.swapaxes(delta_rows, 1, 2).astype(jnp.bfloat16), "blk", axis=1, tiled=True
            ).astype(jnp.float32),
            lax.all_gather(firsts, "blk", axis=1, tiled=True),
        ),
        block_rows,
    )
    grad_query_flat = grad_query.reshape(seq_count, block_rows, group_width)
    grad_key_flat = grad_keys.reshape(seq_count, block_rows, group_width)
    grad_value_flat = grad_values.reshape(seq_count, block_rows, group_width)
    stacked = jnp.stack([grad_query_flat, grad_key_flat, grad_value_flat], axis=2).astype(
        jnp.bfloat16
    )
    stacked = stacked.reshape(seq_count, block_rows, 3, 1, group_width)
    grad_qkv = lax.all_to_all(stacked, "uly", split_axis=1, concat_axis=3, tiled=True).reshape(
        seq_count, tok_dev, 3 * model_width
    )
    grad_w_qkv = weight_grad(normed_low, grad_qkv)
    grad_norm_one = project_back(grad_qkv, wide_qkv)
    grad_in_part, grad_gain_one, grad_bias_one = norm_one_back(grad_norm_one)
    grad_inputs = grad_middle + grad_in_part
    column_sums = (
        lax.psum_scatter(
            grad_w_qkv.astype(jnp.bfloat16), "uly", scatter_dimension=1, tiled=True
        ).astype(jnp.float32),
        lax.psum_scatter(
            grad_w_attn.astype(jnp.bfloat16), "uly", scatter_dimension=1, tiled=True
        ).astype(jnp.float32),
        lax.psum_scatter(
            grad_w_up.astype(jnp.bfloat16), "uly", scatter_dimension=1, tiled=True
        ).astype(jnp.float32),
        lax.psum_scatter(
            grad_w_down.astype(jnp.bfloat16), "uly", scatter_dimension=1, tiled=True
        ).astype(jnp.float32),
        lax.psum_scatter(
            jnp.tile(grad_gain_one, groups).astype(jnp.bfloat16),
            "uly",
            scatter_dimension=0,
            tiled=True,
        ).astype(jnp.float32),
        lax.psum_scatter(
            jnp.tile(grad_bias_one, groups).astype(jnp.bfloat16),
            "uly",
            scatter_dimension=0,
            tiled=True,
        ).astype(jnp.float32),
        lax.psum_scatter(
            jnp.tile(grad_gain_two, groups).astype(jnp.bfloat16),
            "uly",
            scatter_dimension=0,
            tiled=True,
        ).astype(jnp.float32),
        lax.psum_scatter(
            jnp.tile(grad_bias_two, groups).astype(jnp.bfloat16),
            "uly",
            scatter_dimension=0,
            tiled=True,
        ).astype(jnp.float32),
    )
    owned = (
        lax.psum_scatter(column_sums[0], "blk", scatter_dimension=0, tiled=True),
        lax.psum_scatter(column_sums[1], "blk", scatter_dimension=0, tiled=True),
        lax.psum_scatter(column_sums[2], "blk", scatter_dimension=0, tiled=True),
        lax.psum_scatter(column_sums[3], "blk", scatter_dimension=0, tiled=True),
        lax.psum_scatter(column_sums[4], "blk", scatter_dimension=0, tiled=True),
        lax.psum_scatter(column_sums[5], "blk", scatter_dimension=0, tiled=True),
        lax.psum_scatter(column_sums[6], "blk", scatter_dimension=0, tiled=True),
        lax.psum_scatter(column_sums[7], "blk", scatter_dimension=0, tiled=True),
    )
    return (
        output,
        grad_inputs,
        owned[4],
        owned[5],
        owned[0],
        owned[1],
        owned[6],
        owned[7],
        owned[2],
        owned[3],
    )


UNITS = 4
FULL_TOK = 2048
TILE = 256
LOG2E = 1.4426950408889634


def fits_fast(mesh):
    return dict(mesh.shape) == {"blk": 8, "uly": 4}


def halves_in(rows):
    half = rows.shape[-2] // 2
    return jnp.concatenate([rows[..., :half, :], rows[..., half:, :]], axis=-1)


def halves_out(packed):
    half = packed.shape[-1] // 2
    return jnp.concatenate([packed[..., :half], packed[..., half:]], axis=-2)


def attn_forward_kernel(pack_ref, first_ref, out_ref, log_ref, q_rows, k_rows, v_cols):
    tiles = FULL_TOK // TILE
    scale = LOG2E * HEAD_DIM**-0.5
    for t in range(tiles):
        rows = pl.ds(t * TILE, TILE)
        pair = pack_ref[t, :TILE, :]
        q_rows[rows, :] = pair[:, :HEAD_DIM]
        k_rows[rows, :] = pair[:, HEAD_DIM:]
        v_cols[:, rows] = halves_out(pack_ref[t, TILE:, :]).T
    key_iota = lax.broadcasted_iota(jnp.int32, (TILE, TILE), 0)
    query_iota = lax.broadcasted_iota(jnp.int32, (TILE, TILE), 1)
    causal = key_iota <= query_iota
    for i in range(tiles):
        q_rows_i = pl.ds(i * TILE, TILE)
        queries = q_rows[q_rows_i, :]
        first = first_ref[:, q_rows_i]
        top = total = acc = None
        for j in range(i, -1, -1):
            k_at = pl.ds(j * TILE, TILE)
            scores = lax.dot_general(
                k_rows[k_at, :], queries, (((1,), (1,)), ((), ())), preferred_element_type=jnp.float32
            )
            allowed = key_iota >= first - j * TILE
            if j == i:
                allowed = allowed & causal
            scores = jnp.where(allowed, scores * scale, neg_large)
            tile_top = jnp.max(scores, axis=0, keepdims=True)
            new_top = tile_top if top is None else jnp.maximum(top, tile_top)
            weights = jnp.exp2(scores - new_top)
            tile_sum = jnp.sum(weights, axis=0, keepdims=True)
            tile_acc = jnp.dot(
                v_cols[:, k_at], weights.astype(jnp.bfloat16), preferred_element_type=jnp.float32
            )
            if top is None:
                total, acc = tile_sum, tile_acc
            else:
                factor = jnp.exp2(top - new_top)
                total = factor * total + tile_sum
                acc = factor * acc + tile_acc
            top = new_top
        out_ref[:, q_rows_i] = acc / total
        log_ref[:, q_rows_i] = top + jnp.log2(total)


def attn_backward_kernel(
    pack_ref, grad_ref, out_cols, log_ref, first_ref, dpack_ref, q_rows, k_rows, v_rows, g_rows, k_cols, delta, dq_cols
):
    tiles = FULL_TOK // TILE
    scale = LOG2E * HEAD_DIM**-0.5
    for t in range(tiles):
        rows = pl.ds(t * TILE, TILE)
        pair = pack_ref[t, :TILE, :]
        q_rows[rows, :] = pair[:, :HEAD_DIM]
        keys = pair[:, HEAD_DIM:]
        k_rows[rows, :] = keys
        k_cols[:, rows] = keys.T
        v_rows[rows, :] = halves_out(pack_ref[t, TILE:, :])
        g_tile = halves_out(grad_ref[t])
        g_rows[rows, :] = g_tile
        g_cols = g_tile.T.astype(jnp.float32)
        delta[:, rows] = jnp.sum(g_cols * out_cols[:, rows], axis=0, keepdims=True)
    key_iota = lax.broadcasted_iota(jnp.int32, (TILE, TILE), 0)
    query_iota = lax.broadcasted_iota(jnp.int32, (TILE, TILE), 1)
    causal = key_iota <= query_iota
    across = (((1,), (1,)), ((), ()))
    for j in range(tiles):
        k_at = pl.ds(j * TILE, TILE)
        keys, values, keys_t = k_rows[k_at, :], v_rows[k_at, :], k_cols[:, k_at]
        dk = dv = None
        for i in range(j, tiles):
            q_at = pl.ds(i * TILE, TILE)
            queries, grads = q_rows[q_at, :], g_rows[q_at, :]
            scores = lax.dot_general(keys, queries, across, preferred_element_type=jnp.float32)
            allowed = key_iota >= first_ref[:, q_at] - j * TILE
            if i == j:
                allowed = allowed & causal
            probs = jnp.exp2(jnp.where(allowed, scores * scale - log_ref[:, q_at], neg_large))
            dprobs = lax.dot_general(values, grads, across, preferred_element_type=jnp.float32)
            dscores = (probs * (dprobs - delta[:, q_at])).astype(jnp.bfloat16)
            dv_tile = jnp.dot(probs.astype(jnp.bfloat16), grads, preferred_element_type=jnp.float32)
            dk_tile = jnp.dot(dscores, queries, preferred_element_type=jnp.float32)
            dq_tile = jnp.dot(keys_t, dscores, preferred_element_type=jnp.float32)
            dv = dv_tile if dv is None else dv + dv_tile
            dk = dk_tile if dk is None else dk + dk_tile
            if j == 0:
                dq_cols[:, q_at] = dq_tile
            else:
                dq_cols[:, q_at] += dq_tile
        dq = (dq_cols[:, k_at] * HEAD_DIM**-0.5).T
        dpack_ref[j, :TILE, :HEAD_DIM] = dq.astype(jnp.bfloat16)
        dpack_ref[j, :TILE, HEAD_DIM:] = (dk * HEAD_DIM**-0.5).astype(jnp.bfloat16)
        dpack_ref[j, TILE:, :] = halves_in(dv.astype(jnp.bfloat16))


def whole(count):
    return [pl.BlockSpec(memory_space=pltpu.VMEM)] * count


def attn_forward(pack, first_row):
    return pl.pallas_call(
        attn_forward_kernel,
        out_shape=(
            jax.ShapeDtypeStruct((HEAD_DIM, FULL_TOK), jnp.float32),
            jax.ShapeDtypeStruct((1, FULL_TOK), jnp.float32),
        ),
        in_specs=whole(2),
        out_specs=tuple(whole(2)),
        scratch_shapes=[
            pltpu.VMEM((FULL_TOK, HEAD_DIM), jnp.bfloat16),
            pltpu.VMEM((FULL_TOK, HEAD_DIM), jnp.bfloat16),
            pltpu.VMEM((HEAD_DIM, FULL_TOK), jnp.bfloat16),
        ],
        compiler_params=pltpu.CompilerParams(vmem_limit_bytes=40 * 2**20),
        cost_estimate=pl.CostEstimate(flops=2**30, bytes_accessed=2**21, transcendentals=2**21),
        name="attn_forward",
    )(pack, first_row)


def attn_backward(pack, grads, out_cols, log_row, first_row):
    rows = pltpu.VMEM((FULL_TOK, HEAD_DIM), jnp.bfloat16)
    return pl.pallas_call(
        attn_backward_kernel,
        out_shape=jax.ShapeDtypeStruct(pack.shape, jnp.bfloat16),
        in_specs=whole(5),
        out_specs=whole(1)[0],
        scratch_shapes=[
            rows,
            rows,
            rows,
            rows,
            pltpu.VMEM((HEAD_DIM, FULL_TOK), jnp.bfloat16),
            pltpu.VMEM((1, FULL_TOK), jnp.float32),
            pltpu.VMEM((HEAD_DIM, FULL_TOK), jnp.float32),
        ],
        compiler_params=pltpu.CompilerParams(vmem_limit_bytes=40 * 2**20),
        cost_estimate=pl.CostEstimate(flops=2**31, bytes_accessed=2**22, transcendentals=2**21),
        name="attn_backward",
    )(pack, grads, out_cols, log_row, first_row)


def pick(stacked, index):
    return lax.dynamic_index_in_dim(stacked, index, 0, keepdims=False)


def swap_z(value, shift):
    return lax.ppermute(value, "uly", [(i, i ^ shift) for i in range(4)])


def sum_z(parts, place):
    total = pick(parts, place).astype(jnp.float32)
    for shift in (1, 2, 3):
        total = total + swap_z(pick(parts, place ^ shift), shift).astype(jnp.float32)
    return total


SEND_A = ((0, 1), (1, 3), (2, 0), (3, 2))
SEND_B = ((0, 2), (1, 0), (2, 3), (3, 1))
PART_SELF, PART_A, PART_B = (0, 2, 0, 2), (1, 0, 2, 1), (2, 1, 1, 0)
ORDER = ((0, 2, 1), (1, 0, 2), (2, 0, 1), (1, 2, 0))


def at_place(table, place):
    return pick(jnp.asarray(table, jnp.int32), place)


def heads_of_place(shard, place):
    groups = jnp.moveaxis(shard.reshape(shard.shape[0], 3, 192), 1, 0)
    got = jnp.stack(
        [
            pick(groups, at_place(PART_SELF, place)),
            lax.ppermute(pick(groups, at_place(PART_A, place)), "uly", SEND_A),
            lax.ppermute(pick(groups, at_place(PART_B, place)), "uly", SEND_B),
        ]
    )
    order = at_place(ORDER, place)
    parts = jnp.stack([pick(got, order[p]) for p in range(3)], axis=1)
    return parts.reshape(-1, 3, 3, HEAD_DIM).transpose(0, 2, 1, 3).reshape(-1, 576)


def back_to_place(value, place):
    parts = value.reshape(-1, 3, 3, HEAD_DIM).transpose(2, 0, 1, 3).reshape(3, -1, 192)
    order = at_place(ORDER, place)
    inverse = [
        jnp.where(order[0] == n, 0, jnp.where(order[1] == n, 1, 2)) for n in range(3)
    ]
    own = pick(parts, inverse[0])
    from_a = lax.ppermute(pick(parts, inverse[1]), "uly", [(d, s) for s, d in SEND_A])
    from_b = lax.ppermute(pick(parts, inverse[2]), "uly", [(d, s) for s, d in SEND_B])
    got = jnp.stack([own, from_a, from_b])
    where_self, where_a = at_place(PART_SELF, place), at_place(PART_A, place)
    groups = [
        pick(got, jnp.where(where_self == g, 0, jnp.where(where_a == g, 1, 2))) for g in range(3)
    ]
    return jnp.concatenate(groups, axis=1)


DOWN_MOVES = [(b * 4 + u, (2 * u + b % 2) * 4 + b // 2) for b in range(8) for u in range(4)]


def norm_stats(values):
    center = values - jnp.mean(values, axis=-1, keepdims=True)
    scale = lax.rsqrt(jnp.mean(center * center, axis=-1, keepdims=True) + norm_epsilon)
    return center * scale, scale


def norm_back(grad_out, normal, scale, gain):
    grad_normal = grad_out * gain
    mean_one = jnp.mean(grad_normal, axis=-1, keepdims=True)
    mean_two = jnp.mean(grad_normal * normal, axis=-1, keepdims=True)
    return (grad_normal - mean_one - normal * mean_two) * scale


def dot32(left, right, dims):
    return lax.dot_general(left, right, (dims, ((), ())), preferred_element_type=jnp.float32)


def local_fast(
    inputs,
    doc_starts,
    out_grad,
    first_gain,
    first_bias,
    query_key_value_weight,
    attention_out_weight,
    second_gain,
    second_bias,
    up_weight,
    down_weight,
):
    bf16, f32 = jnp.bfloat16, jnp.float32
    blk, uly = lax.axis_index("blk"), lax.axis_index("uly")
    width = inputs.shape[2]

    qkv_shard = heads_of_place(query_key_value_weight, uly)
    vectors = jnp.stack([first_gain, first_bias, second_gain, second_bias], axis=1)
    qkv_shard = jnp.concatenate([qkv_shard, jnp.pad(vectors, ((0, 0), (0, 60)))], axis=1)
    qkv_full = lax.all_gather(qkv_shard, "blk", axis=0, tiled=True)
    w_qkv = qkv_full[:, :576]
    vectors = qkv_full[:, 576:580].astype(f32).T
    gain_one, bias_one, gain_two, bias_two = (vectors[n : n + 1] for n in range(4))
    starts = lax.all_gather(doc_starts, ("blk", "uly"), axis=1, tiled=True)
    first_row = jnp.where(blk < 4, starts[0:1], starts[1:2])
    x_rows = lax.all_gather(inputs, "uly", axis=1, tiled=True)
    out_shard = lax.all_gather(attention_out_weight, "uly", axis=1, tiled=True)
    down_shard = lax.ppermute(down_weight, ("blk", "uly"), DOWN_MOVES)
    w_out = lax.all_gather(out_shard, "blk", axis=0, tiled=True)
    w_up = lax.all_gather(up_weight, "blk", axis=0, tiled=True)
    w_down = lax.all_gather(down_shard, "blk", axis=0)
    w_down = w_down.reshape(4, 2, 384, 192).transpose(1, 2, 0, 3).reshape(768, 768)
    g_rows = lax.all_gather(out_grad, "uly", axis=1, tiled=True)

    residual = x_rows.astype(f32).reshape(512, width)
    normal_one, scale_one = norm_stats(residual)
    normed_one = (normal_one * gain_one + bias_one).astype(bf16)
    qkv = dot32(normed_one, w_qkv, ((1,), (0,))).astype(bf16).reshape(2, 256, 3, 192)
    qkv = jnp.concatenate([qkv, qkv[:, :, 2:]], axis=2).transpose(0, 2, 1, 3)
    pack = jnp.concatenate([qkv[..., :128], halves_in(qkv[..., 128:])], axis=2)
    pack = lax.all_to_all(pack.reshape(8, 384, 128), "blk", 0, 0, tiled=True)

    out_cols, log_row = attn_forward(pack, first_row)
    attn_pack = halves_in(
        out_cols.astype(bf16).reshape(HEAD_DIM, 8, 256).transpose(1, 2, 0)
    )
    attn_pack = lax.all_to_all(attn_pack, "blk", 0, 0, tiled=True)
    attn_pack = attn_pack.reshape(2, 4, 128, 128)[:, :3]
    mixed = lax.all_gather(attn_pack, "uly", axis=0)
    mixed = halves_out(mixed)
    mixed = mixed.transpose(1, 3, 0, 2, 4).reshape(512, width)

    middle = residual + branch_scale * dot32(mixed, w_out, ((1,), (0,)))
    normal_two, scale_two = norm_stats(middle)
    normed_two = (normal_two * gain_two + bias_two).astype(bf16)
    pre_act = dot32(normed_two, w_up, ((1,), (0,)))
    act, gate_back = jax.vjp(smooth_gate, pre_act)
    act = act.astype(bf16)
    grad_branch = (branch_scale * g_rows.astype(f32)).astype(bf16).reshape(512, width)
    grad_act = dot32(grad_branch, w_down, ((1,), (1,)))
    grad_pre = gate_back(grad_act)[0].astype(bf16)
    grad_norm_two = dot32(grad_pre, w_up, ((1,), (1,))).astype(bf16)
    chunks = lambda rows: rows.reshape(2, 4, 64, width).transpose(1, 0, 2, 3)
    grad_norm_two = sum_z(chunks(grad_norm_two), uly)
    feed = dot32(act, w_down, ((1,), (0,))).astype(bf16)
    g_w_up = dot32(normed_two, grad_pre, ((0,), (0,)))
    g_w_down = dot32(act, grad_branch, ((0,), (0,)))
    g_w_down = g_w_down.reshape(2, 384, 4, 192).transpose(2, 0, 1, 3).reshape(8 * 384, 192)
    g_w_up = lax.psum_scatter(g_w_up.astype(bf16), "blk", scatter_dimension=0, tiled=True)
    g_w_down = lax.psum_scatter(g_w_down.astype(bf16), "blk", scatter_dimension=0, tiled=True)
    back_moves = [(d, s) for s, d in DOWN_MOVES]
    g_w_down = lax.ppermute(g_w_down, ("blk", "uly"), back_moves).astype(f32)

    own = lambda rows: pick(chunks(rows), uly)
    middle_own = own(middle)
    output = (middle_own + branch_scale * sum_z(chunks(feed), uly)).astype(bf16)
    normal_two_own, scale_two_own = norm_stats(middle_own)
    grad_middle = out_grad.astype(f32) + norm_back(
        grad_norm_two, normal_two_own, scale_two_own, gain_two
    )
    d_gain_two = jnp.sum(grad_norm_two * normal_two_own, axis=(0, 1))
    d_bias_two = jnp.sum(grad_norm_two, axis=(0, 1))
    grad_attn = (branch_scale * grad_middle).astype(bf16)
    grad_mixed = dot32(grad_attn, w_out, ((2,), (1,))).astype(bf16)
    grad_mixed = halves_in(grad_mixed.reshape(2, 64, 4, 3, HEAD_DIM).transpose(2, 0, 3, 1, 4))
    grad_mixed = lax.all_to_all(grad_mixed, "uly", 0, 0, tiled=True)
    grad_mixed = halves_out(grad_mixed).transpose(1, 2, 0, 3, 4).reshape(2, 3, 256, HEAD_DIM)
    grad_mixed = jnp.concatenate([grad_mixed, grad_mixed[:, 2:]], axis=1)
    grad_pack = halves_in(grad_mixed).reshape(8, 128, 128)
    grad_pack = lax.all_to_all(grad_pack, "blk", 0, 0, tiled=True)

    grad_cols = grad_attn.reshape(2, 64, 4, 192).transpose(2, 0, 1, 3)
    grad_cols = lax.all_to_all(grad_cols, "uly", 0, 0, tiled=True)
    grad_cols = grad_cols.transpose(1, 0, 2, 3).reshape(512, 192)
    g_w_out = dot32(mixed, grad_cols, ((0,), (0,)))
    g_w_out = lax.psum_scatter(g_w_out.astype(bf16), "blk", scatter_dimension=0, tiled=True)

    dpack = attn_backward(pack, grad_pack, out_cols, log_row, first_row)
    dpack = lax.all_to_all(dpack, "blk", 0, 0, tiled=True)
    dpack = dpack.reshape(2, 4, 384, 128)[:, :3]
    grad_qkv = jnp.concatenate([dpack[:, :, :256], halves_out(dpack[:, :, 256:])], axis=3)
    grad_qkv = grad_qkv.transpose(0, 2, 1, 3).reshape(512, 576)
    grad_norm_one = dot32(grad_qkv, w_qkv, ((1,), (1,)))
    d_gain_one = jnp.sum(grad_norm_one * normal_one, axis=0)
    d_bias_one = jnp.sum(grad_norm_one, axis=0)
    grad_norm_one = sum_z(chunks(grad_norm_one.astype(bf16)), uly)
    normal_own, scale_own = norm_stats(inputs.astype(f32))
    grad_inputs = grad_middle + norm_back(grad_norm_one, normal_own, scale_own, gain_one)

    g_w_qkv = dot32(normed_one, grad_qkv, ((0,), (0,)))
    d_vectors = jnp.stack([d_gain_one, d_bias_one, d_gain_two, d_bias_two], axis=1)
    tail = jnp.concatenate([g_w_qkv, jnp.pad(d_vectors, ((0, 0), (0, 60)))], axis=1)
    tail = lax.psum_scatter(tail.astype(bf16), "blk", scatter_dimension=0, tiled=True).astype(f32)
    g_w_qkv = back_to_place(tail[:, :576], uly)
    d_vectors = tail[:, 576:580]
    d_vectors = d_vectors + sum(swap_z(d_vectors, shift) for shift in (1, 2, 3))
    return (
        output,
        grad_inputs,
        d_vectors[:, 0],
        d_vectors[:, 1],
        g_w_qkv,
        g_w_out.astype(f32),
        d_vectors[:, 2],
        d_vectors[:, 3],
        g_w_up.astype(f32),
        g_w_down,
    )


def solution(mesh):
    local = local_fast if fits_fast(mesh) else local_general
    placed = (
        P(None, ("blk", "uly"), None),
        P(None, ("blk", "uly")),
        P(None, ("blk", "uly"), None),
        P("blk"),
        P("blk"),
        P("blk", "uly"),
        P("blk", "uly"),
        P("blk"),
        P("blk"),
        P("blk", "uly"),
        P("blk", "uly"),
    )
    return jax.shard_map(
        local,
        mesh=mesh,
        in_specs=placed,
        out_specs=(
            P(None, ("blk", "uly"), None),
            P(None, ("blk", "uly"), None),
            P("blk"),
            P("blk"),
            P("blk", "uly"),
            P("blk", "uly"),
            P("blk"),
            P("blk"),
            P("blk", "uly"),
            P("blk", "uly"),
        ),
        check_vma=False,
    )
```

```python
import functools
import math

import jax
import jax.numpy as jnp
from jax import lax
from jax.experimental import pallas as pl
from jax.experimental.pallas import tpu as pltpu
from jax.sharding import PartitionSpec as P

HEAD_DIM = 64


branch_scale = 48.0 ** (-0.5)
norm_epsilon = 1e-05
neg_large = -1e30


def layer_norm(values, gain_vec, shift_vec):
    center = values - jnp.mean(values, axis=-1, keepdims=True)
    spread = jnp.mean(center * center, axis=-1, keepdims=True)
    return center * lax.rsqrt(spread + norm_epsilon) * gain_vec + shift_vec


def smooth_gate(values):
    return jax.nn.gelu(values, approximate=True)


def project(left, right):
    return jnp.einsum("stk,kn->stn", left, right, preferred_element_type=jnp.float32)


def project_back(left, right):
    return jnp.einsum("stn,kn->stk", left, right, preferred_element_type=jnp.float32)


def weight_grad(left, right):
    return jnp.einsum("stk,stn->kn", left, right, preferred_element_type=jnp.float32)


def visible(query_pos, query_first, key_pos):
    return (key_pos[None, :] <= query_pos[:, None]) & (key_pos[None, :] >= query_first[:, None])


def live_pair(query_pos, query_first, key_pos):
    return (key_pos[0] <= query_pos[-1]) & (key_pos[-1] >= query_first[0])


def forward_pair(carried, queries, key_rows, value_rows, query_pos, query_first, key_pos):
    run_max, run_sum, run_acc = carried
    score_scale = queries.shape[-1] ** (-0.5)
    scores = (
        jnp.einsum("qhd,khd->hqk", queries, key_rows, preferred_element_type=jnp.float32)
        * score_scale
    )
    allowed = visible(query_pos, query_first, key_pos)[None]
    scores = jnp.where(allowed, scores, neg_large)
    new_max = jnp.maximum(run_max, jnp.max(scores, axis=-1))
    weights = jnp.where(allowed, jnp.exp(scores - new_max[..., None]), 0.0)
    factor = jnp.exp(run_max - new_max)
    new_sum = factor * run_sum + jnp.sum(weights, axis=-1)
    attention_mixed = jnp.einsum(
        "hqk,khd->hqd", weights.astype(jnp.bfloat16), value_rows, preferred_element_type=jnp.float32
    )
    return (new_max, new_sum, factor[..., None] * run_acc + attention_mixed)


def backward_pair(
    queries,
    grad_rows,
    log_sum,
    delta_rows,
    key_rows,
    value_rows,
    query_pos,
    query_first,
    key_pos,
    want_query,
    want_keys,
):
    score_scale = queries.shape[-1] ** (-0.5)
    scores = (
        jnp.einsum("qhd,khd->hqk", queries, key_rows, preferred_element_type=jnp.float32)
        * score_scale
    )
    allowed = visible(query_pos, query_first, key_pos)[None]
    probs = jnp.where(
        allowed, jnp.exp(jnp.where(allowed, scores, neg_large) - log_sum[..., None]), 0.0
    )
    grad_probs = jnp.einsum(
        "qhd,khd->hqk", grad_rows, value_rows, preferred_element_type=jnp.float32
    )
    grad_scores = (probs * (grad_probs - delta_rows[..., None])).astype(jnp.bfloat16)
    results = ()
    if want_query:
        results = results + (
            jnp.einsum("hqk,khd->qhd", grad_scores, key_rows, preferred_element_type=jnp.float32)
            * score_scale,
        )
    if want_keys:
        grad_key_rows = (
            jnp.einsum("hqk,qhd->khd", grad_scores, queries, preferred_element_type=jnp.float32)
            * score_scale
        )
        grad_value_rows = jnp.einsum(
            "hqk,qhd->khd",
            probs.astype(jnp.bfloat16),
            grad_rows,
            preferred_element_type=jnp.float32,
        )
        results = results + (grad_key_rows, grad_value_rows)
    return results


def each_block(update, carried, arrays, row_limit):
    total_rows = arrays[0].shape[1]
    span_rows = math.gcd(total_rows, row_limit)
    block_count = total_rows // span_rows
    split_arrays = tuple(
        (
            jnp.swapaxes(
                member.reshape((member.shape[0], block_count, span_rows) + member.shape[2:]), 0, 1
            )
            for member in arrays
        )
    )

    def advance(running, inputs):
        number, blocks = inputs
        return (update(running, blocks, number * span_rows), None)

    result, unused = lax.scan(
        advance, carried, (jnp.arange(block_count, dtype=jnp.int32), split_arrays)
    )
    return result


def local_general(
    inputs,
    doc_starts,
    out_grad,
    first_gain,
    first_bias,
    query_key_value_weight,
    attention_out_weight,
    second_gain,
    second_bias,
    up_weight,
    down_weight,
):
    groups = lax.axis_size("uly")
    cycle_place = lax.axis_index("blk")
    seq_count, tok_dev, model_width = inputs.shape
    block_rows = tok_dev * groups
    group_width = model_width // groups
    heads_here = group_width // HEAD_DIM
    qkv_cols, attn_cols, up_cols, down_cols = (
        lax.all_gather(query_key_value_weight, "uly", axis=1, tiled=True),
        lax.all_gather(attention_out_weight, "uly", axis=1, tiled=True),
        lax.all_gather(up_weight, "uly", axis=1, tiled=True),
        lax.all_gather(down_weight, "uly", axis=1, tiled=True),
    )
    gathered = (
        lax.all_gather(qkv_cols, "blk", axis=0, tiled=True),
        lax.all_gather(attn_cols, "blk", axis=0, tiled=True),
        lax.all_gather(up_cols, "blk", axis=0, tiled=True),
        lax.all_gather(down_cols, "blk", axis=0, tiled=True),
        lax.all_gather(first_gain, "blk", axis=0, tiled=True),
        lax.all_gather(first_bias, "blk", axis=0, tiled=True),
        lax.all_gather(second_gain, "blk", axis=0, tiled=True),
        lax.all_gather(second_bias, "blk", axis=0, tiled=True),
    )
    wide_qkv, wide_attn, wide_up, wide_down = (gathered[0], gathered[1], gathered[2], gathered[3])
    gain_one = gathered[4].astype(jnp.float32)
    bias_one = gathered[5].astype(jnp.float32)
    gain_two = gathered[6].astype(jnp.float32)
    bias_two = gathered[7].astype(jnp.float32)
    residual = inputs.astype(jnp.float32)
    first_normalized, norm_one_back = jax.vjp(layer_norm, residual, gain_one, bias_one)
    normed_low = first_normalized.astype(jnp.bfloat16)
    query_key_value = project(normed_low, wide_qkv).astype(jnp.bfloat16)
    packed = query_key_value.reshape(seq_count, tok_dev, 3, groups, group_width)
    spread = lax.all_to_all(packed, "uly", split_axis=3, concat_axis=1, tiled=True)
    query_flat = spread[:, :, 0, 0]
    key_flat = spread[:, :, 1, 0]
    value_flat = spread[:, :, 2, 0]
    queries = query_flat.reshape(seq_count, block_rows, heads_here, HEAD_DIM)
    key_heads = key_flat.reshape(seq_count, block_rows, heads_here, HEAD_DIM)
    value_heads = value_flat.reshape(seq_count, block_rows, heads_here, HEAD_DIM)
    firsts = lax.all_gather(doc_starts, "uly", axis=1, tiled=True)
    query_pos = cycle_place * block_rows + jnp.arange(block_rows, dtype=jnp.int32)

    def forward_update(carried, blocks, first_row):
        span_rows = blocks[0].shape[1]
        key_pos = first_row + jnp.arange(span_rows, dtype=jnp.int32)
        new_max, new_sum, new_acc = ([], [], [])
        for seq_index in range(seq_count):
            one_state = (carried[0][seq_index], carried[1][seq_index], carried[2][seq_index])
            key_one = blocks[0][seq_index].reshape(span_rows, heads_here, HEAD_DIM)
            value_one = blocks[1][seq_index].reshape(span_rows, heads_here, HEAD_DIM)

            def advance_state(state_in):
                return forward_pair(
                    state_in,
                    queries[seq_index],
                    key_one,
                    value_one,
                    query_pos,
                    firsts[seq_index],
                    key_pos,
                )

            def keep_state(state_in):
                return state_in

            updated = lax.cond(
                live_pair(query_pos, firsts[seq_index], key_pos),
                advance_state,
                keep_state,
                one_state,
            )
            new_max.append(updated[0])
            new_sum.append(updated[1])
            new_acc.append(updated[2])
        return (jnp.stack(new_max), jnp.stack(new_sum), jnp.stack(new_acc))

    start_state = (
        jnp.full((seq_count, heads_here, block_rows), neg_large, jnp.float32),
        jnp.zeros((seq_count, heads_here, block_rows), jnp.float32),
        jnp.zeros((seq_count, heads_here, block_rows, HEAD_DIM), jnp.float32),
    )
    run_max, run_sum, run_acc = each_block(
        forward_update,
        start_state,
        (
            lax.all_gather(key_flat, "blk", axis=1, tiled=True),
            lax.all_gather(value_flat, "blk", axis=1, tiled=True),
        ),
        block_rows,
    )
    attn_heads = jnp.swapaxes(run_acc / run_sum[..., None], 1, 2)
    log_sum = run_max + jnp.log(run_sum)
    attn_low = attn_heads.reshape(seq_count, block_rows, 1, group_width).astype(jnp.bfloat16)
    back_rows = lax.all_to_all(attn_low, "uly", split_axis=1, concat_axis=2, tiled=True).reshape(
        seq_count, tok_dev, model_width
    )
    attention_projected = project(back_rows, wide_attn)
    middle = residual + branch_scale * attention_projected
    second_normalized, norm_two_back = jax.vjp(layer_norm, middle, gain_two, bias_two)
    normed_two_low = second_normalized.astype(jnp.bfloat16)
    before_activation = project(normed_two_low, wide_up)
    act_value, gate_back = jax.vjp(smooth_gate, before_activation)
    act_low = act_value.astype(jnp.bfloat16)
    feedforward_output = project(act_low, wide_down)
    output = (middle + branch_scale * feedforward_output).astype(jnp.bfloat16)
    grad_res = out_grad.astype(jnp.float32)
    grad_branch = (branch_scale * grad_res).astype(jnp.bfloat16)
    grad_w_down = weight_grad(act_low, grad_branch)
    grad_act = project_back(grad_branch, wide_down)
    grad_pre = gate_back(grad_act)[0].astype(jnp.bfloat16)
    grad_w_up = weight_grad(normed_two_low, grad_pre)
    grad_norm_two = project_back(grad_pre, wide_up)
    grad_mid_part, grad_gain_two, grad_bias_two = norm_two_back(grad_norm_two)
    grad_middle = grad_res + grad_mid_part
    grad_attn = (branch_scale * grad_middle).astype(jnp.bfloat16)
    grad_w_attn = weight_grad(back_rows, grad_attn)
    grad_mixed = project_back(grad_attn, wide_attn).astype(jnp.bfloat16)
    grad_spread = lax.all_to_all(
        grad_mixed.reshape(seq_count, tok_dev, groups, group_width),
        "uly",
        split_axis=2,
        concat_axis=1,
        tiled=True,
    )
    grad_flat = grad_spread[:, :, 0]
    grad_heads = grad_flat.reshape(seq_count, block_rows, heads_here, HEAD_DIM)
    delta_rows = jnp.swapaxes(jnp.sum(attn_heads * grad_heads.astype(jnp.float32), axis=-1), 1, 2)

    def query_update(grad_query, blocks, first_row):
        span_rows = blocks[0].shape[1]
        key_pos = first_row + jnp.arange(span_rows, dtype=jnp.int32)
        new_terms = []
        for seq_index in range(seq_count):
            key_one = blocks[0][seq_index].reshape(span_rows, heads_here, HEAD_DIM)
            value_one = blocks[1][seq_index].reshape(span_rows, heads_here, HEAD_DIM)

            def query_compute_terms(unused):
                return backward_pair(
                    queries[seq_index],
                    grad_heads[seq_index],
                    log_sum[seq_index],
                    delta_rows[seq_index],
                    key_one,
                    value_one,
                    query_pos,
                    firsts[seq_index],
                    key_pos,
                    True,
                    False,
                )[0]

            def query_zero_terms(unused):
                return jnp.zeros((block_rows, heads_here, HEAD_DIM), jnp.float32)

            new_terms.append(
                grad_query[seq_index]
                + lax.cond(
                    live_pair(query_pos, firsts[seq_index], key_pos),
                    query_compute_terms,
                    query_zero_terms,
                    0,
                )
            )
        return jnp.stack(new_terms)

    grad_query = each_block(
        query_update,
        jnp.zeros((seq_count, block_rows, heads_here, HEAD_DIM), jnp.float32),
        (
            lax.all_gather(key_flat, "blk", axis=1, tiled=True),
            lax.all_gather(value_flat, "blk", axis=1, tiled=True),
        ),
        block_rows,
    )

    def key_update(carried, blocks, first_row):
        span_rows = blocks[0].shape[1]
        other_pos = first_row + jnp.arange(span_rows, dtype=jnp.int32)
        key_sums, value_sums = ([], [])
        for seq_index in range(seq_count):
            query_one = blocks[0][seq_index].reshape(span_rows, heads_here, HEAD_DIM)
            grad_one = blocks[1][seq_index].reshape(span_rows, heads_here, HEAD_DIM)
            lse_one = jnp.transpose(blocks[2][seq_index])
            delta_one = jnp.transpose(blocks[3][seq_index])
            first_one = blocks[4][seq_index]

            def key_compute_terms(unused):
                return backward_pair(
                    query_one,
                    grad_one,
                    lse_one,
                    delta_one,
                    key_heads[seq_index],
                    value_heads[seq_index],
                    other_pos,
                    first_one,
                    query_pos,
                    False,
                    True,
                )

            def key_zero_terms(unused):
                zero_rows = jnp.zeros((block_rows, heads_here, HEAD_DIM), jnp.float32)
                return (zero_rows, zero_rows)

            terms = lax.cond(
                live_pair(other_pos, first_one, query_pos), key_compute_terms, key_zero_terms, 0
            )
            key_sums.append(carried[0][seq_index] + terms[0])
            value_sums.append(carried[1][seq_index] + terms[1])
        return (jnp.stack(key_sums), jnp.stack(value_sums))

    zero_heads = jnp.zeros((seq_count, block_rows, heads_here, HEAD_DIM), jnp.float32)
    grad_keys, grad_values = each_block(
        key_update,
        (zero_heads, zero_heads),
        (
            lax.all_gather(query_flat, "blk", axis=1, tiled=True),
            lax.all_gather(grad_flat, "blk", axis=1, tiled=True),
            lax.all_gather(
                jnp.swapaxes(log_sum, 1, 2).astype(jnp.bfloat16), "blk", axis=1, tiled=True
            ).astype(jnp.float32),
            lax.all_gather(
                jnp.swapaxes(delta_rows, 1, 2).astype(jnp.bfloat16), "blk", axis=1, tiled=True
            ).astype(jnp.float32),
            lax.all_gather(firsts, "blk", axis=1, tiled=True),
        ),
        block_rows,
    )
    grad_query_flat = grad_query.reshape(seq_count, block_rows, group_width)
    grad_key_flat = grad_keys.reshape(seq_count, block_rows, group_width)
    grad_value_flat = grad_values.reshape(seq_count, block_rows, group_width)
    stacked = jnp.stack([grad_query_flat, grad_key_flat, grad_value_flat], axis=2).astype(
        jnp.bfloat16
    )
    stacked = stacked.reshape(seq_count, block_rows, 3, 1, group_width)
    grad_qkv = lax.all_to_all(stacked, "uly", split_axis=1, concat_axis=3, tiled=True).reshape(
        seq_count, tok_dev, 3 * model_width
    )
    grad_w_qkv = weight_grad(normed_low, grad_qkv)
    grad_norm_one = project_back(grad_qkv, wide_qkv)
    grad_in_part, grad_gain_one, grad_bias_one = norm_one_back(grad_norm_one)
    grad_inputs = grad_middle + grad_in_part
    column_sums = (
        lax.psum_scatter(
            grad_w_qkv.astype(jnp.bfloat16), "uly", scatter_dimension=1, tiled=True
        ).astype(jnp.float32),
        lax.psum_scatter(
            grad_w_attn.astype(jnp.bfloat16), "uly", scatter_dimension=1, tiled=True
        ).astype(jnp.float32),
        lax.psum_scatter(
            grad_w_up.astype(jnp.bfloat16), "uly", scatter_dimension=1, tiled=True
        ).astype(jnp.float32),
        lax.psum_scatter(
            grad_w_down.astype(jnp.bfloat16), "uly", scatter_dimension=1, tiled=True
        ).astype(jnp.float32),
        lax.psum_scatter(
            jnp.tile(grad_gain_one, groups).astype(jnp.bfloat16),
            "uly",
            scatter_dimension=0,
            tiled=True,
        ).astype(jnp.float32),
        lax.psum_scatter(
            jnp.tile(grad_bias_one, groups).astype(jnp.bfloat16),
            "uly",
            scatter_dimension=0,
            tiled=True,
        ).astype(jnp.float32),
        lax.psum_scatter(
            jnp.tile(grad_gain_two, groups).astype(jnp.bfloat16),
            "uly",
            scatter_dimension=0,
            tiled=True,
        ).astype(jnp.float32),
        lax.psum_scatter(
            jnp.tile(grad_bias_two, groups).astype(jnp.bfloat16),
            "uly",
            scatter_dimension=0,
            tiled=True,
        ).astype(jnp.float32),
    )
    owned = (
        lax.psum_scatter(column_sums[0], "blk", scatter_dimension=0, tiled=True),
        lax.psum_scatter(column_sums[1], "blk", scatter_dimension=0, tiled=True),
        lax.psum_scatter(column_sums[2], "blk", scatter_dimension=0, tiled=True),
        lax.psum_scatter(column_sums[3], "blk", scatter_dimension=0, tiled=True),
        lax.psum_scatter(column_sums[4], "blk", scatter_dimension=0, tiled=True),
        lax.psum_scatter(column_sums[5], "blk", scatter_dimension=0, tiled=True),
        lax.psum_scatter(column_sums[6], "blk", scatter_dimension=0, tiled=True),
        lax.psum_scatter(column_sums[7], "blk", scatter_dimension=0, tiled=True),
    )
    return (
        output,
        grad_inputs,
        owned[4],
        owned[5],
        owned[0],
        owned[1],
        owned[6],
        owned[7],
        owned[2],
        owned[3],
    )


FULL_TOK = 2048
TILE = 256
TILES = FULL_TOK // TILE
LOG2E = 1.4426950408889634
WIDE = 768
PACK = 400
ACROSS = (((1,), (1,)), ((), ()))


def fits_fast(mesh):
    return dict(mesh.shape) == {"blk": 8, "uly": 4}


def halves_in(rows):
    half = rows.shape[-2] // 2
    return jnp.concatenate([rows[..., :half, :], rows[..., half:, :]], axis=-1)


def halves_out(packed):
    half = packed.shape[-1] // 2
    return jnp.concatenate([packed[..., :half], packed[..., half:]], axis=-2)


def in_f32(value):
    return value.astype(jnp.float32)


def in_bf16(value):
    return value.astype(jnp.bfloat16)


def norm_stats(values):
    center = values - jnp.mean(values, axis=-1, keepdims=True)
    scale = lax.rsqrt(jnp.mean(center * center, axis=-1, keepdims=True) + norm_epsilon)
    return center * scale, scale


def norm_back(grad_out, normal, scale, gain):
    grad_normal = grad_out * gain
    mean_one = jnp.mean(grad_normal, axis=-1, keepdims=True)
    mean_two = jnp.mean(grad_normal * normal, axis=-1, keepdims=True)
    return (grad_normal - mean_one - normal * mean_two) * scale


def mul(left, right):
    return jnp.dot(left, right, preferred_element_type=jnp.float32)


def mul_t(left, right):
    return lax.dot_general(left, right, ACROSS, preferred_element_type=jnp.float32)


def copies(pairs, sems):
    moves = [pltpu.make_async_copy(source, target, sems.at[n]) for n, (source, target) in enumerate(pairs)]
    for move in moves:
        move.start()
    return moves


def finish(moves):
    for move in moves:
        move.wait()


def group_places(uly):
    query = jnp.minimum(uly, 2)
    key = 1 - lax.rem((uly + 1) // 2, 2)
    return query, key, 3 - query - key


def first_kernel(place, x0, x1, x2, x3, starts, weight_in, pack, normed, rows_out, vectors, weight, rows, parts, sems):
    uly = place[1]
    moves = copies(
        [(weight_in, weight)]
        + [
            (part.at[seq], rows.at[seq, uly ^ shift])
            for shift, part in enumerate((x0, x1, x2))
            for seq in range(2)
        ]
        + [(x3.at[pl.ds(64 * seq, 64)], rows.at[seq, uly ^ 3]) for seq in range(2)],
        sems,
    )
    known = in_f32(starts[...])
    even, low_half = lax.rem(uly, 2) == 0, uly < 2
    for seq in range(2):
        chunks = [known[2 * shift + seq : 2 * shift + seq + 1] for shift in range(4)]
        lines = []
        for part in (slice(0, 64), slice(64, 128)):
            near, next_to, far, far_next = (chunk[:, part] for chunk in chunks)
            near = jnp.where(
                even, jnp.concatenate([near, next_to], axis=1), jnp.concatenate([next_to, near], axis=1)
            )
            far = jnp.where(
                even, jnp.concatenate([far, far_next], axis=1), jnp.concatenate([far_next, far], axis=1)
            )
            lines += [jnp.where(low_half, near, far), jnp.where(low_half, far, near)]
        lines = in_bf16(jnp.concatenate(lines + [jnp.zeros((12, 128), jnp.float32)], axis=0))
        for head in range(3):
            pack[4 * seq + head, 384:, :] = lines
        pack[4 * seq + 3] = jnp.zeros((PACK, 128), jnp.bfloat16)
    finish(moves)
    rows_out[...] = rows[...]
    vector_rows = in_f32(weight[:, 512:640]).T[64:72]
    vectors[...] = vector_rows
    normal, unused = norm_stats(in_f32(rows[...].reshape(512, WIDE)))
    value = in_bf16(normal * vector_rows[0:1] + vector_rows[1:2])
    normed[...] = value
    product = in_bf16(mul(value, weight[:, :576]))
    for number in range(3):
        parts[number] = product[:, 192 * number : 192 * (number + 1)]
    queries, keys, values = (parts[at] for at in group_places(uly))
    for seq in range(2):
        at_rows = slice(256 * seq, 256 * (seq + 1))
        for head in range(3):
            at = slice(HEAD_DIM * head, HEAD_DIM * (head + 1))
            pack[4 * seq + head, :256, :] = jnp.concatenate([queries[at_rows, at], keys[at_rows, at]], axis=1)
            pack[4 * seq + head, 256:384, :] = halves_in(values[at_rows, at])


def first_row(pack, tile):
    high, low = (
        jnp.concatenate([rows[0:1], rows[1:2]], axis=1)
        for rows in (in_f32(pack[tile, 384:386, :]), in_f32(pack[tile, 386:388, :]))
    )
    return high * 128.0 + low


def iotas():
    key_at = lax.broadcasted_iota(jnp.int32, (TILE, TILE), 0)
    query_at = lax.broadcasted_iota(jnp.int32, (TILE, TILE), 1)
    return in_f32(key_at), key_at <= query_at


def attn_forward_kernel(pack, packed_out, out_cols, log_row, q_rows, k_rows, v_cols):
    scale = LOG2E * HEAD_DIM**-0.5
    for t in range(TILES):
        rows = pl.ds(t * TILE, TILE)
        pair = pack[t, :TILE, :]
        q_rows[rows, :] = pair[:, :HEAD_DIM]
        k_rows[rows, :] = pair[:, HEAD_DIM:]
        v_cols[:, rows] = halves_out(pack[t, TILE:384, :]).T
    key_at, causal = iotas()
    for i in range(TILES):
        q_at = pl.ds(i * TILE, TILE)
        queries = q_rows[q_at, :]
        first = first_row(pack, i)
        top = total = acc = None
        for j in range(i, -1, -1):
            k_at = pl.ds(j * TILE, TILE)
            scores = mul_t(k_rows[k_at, :], queries)
            allowed = key_at >= first - float(j * TILE)
            if j == i:
                allowed = allowed & causal
            scores = jnp.where(allowed, scores * scale, neg_large)
            tile_top = jnp.max(scores, axis=0, keepdims=True)
            new_top = tile_top if top is None else jnp.maximum(top, tile_top)
            weights = jnp.exp2(scores - new_top)
            tile_sum = jnp.sum(weights, axis=0, keepdims=True)
            tile_acc = mul(v_cols[:, k_at], in_bf16(weights))
            if top is None:
                total, acc = tile_sum, tile_acc
            else:
                factor = jnp.exp2(top - new_top)
                total = factor * total + tile_sum
                acc = factor * acc + tile_acc
            top = new_top
        acc = acc / total
        out_cols[:, q_at] = acc
        log_row[:, q_at] = top + jnp.log2(total)
        packed_out[i] = in_bf16(halves_in(acc.T))


def attn_backward_kernel(
    pack, grad, out_cols, log_row, dpack, q_rows, k_rows, v_rows, g_rows, k_cols, delta, firsts, dq_cols
):
    scale = LOG2E * HEAD_DIM**-0.5
    for t in range(TILES):
        rows = pl.ds(t * TILE, TILE)
        pair = pack[t, :TILE, :]
        q_rows[rows, :] = pair[:, :HEAD_DIM]
        keys = pair[:, HEAD_DIM:]
        k_rows[rows, :] = keys
        k_cols[:, rows] = keys.T
        v_rows[rows, :] = halves_out(pack[t, TILE:384, :])
        g_tile = halves_out(grad[pl.ds(4 * t, 4)]).reshape(TILE, HEAD_DIM)
        g_rows[rows, :] = g_tile
        delta[:, rows] = jnp.sum(in_f32(g_tile.T) * out_cols[:, rows], axis=0, keepdims=True)
        firsts[:, rows] = first_row(pack, t)
    key_at, causal = iotas()
    for j in range(TILES):
        k_at = pl.ds(j * TILE, TILE)
        keys, values, keys_t = k_rows[k_at, :], v_rows[k_at, :], k_cols[:, k_at]
        dk = dv = None
        for i in range(j, TILES):
            q_at = pl.ds(i * TILE, TILE)
            queries, grads = q_rows[q_at, :], g_rows[q_at, :]
            allowed = key_at >= firsts[:, q_at] - float(j * TILE)
            if i == j:
                allowed = allowed & causal
            scores = mul_t(keys, queries) * scale - log_row[:, q_at]
            probs = jnp.exp2(jnp.where(allowed, scores, neg_large))
            dscores = in_bf16(probs * (mul_t(values, grads) - delta[:, q_at]))
            dv_tile = mul(in_bf16(probs), grads)
            dk_tile = mul(dscores, queries)
            dq_tile = mul(keys_t, dscores)
            dv = dv_tile if dv is None else dv + dv_tile
            dk = dk_tile if dk is None else dk + dk_tile
            if j == 0:
                dq_cols[:, q_at] = dq_tile
            else:
                dq_cols[:, q_at] += dq_tile
        dq = (dq_cols[:, k_at] * HEAD_DIM**-0.5).T
        dk = dk * HEAD_DIM**-0.5
        dpack[j, :TILE, :] = in_bf16(jnp.concatenate([dq, dk], axis=1))
        dpack[j, TILE:, :] = halves_in(in_bf16(dv))


def down_from(weights, columns, full):
    for at in range(8):
        for number in range(4):
            lane = WIDE + 192 * number
            columns[at // 2, pl.ds(384 * (at % 2) + 96 * number, 96), :] = weights[at, :, lane : lane + 192]
    for group in range(4):
        full[:, 192 * group : 192 * (group + 1)] = columns[group]


def out_from(weights, uly, columns, full):
    for shift in range(4):
        lane = 2 * WIDE + 192 * shift
        columns[uly ^ shift] = weights[:, :, lane : lane + 192].reshape(WIDE, 192)
    for group in range(4):
        full[:, 192 * group : 192 * (group + 1)] = columns[group]


def middle_kernel(place, mixed_pack, rows_in, g0, g1, g2, g3, weights_in, vectors, *refs):
    outs, (weights, columns, down, w_out, rows, parts, slots, sems) = refs[:10], refs[10:]
    grad_outs, (mixed, middle_own, normed, act_out, pre_out, grad_branch) = outs[:4], outs[4:]
    uly = place[1]
    moves = copies(
        [(weights_in, weights), (rows_in, rows)]
        + [
            (part.at[seq], parts.at[seq, uly ^ shift])
            for shift, part in enumerate((g0, g1, g2, g3))
            for seq in range(2)
        ],
        sems,
    )
    for group in range(4):
        for seq in range(2):
            for head in range(3):
                at = 192 * group + HEAD_DIM * head
                mixed[pl.ds(256 * seq, 256), at : at + HEAD_DIM] = halves_out(mixed_pack[group, seq, head])
    finish(moves)
    out_from(weights, uly, columns, w_out)
    middle = in_f32(rows[...].reshape(512, WIDE)) + branch_scale * mul(mixed[...], w_out[...])
    normal, unused = norm_stats(middle)
    normed[...] = in_bf16(normal * vectors[2:3] + vectors[3:4])
    chunks = middle.reshape(2, 4, 64, WIDE)
    middle_own[...] = jnp.where(
        uly < 2,
        jnp.where(uly == 0, chunks[:, 0], chunks[:, 1]),
        jnp.where(uly == 2, chunks[:, 2], chunks[:, 3]),
    )
    down_from(weights, columns, down)
    grad_branch[...] = in_bf16(branch_scale * in_f32(parts[...])).reshape(512, WIDE)
    up_full = weights[:, :, :WIDE].reshape(WIDE, WIDE)
    pre = mul(normed[...], up_full)
    grad_act = mul_t(grad_branch[...], down[...])
    square = pre * pre
    bend = jnp.tanh(math.sqrt(2.0 / math.pi) * pre * (1.0 + 0.044715 * square))
    half = 0.5 * (1.0 + bend)
    act_out[...] = in_bf16(pre * half)
    slope = math.sqrt(2.0 / math.pi) * (1.0 + 3 * 0.044715 * square)
    gate = half + 0.5 * pre * (1.0 - bend * bend) * slope
    pre_out[...] = in_bf16(grad_act * gate)
    result = in_bf16(mul_t(pre_out[...], up_full)).reshape(2, 4, 64, WIDE)
    for to in range(4):
        slots[to] = result[:, to]
    for shift, out in enumerate(grad_outs):
        out[...] = slots[uly ^ shift]


def feed_grads_kernel(place, normed, act, grad_pre, grad_branch, weights_in, *refs):
    feed, keep, send, w_out, weights, up_grad, down_grad, columns, down, sems = refs
    blk, uly = place[0], place[1]
    moves = copies([(weights_in, weights)], sems)
    chip, core = blk // 2, lax.rem(blk, 2)
    up_grad[...] = in_bf16(mul(normed[...].T, grad_pre[...])).reshape(8, 96, WIDE)
    grad = in_bf16(mul(act[...].T, grad_branch[...]))
    for group in range(4):
        for half in range(2):
            for number in range(4):
                at = 384 * half + 96 * number
                down_grad[2 * group + half, :, 192 * number : 192 * (number + 1)] = grad[
                    at : at + 96, 192 * group : 192 * (group + 1)
                ]
    for shift in range(4):
        same, other = 2 * (chip ^ shift) + core, 2 * (chip ^ shift) + 1 - core
        keep[shift, 0], keep[shift, 1] = up_grad[same], down_grad[same]
        send[shift, 0], send[shift, 1] = up_grad[other], down_grad[other]
    finish(moves)
    out_from(weights, uly, columns, w_out)
    down_from(weights, columns, down)
    feed[...] = in_bf16(mul(act[...], down[...])).reshape(2, 256, WIDE)


def second_back_kernel(
    place, g0, g1, g2, g3, middle, out_grad, w_out, vectors, grad_middle, pack, sums, a0, a1, a2, a3, columns
):
    uly = place[1]
    grad = in_f32(g0[...]) + in_f32(g1[...]) + in_f32(g2[...]) + in_f32(g3[...])
    grad = grad.reshape(128, WIDE)
    normal, scale = norm_stats(middle[...].reshape(128, WIDE))
    sums[...] = jnp.concatenate(
        [
            jnp.sum(grad * normal, axis=0, keepdims=True),
            jnp.sum(grad, axis=0, keepdims=True),
            jnp.zeros((6, WIDE), jnp.float32),
        ],
        axis=0,
    )
    result = in_f32(out_grad[...].reshape(128, WIDE)) + norm_back(grad, normal, scale, vectors[2:3])
    grad_middle[...] = result.reshape(2, 64, WIDE)
    low = in_bf16(branch_scale * result)
    mixed = in_bf16(mul_t(low, w_out[...]))
    for group in range(4):
        columns[group] = low[:, 192 * group : 192 * (group + 1)]
        for seq in range(2):
            rows = mixed[64 * seq : 64 * (seq + 1)]
            for head in range(3):
                at = 192 * group + HEAD_DIM * head
                pack[4 * seq + head, group] = halves_in(rows[:, at : at + HEAD_DIM])
            pack[4 * seq + 3, group] = jnp.zeros((32, 128), jnp.bfloat16)
    for shift, out in enumerate((a0, a1, a2, a3)):
        out[...] = columns[uly ^ shift]


def last_kernel(place, dpack, weight_in, rows_in, *refs):
    grad_norm, grad_qkv, sums, weight, rows_low, parts, sems = refs
    uly = place[1]
    moves = copies([(weight_in, weight), (rows_in, rows_low)], sems)
    for seq in range(2):
        rows = pl.ds(256 * seq, 256)
        for head in range(3):
            at = slice(HEAD_DIM * head, HEAD_DIM * (head + 1))
            pair = dpack[4 * seq + head, :256, :]
            parts[0, rows, at] = pair[:, :HEAD_DIM]
            parts[1, rows, at] = pair[:, HEAD_DIM:]
            parts[2, rows, at] = halves_out(dpack[4 * seq + head, 256:, :])
    query, key, value = group_places(uly)
    for number in range(3):
        part = jnp.where(query == number, 0, jnp.where(key == number, 1, 2))
        grad_qkv[:, 192 * number : 192 * (number + 1)] = parts[part]
    finish(moves)
    grad = mul_t(grad_qkv[...], weight[:, :576])
    grad_norm[...] = in_bf16(grad).reshape(2, 256, WIDE)
    normal, unused = norm_stats(in_f32(rows_low[...].reshape(512, WIDE)))
    sums[...] = jnp.concatenate(
        [
            jnp.sum(grad * normal, axis=0, keepdims=True),
            jnp.sum(grad, axis=0, keepdims=True),
            jnp.zeros((6, WIDE), jnp.float32),
        ],
        axis=0,
    )


TAIL = 832


def late_grads_kernel(
    place, normed, grad_qkv, sums_one, sums_two, mixed, a0, a1, a2, a3, keep, send, full, columns
):
    blk, uly = place[0], place[1]
    chip, core = blk // 2, lax.rem(blk, 2)
    for shift, part in enumerate((a0, a1, a2, a3)):
        for seq in range(2):
            columns[seq, uly ^ shift] = part[64 * seq : 64 * (seq + 1)]
    grad = mul(normed[...].T, grad_qkv[...])
    out_grad = mul(mixed[...].T, columns[...].reshape(512, 192))
    sums = jnp.concatenate([sums_one[0:2], sums_two[0:2], jnp.zeros((60, WIDE), jnp.float32)], axis=0)
    full[...] = in_bf16(jnp.concatenate([grad, sums.T, out_grad], axis=1)).reshape(8, 96, TAIL)
    for shift in range(4):
        keep[shift] = full[2 * (chip ^ shift) + core]
        send[shift] = full[2 * (chip ^ shift) + 1 - core]


def chip_sum_kernel(keep, got, own, to_x, to_y, to_xy):
    own[...] = in_f32(keep[0]) + in_f32(got[0])
    for shift, out in ((1, to_x), (2, to_y), (3, to_xy)):
        out[...] = in_bf16(in_f32(keep[shift]) + in_f32(got[shift]))


VMEM_SPEC = pl.BlockSpec(memory_space=pltpu.VMEM)
FREE_SPEC = pl.BlockSpec(memory_space=pl.ANY)


def on_core(kernel, outs, operands, scratch=(), flops=0, place=False, free=(), sems=0):
    size = lambda item: math.prod(item.shape) * item.dtype.itemsize
    shapes = [jax.ShapeDtypeStruct(shape, dtype) for shape, dtype in outs]
    specs = [FREE_SPEC if n in free else VMEM_SPEC for n in range(len(operands))]
    if place:
        specs[0] = pl.BlockSpec(memory_space=pltpu.SMEM)
    scratch = [pltpu.VMEM(shape, dtype) for shape, dtype in scratch]
    if sems:
        scratch.append(pltpu.SemaphoreType.DMA((sems,)))
    moved = sum(size(item) for item in operands) + sum(size(item) for item in shapes)
    return pl.pallas_call(
        kernel,
        out_shape=shapes,
        in_specs=specs,
        out_specs=[VMEM_SPEC] * len(shapes),
        scratch_shapes=scratch,
        compiler_params=pltpu.CompilerParams(vmem_limit_bytes=(VMEM_MB if free else 24) * 2**20),
        cost_estimate=pl.CostEstimate(flops=flops, bytes_accessed=moved, transcendentals=0),
        name=kernel.__name__,
    )(*operands)


VMEM_MB = 56


def swap_z(value, shift):
    return lax.ppermute(value, "uly", [(i, i ^ shift) for i in range(4)])


def swap_blk(value, mask):
    return lax.ppermute(value, "blk", [(i, i ^ mask) for i in range(8)])


def swap_parts(parts):
    return [parts[0]] + [swap_z(parts[shift], shift) for shift in (1, 2, 3)]


def sum_blk(keep, send):
    got = swap_blk(send, 1)
    shape = keep.shape[1:]
    own, to_x, to_y, to_xy = on_core(
        chip_sum_kernel, [(shape, jnp.float32)] + [(shape, jnp.bfloat16)] * 3, (keep, got)
    )
    return own, to_x, to_y, to_xy


def finish_sum(own, to_x, to_y, to_xy):
    return own + in_f32(swap_blk(to_x, 2)) + in_f32(swap_blk(to_y, 4)) + in_f32(swap_blk(to_xy, 6))


def after(value, *others):
    return lax.optimization_barrier((value,) + others)[0]


DOWN_MOVES = [(b * 4 + u, (2 * u + b % 2) * 4 + b // 2) for b in range(8) for u in range(4)]


def local_fast(
    inputs,
    doc_starts,
    out_grad,
    first_gain,
    first_bias,
    query_key_value_weight,
    attention_out_weight,
    second_gain,
    second_bias,
    up_weight,
    down_weight,
):
    bf16, f32 = jnp.bfloat16, jnp.float32
    blk, uly = lax.axis_index("blk"), lax.axis_index("uly")
    place = jnp.stack([blk, uly]).astype(jnp.int32)
    even = lax.rem(uly, 2) == 0
    square = (WIDE, WIDE)

    groups = [query_key_value_weight[:, 192 * n : 192 * (n + 1)] for n in range(3)]
    own_starts = jnp.concatenate([doc_starts // 128, lax.rem(doc_starts, 128)], axis=1).astype(bf16)
    shared = jnp.concatenate([attention_out_weight, jnp.pad(own_starts, ((0, 14), (0, 64)))], axis=0)
    to_one = jnp.concatenate([groups[1], shared], axis=0)
    to_two = jnp.concatenate([jnp.where(even, groups[2], groups[0]), shared], axis=0)
    to_three = jnp.concatenate(
        [inputs.reshape(128, WIDE), jnp.concatenate([shared[28 * n : 28 * (n + 1)] for n in range(4)], axis=1),
         jnp.zeros((4, WIDE), bf16)], axis=0
    )
    got_one, got_two = swap_z(to_one, 1), swap_z(to_two, 2)
    got_three = swap_z(to_three, 3)
    x_own = after(inputs, to_one, to_two)
    x_parts = [inputs, swap_z(x_own, 1), swap_z(x_own, 2), got_three]
    shared_three = jnp.concatenate([got_three[128:156, 192 * n : 192 * (n + 1)] for n in range(4)], axis=0)
    vectors = jnp.stack([first_gain, first_bias, second_gain, second_bias], axis=1)
    qkv_shard = jnp.concatenate(
        [
            jnp.where(even, groups[0], groups[2]),
            got_one[:96],
            got_two[:96],
            jnp.pad(vectors, ((0, 0), (0, 60))),
        ],
        axis=1,
    )
    starts = jnp.concatenate(
        [own_starts, got_one[192:194, :128], got_two[192:194, :128], shared_three[96:98, :128]], axis=0
    )
    w_qkv = lax.all_gather(qkv_shard, "blk", axis=0, tiled=True)
    down_shard = lax.ppermute(down_weight, ("blk", "uly"), DOWN_MOVES)

    pack, normed_one, rows, vectors = on_core(
        first_kernel,
        [((8, PACK, 128), bf16), ((512, WIDE), bf16), ((2, 4, 64, WIDE), bf16), ((8, WIDE), f32)],
        [place] + x_parts + [starts, w_qkv],
        scratch=[((WIDE, 640), bf16), ((2, 4, 64, WIDE), bf16), ((3, 512, 192), bf16)],
        flops=2 * 512 * 768 * 576,
        place=True,
        free=(1, 2, 3, 4, 6),
        sems=9,
    )
    weights = jnp.concatenate(
        [up_weight]
        + [down_shard[96 * n : 96 * (n + 1)] for n in range(4)]
        + [attention_out_weight, got_one[96:192], got_two[96:192], shared_three[:96]],
        axis=1,
    )
    pack = lax.all_to_all(pack, "blk", 0, 0, tiled=True)
    weights = lax.all_gather(after(weights, pack), "blk", axis=0)
    g_parts = swap_parts([after(out_grad, normed_one)] * 4)

    head_rows = ((FULL_TOK, HEAD_DIM), bf16)
    head_cols = ((HEAD_DIM, FULL_TOK), bf16)
    attn_pack, out_cols, log_row = on_core(
        attn_forward_kernel,
        [((8, 128, 128), bf16), ((HEAD_DIM, FULL_TOK), f32), ((1, FULL_TOK), f32)],
        [pack],
        scratch=[head_rows, head_rows, head_cols],
        flops=4 * FULL_TOK * FULL_TOK * HEAD_DIM,
    )
    attn_pack, *g_parts = lax.optimization_barrier([attn_pack] + g_parts)
    attn_pack = lax.all_to_all(attn_pack, "blk", 0, 0, tiled=True)
    attn_pack = lax.all_gather(attn_pack.reshape(2, 4, 128, 128)[:, :3], "uly", axis=0)

    big = [((8, 96, 3 * WIDE), bf16), ((4, WIDE, 192), bf16), (square, bf16)]
    tok_rows = ((512, WIDE), bf16)
    own_rows = ((2, 64, WIDE), bf16)
    *grad_norm, mixed, middle_own, normed_two, act, grad_pre, grad_branch = on_core(
        middle_kernel,
        [own_rows] * 4 + [tok_rows, ((2, 64, WIDE), f32)] + [tok_rows] * 4,
        [place, attn_pack, rows] + g_parts + [weights, vectors],
        scratch=big + [(square, bf16), ((2, 4, 64, WIDE), bf16), ((2, 4, 64, WIDE), bf16), ((4, 2, 64, WIDE), bf16)],
        flops=8 * 512 * 768 * 768,
        place=True,
        free=(2, 3, 4, 5, 6, 7),
        sems=10,
    )
    grad_norm = swap_parts(grad_norm)
    feed, keep, send, w_out = on_core(
        feed_grads_kernel,
        [((2, 256, WIDE), bf16), ((4, 2, 96, WIDE), bf16), ((4, 2, 96, WIDE), bf16), (square, bf16)],
        [place, normed_two, act, grad_pre, grad_branch, weights],
        scratch=[big[0], ((8, 96, WIDE), bf16), ((8, 96, WIDE), bf16)] + big[1:],
        flops=6 * 512 * 768 * 768,
        place=True,
        free=(5,),
        sems=1,
    )
    grad_middle, grad_pack, sums_two, *grad_cols = on_core(
        second_back_kernel,
        [((2, 64, WIDE), f32), ((8, 4, 32, 128), bf16), ((8, WIDE), f32)] + [((128, 192), bf16)] * 4,
        [place] + grad_norm + [middle_own, out_grad, w_out, vectors],
        scratch=[((4, 128, 192), bf16)],
        flops=2 * 128 * 768 * 768,
        place=True,
    )
    grad_pack = lax.all_to_all(grad_pack.reshape(32, 32, 128), ("blk", "uly"), 0, 0, tiled=True)
    feed = in_f32(lax.psum_scatter(after(feed, grad_pack), "uly", scatter_dimension=1, tiled=True))
    output = in_bf16(middle_own + branch_scale * feed)
    sums = sum_blk(keep, after(send, sums_two))
    grad_pack, *sums = lax.optimization_barrier([grad_pack] + list(sums))

    (dpack,) = on_core(
        attn_backward_kernel,
        [((8, 384, 128), bf16)],
        [pack, grad_pack, out_cols, log_row],
        scratch=[head_rows] * 4 + [head_cols] + [((1, FULL_TOK), f32)] * 2 + [((HEAD_DIM, FULL_TOK), f32)],
        flops=10 * FULL_TOK * FULL_TOK * HEAD_DIM,
    )
    up_down, dpack = lax.optimization_barrier((finish_sum(*sums), dpack))
    g_w_up = up_down[0]
    g_w_down = jnp.concatenate([up_down[1][:, 192 * n : 192 * (n + 1)] for n in range(4)], axis=0)
    g_w_down = lax.ppermute(in_bf16(g_w_down), ("blk", "uly"), [(to, at) for at, to in DOWN_MOVES])
    grad_cols = swap_parts([after(part, dpack) for part in grad_cols])
    dpack = lax.all_to_all(dpack, "blk", 0, 0, tiled=True)
    dpack, g_w_down, *grad_cols = lax.optimization_barrier([dpack, g_w_down] + grad_cols)
    grad_norm, grad_qkv, sums_one = on_core(
        last_kernel,
        [((2, 256, WIDE), bf16)] + [((512, 576), bf16), ((8, WIDE), f32)],
        [place, dpack, w_qkv, rows],
        scratch=[((WIDE, 640), bf16), ((2, 4, 64, WIDE), bf16), ((3, 512, 192), bf16)],
        flops=2 * 512 * 768 * 576,
        place=True,
        free=(2, 3),
        sems=2,
    )
    grad_norm = lax.psum_scatter(grad_norm, "uly", scatter_dimension=1, tiled=True)
    keep, send = on_core(
        late_grads_kernel,
        [((4, 96, TAIL), bf16)] * 2,
        [place, normed_one, grad_qkv, sums_one, sums_two, mixed] + grad_cols,
        scratch=[((8, 96, TAIL), bf16), ((2, 4, 64, 192), bf16)],
        flops=2 * 512 * 768 * 768,
        place=True,
    )
    tail = finish_sum(*sum_blk(keep, send))
    d_vectors = tail[:, 576:580]
    got_one = in_f32(swap_z(in_bf16(jnp.concatenate([tail[:, 192:384], d_vectors], axis=1)), 1))
    d_vectors = d_vectors + got_one[:, 192:]
    got_two = in_f32(swap_z(in_bf16(jnp.concatenate([tail[:, 384:576], d_vectors], axis=1)), 2))
    d_vectors = (d_vectors + got_two[:, 192:]).T
    g_w_qkv = jnp.concatenate(
        [
            jnp.where(even, tail[:, :192], got_two[:, :192]),
            got_one[:, :192],
            jnp.where(even, got_two[:, :192], tail[:, :192]),
        ],
        axis=1,
    )

    grad_norm = in_f32(grad_norm)
    normal, scale = norm_stats(in_f32(inputs))
    grad_inputs = grad_middle + norm_back(grad_norm, normal, scale, vectors[0:1])
    return (
        output,
        grad_inputs,
        d_vectors[0],
        d_vectors[1],
        g_w_qkv,
        tail[:, 640:],
        d_vectors[2],
        d_vectors[3],
        g_w_up,
        in_f32(g_w_down),
    )


def solution(mesh):
    local = local_fast if fits_fast(mesh) else local_general
    placed = (
        P(None, ("blk", "uly"), None),
        P(None, ("blk", "uly")),
        P(None, ("blk", "uly"), None),
        P("blk"),
        P("blk"),
        P("blk", "uly"),
        P("blk", "uly"),
        P("blk"),
        P("blk"),
        P("blk", "uly"),
        P("blk", "uly"),
    )
    return jax.shard_map(
        local,
        mesh=mesh,
        in_specs=placed,
        out_specs=(
            P(None, ("blk", "uly"), None),
            P(None, ("blk", "uly"), None),
            P("blk"),
            P("blk"),
            P("blk", "uly"),
            P("blk", "uly"),
            P("blk"),
            P("blk"),
            P("blk", "uly"),
            P("blk", "uly"),
        ),
        check_vma=False,
    )
```

```python
import functools
import math

import jax
import jax.numpy as jnp
from jax import lax
from jax.experimental import pallas as pl
from jax.experimental.pallas import tpu as pltpu
from jax.sharding import PartitionSpec as P

HEAD_DIM = 64


branch_scale = 48.0 ** (-0.5)
norm_epsilon = 1e-05
neg_large = -1e30


def layer_norm(values, gain_vec, shift_vec):
    center = values - jnp.mean(values, axis=-1, keepdims=True)
    spread = jnp.mean(center * center, axis=-1, keepdims=True)
    return center * lax.rsqrt(spread + norm_epsilon) * gain_vec + shift_vec


def smooth_gate(values):
    return jax.nn.gelu(values, approximate=True)


def project(left, right):
    return jnp.einsum("stk,kn->stn", left, right, preferred_element_type=jnp.float32)


def project_back(left, right):
    return jnp.einsum("stn,kn->stk", left, right, preferred_element_type=jnp.float32)


def weight_grad(left, right):
    return jnp.einsum("stk,stn->kn", left, right, preferred_element_type=jnp.float32)


def visible(query_pos, query_first, key_pos):
    return (key_pos[None, :] <= query_pos[:, None]) & (key_pos[None, :] >= query_first[:, None])


def live_pair(query_pos, query_first, key_pos):
    return (key_pos[0] <= query_pos[-1]) & (key_pos[-1] >= query_first[0])


def forward_pair(carried, queries, key_rows, value_rows, query_pos, query_first, key_pos):
    run_max, run_sum, run_acc = carried
    score_scale = queries.shape[-1] ** (-0.5)
    scores = (
        jnp.einsum("qhd,khd->hqk", queries, key_rows, preferred_element_type=jnp.float32)
        * score_scale
    )
    allowed = visible(query_pos, query_first, key_pos)[None]
    scores = jnp.where(allowed, scores, neg_large)
    new_max = jnp.maximum(run_max, jnp.max(scores, axis=-1))
    weights = jnp.where(allowed, jnp.exp(scores - new_max[..., None]), 0.0)
    factor = jnp.exp(run_max - new_max)
    new_sum = factor * run_sum + jnp.sum(weights, axis=-1)
    attention_mixed = jnp.einsum(
        "hqk,khd->hqd", weights.astype(jnp.bfloat16), value_rows, preferred_element_type=jnp.float32
    )
    return (new_max, new_sum, factor[..., None] * run_acc + attention_mixed)


def backward_pair(
    queries,
    grad_rows,
    log_sum,
    delta_rows,
    key_rows,
    value_rows,
    query_pos,
    query_first,
    key_pos,
    want_query,
    want_keys,
):
    score_scale = queries.shape[-1] ** (-0.5)
    scores = (
        jnp.einsum("qhd,khd->hqk", queries, key_rows, preferred_element_type=jnp.float32)
        * score_scale
    )
    allowed = visible(query_pos, query_first, key_pos)[None]
    probs = jnp.where(
        allowed, jnp.exp(jnp.where(allowed, scores, neg_large) - log_sum[..., None]), 0.0
    )
    grad_probs = jnp.einsum(
        "qhd,khd->hqk", grad_rows, value_rows, preferred_element_type=jnp.float32
    )
    grad_scores = (probs * (grad_probs - delta_rows[..., None])).astype(jnp.bfloat16)
    results = ()
    if want_query:
        results = results + (
            jnp.einsum("hqk,khd->qhd", grad_scores, key_rows, preferred_element_type=jnp.float32)
            * score_scale,
        )
    if want_keys:
        grad_key_rows = (
            jnp.einsum("hqk,qhd->khd", grad_scores, queries, preferred_element_type=jnp.float32)
            * score_scale
        )
        grad_value_rows = jnp.einsum(
            "hqk,qhd->khd",
            probs.astype(jnp.bfloat16),
            grad_rows,
            preferred_element_type=jnp.float32,
        )
        results = results + (grad_key_rows, grad_value_rows)
    return results


def each_block(update, carried, arrays, row_limit):
    total_rows = arrays[0].shape[1]
    span_rows = math.gcd(total_rows, row_limit)
    block_count = total_rows // span_rows
    split_arrays = tuple(
        (
            jnp.swapaxes(
                member.reshape((member.shape[0], block_count, span_rows) + member.shape[2:]), 0, 1
            )
            for member in arrays
        )
    )

    def advance(running, inputs):
        number, blocks = inputs
        return (update(running, blocks, number * span_rows), None)

    result, unused = lax.scan(
        advance, carried, (jnp.arange(block_count, dtype=jnp.int32), split_arrays)
    )
    return result


def local_general(
    inputs,
    doc_starts,
    out_grad,
    first_gain,
    first_bias,
    query_key_value_weight,
    attention_out_weight,
    second_gain,
    second_bias,
    up_weight,
    down_weight,
):
    groups = lax.axis_size("uly")
    cycle_place = lax.axis_index("blk")
    seq_count, tok_dev, model_width = inputs.shape
    block_rows = tok_dev * groups
    group_width = model_width // groups
    heads_here = group_width // HEAD_DIM
    qkv_cols, attn_cols, up_cols, down_cols = (
        lax.all_gather(query_key_value_weight, "uly", axis=1, tiled=True),
        lax.all_gather(attention_out_weight, "uly", axis=1, tiled=True),
        lax.all_gather(up_weight, "uly", axis=1, tiled=True),
        lax.all_gather(down_weight, "uly", axis=1, tiled=True),
    )
    gathered = (
        lax.all_gather(qkv_cols, "blk", axis=0, tiled=True),
        lax.all_gather(attn_cols, "blk", axis=0, tiled=True),
        lax.all_gather(up_cols, "blk", axis=0, tiled=True),
        lax.all_gather(down_cols, "blk", axis=0, tiled=True),
        lax.all_gather(first_gain, "blk", axis=0, tiled=True),
        lax.all_gather(first_bias, "blk", axis=0, tiled=True),
        lax.all_gather(second_gain, "blk", axis=0, tiled=True),
        lax.all_gather(second_bias, "blk", axis=0, tiled=True),
    )
    wide_qkv, wide_attn, wide_up, wide_down = (gathered[0], gathered[1], gathered[2], gathered[3])
    gain_one = gathered[4].astype(jnp.float32)
    bias_one = gathered[5].astype(jnp.float32)
    gain_two = gathered[6].astype(jnp.float32)
    bias_two = gathered[7].astype(jnp.float32)
    residual = inputs.astype(jnp.float32)
    first_normalized, norm_one_back = jax.vjp(layer_norm, residual, gain_one, bias_one)
    normed_low = first_normalized.astype(jnp.bfloat16)
    query_key_value = project(normed_low, wide_qkv).astype(jnp.bfloat16)
    packed = query_key_value.reshape(seq_count, tok_dev, 3, groups, group_width)
    spread = lax.all_to_all(packed, "uly", split_axis=3, concat_axis=1, tiled=True)
    query_flat = spread[:, :, 0, 0]
    key_flat = spread[:, :, 1, 0]
    value_flat = spread[:, :, 2, 0]
    queries = query_flat.reshape(seq_count, block_rows, heads_here, HEAD_DIM)
    key_heads = key_flat.reshape(seq_count, block_rows, heads_here, HEAD_DIM)
    value_heads = value_flat.reshape(seq_count, block_rows, heads_here, HEAD_DIM)
    firsts = lax.all_gather(doc_starts, "uly", axis=1, tiled=True)
    query_pos = cycle_place * block_rows + jnp.arange(block_rows, dtype=jnp.int32)

    def forward_update(carried, blocks, first_row):
        span_rows = blocks[0].shape[1]
        key_pos = first_row + jnp.arange(span_rows, dtype=jnp.int32)
        new_max, new_sum, new_acc = ([], [], [])
        for seq_index in range(seq_count):
            one_state = (carried[0][seq_index], carried[1][seq_index], carried[2][seq_index])
            key_one = blocks[0][seq_index].reshape(span_rows, heads_here, HEAD_DIM)
            value_one = blocks[1][seq_index].reshape(span_rows, heads_here, HEAD_DIM)

            def advance_state(state_in):
                return forward_pair(
                    state_in,
                    queries[seq_index],
                    key_one,
                    value_one,
                    query_pos,
                    firsts[seq_index],
                    key_pos,
                )

            def keep_state(state_in):
                return state_in

            updated = lax.cond(
                live_pair(query_pos, firsts[seq_index], key_pos),
                advance_state,
                keep_state,
                one_state,
            )
            new_max.append(updated[0])
            new_sum.append(updated[1])
            new_acc.append(updated[2])
        return (jnp.stack(new_max), jnp.stack(new_sum), jnp.stack(new_acc))

    start_state = (
        jnp.full((seq_count, heads_here, block_rows), neg_large, jnp.float32),
        jnp.zeros((seq_count, heads_here, block_rows), jnp.float32),
        jnp.zeros((seq_count, heads_here, block_rows, HEAD_DIM), jnp.float32),
    )
    run_max, run_sum, run_acc = each_block(
        forward_update,
        start_state,
        (
            lax.all_gather(key_flat, "blk", axis=1, tiled=True),
            lax.all_gather(value_flat, "blk", axis=1, tiled=True),
        ),
        block_rows,
    )
    attn_heads = jnp.swapaxes(run_acc / run_sum[..., None], 1, 2)
    log_sum = run_max + jnp.log(run_sum)
    attn_low = attn_heads.reshape(seq_count, block_rows, 1, group_width).astype(jnp.bfloat16)
    back_rows = lax.all_to_all(attn_low, "uly", split_axis=1, concat_axis=2, tiled=True).reshape(
        seq_count, tok_dev, model_width
    )
    attention_projected = project(back_rows, wide_attn)
    middle = residual + branch_scale * attention_projected
    second_normalized, norm_two_back = jax.vjp(layer_norm, middle, gain_two, bias_two)
    normed_two_low = second_normalized.astype(jnp.bfloat16)
    before_activation = project(normed_two_low, wide_up)
    act_value, gate_back = jax.vjp(smooth_gate, before_activation)
    act_low = act_value.astype(jnp.bfloat16)
    feedforward_output = project(act_low, wide_down)
    output = (middle + branch_scale * feedforward_output).astype(jnp.bfloat16)
    grad_res = out_grad.astype(jnp.float32)
    grad_branch = (branch_scale * grad_res).astype(jnp.bfloat16)
    grad_w_down = weight_grad(act_low, grad_branch)
    grad_act = project_back(grad_branch, wide_down)
    grad_pre = gate_back(grad_act)[0].astype(jnp.bfloat16)
    grad_w_up = weight_grad(normed_two_low, grad_pre)
    grad_norm_two = project_back(grad_pre, wide_up)
    grad_mid_part, grad_gain_two, grad_bias_two = norm_two_back(grad_norm_two)
    grad_middle = grad_res + grad_mid_part
    grad_attn = (branch_scale * grad_middle).astype(jnp.bfloat16)
    grad_w_attn = weight_grad(back_rows, grad_attn)
    grad_mixed = project_back(grad_attn, wide_attn).astype(jnp.bfloat16)
    grad_spread = lax.all_to_all(
        grad_mixed.reshape(seq_count, tok_dev, groups, group_width),
        "uly",
        split_axis=2,
        concat_axis=1,
        tiled=True,
    )
    grad_flat = grad_spread[:, :, 0]
    grad_heads = grad_flat.reshape(seq_count, block_rows, heads_here, HEAD_DIM)
    delta_rows = jnp.swapaxes(jnp.sum(attn_heads * grad_heads.astype(jnp.float32), axis=-1), 1, 2)

    def query_update(grad_query, blocks, first_row):
        span_rows = blocks[0].shape[1]
        key_pos = first_row + jnp.arange(span_rows, dtype=jnp.int32)
        new_terms = []
        for seq_index in range(seq_count):
            key_one = blocks[0][seq_index].reshape(span_rows, heads_here, HEAD_DIM)
            value_one = blocks[1][seq_index].reshape(span_rows, heads_here, HEAD_DIM)

            def query_compute_terms(unused):
                return backward_pair(
                    queries[seq_index],
                    grad_heads[seq_index],
                    log_sum[seq_index],
                    delta_rows[seq_index],
                    key_one,
                    value_one,
                    query_pos,
                    firsts[seq_index],
                    key_pos,
                    True,
                    False,
                )[0]

            def query_zero_terms(unused):
                return jnp.zeros((block_rows, heads_here, HEAD_DIM), jnp.float32)

            new_terms.append(
                grad_query[seq_index]
                + lax.cond(
                    live_pair(query_pos, firsts[seq_index], key_pos),
                    query_compute_terms,
                    query_zero_terms,
                    0,
                )
            )
        return jnp.stack(new_terms)

    grad_query = each_block(
        query_update,
        jnp.zeros((seq_count, block_rows, heads_here, HEAD_DIM), jnp.float32),
        (
            lax.all_gather(key_flat, "blk", axis=1, tiled=True),
            lax.all_gather(value_flat, "blk", axis=1, tiled=True),
        ),
        block_rows,
    )

    def key_update(carried, blocks, first_row):
        span_rows = blocks[0].shape[1]
        other_pos = first_row + jnp.arange(span_rows, dtype=jnp.int32)
        key_sums, value_sums = ([], [])
        for seq_index in range(seq_count):
            query_one = blocks[0][seq_index].reshape(span_rows, heads_here, HEAD_DIM)
            grad_one = blocks[1][seq_index].reshape(span_rows, heads_here, HEAD_DIM)
            lse_one = jnp.transpose(blocks[2][seq_index])
            delta_one = jnp.transpose(blocks[3][seq_index])
            first_one = blocks[4][seq_index]

            def key_compute_terms(unused):
                return backward_pair(
                    query_one,
                    grad_one,
                    lse_one,
                    delta_one,
                    key_heads[seq_index],
                    value_heads[seq_index],
                    other_pos,
                    first_one,
                    query_pos,
                    False,
                    True,
                )

            def key_zero_terms(unused):
                zero_rows = jnp.zeros((block_rows, heads_here, HEAD_DIM), jnp.float32)
                return (zero_rows, zero_rows)

            terms = lax.cond(
                live_pair(other_pos, first_one, query_pos), key_compute_terms, key_zero_terms, 0
            )
            key_sums.append(carried[0][seq_index] + terms[0])
            value_sums.append(carried[1][seq_index] + terms[1])
        return (jnp.stack(key_sums), jnp.stack(value_sums))

    zero_heads = jnp.zeros((seq_count, block_rows, heads_here, HEAD_DIM), jnp.float32)
    grad_keys, grad_values = each_block(
        key_update,
        (zero_heads, zero_heads),
        (
            lax.all_gather(query_flat, "blk", axis=1, tiled=True),
            lax.all_gather(grad_flat, "blk", axis=1, tiled=True),
            lax.all_gather(
                jnp.swapaxes(log_sum, 1, 2).astype(jnp.bfloat16), "blk", axis=1, tiled=True
            ).astype(jnp.float32),
            lax.all_gather(
                jnp.swapaxes(delta_rows, 1, 2).astype(jnp.bfloat16), "blk", axis=1, tiled=True
            ).astype(jnp.float32),
            lax.all_gather(firsts, "blk", axis=1, tiled=True),
        ),
        block_rows,
    )
    grad_query_flat = grad_query.reshape(seq_count, block_rows, group_width)
    grad_key_flat = grad_keys.reshape(seq_count, block_rows, group_width)
    grad_value_flat = grad_values.reshape(seq_count, block_rows, group_width)
    stacked = jnp.stack([grad_query_flat, grad_key_flat, grad_value_flat], axis=2).astype(
        jnp.bfloat16
    )
    stacked = stacked.reshape(seq_count, block_rows, 3, 1, group_width)
    grad_qkv = lax.all_to_all(stacked, "uly", split_axis=1, concat_axis=3, tiled=True).reshape(
        seq_count, tok_dev, 3 * model_width
    )
    grad_w_qkv = weight_grad(normed_low, grad_qkv)
    grad_norm_one = project_back(grad_qkv, wide_qkv)
    grad_in_part, grad_gain_one, grad_bias_one = norm_one_back(grad_norm_one)
    grad_inputs = grad_middle + grad_in_part
    column_sums = (
        lax.psum_scatter(
            grad_w_qkv.astype(jnp.bfloat16), "uly", scatter_dimension=1, tiled=True
        ).astype(jnp.float32),
        lax.psum_scatter(
            grad_w_attn.astype(jnp.bfloat16), "uly", scatter_dimension=1, tiled=True
        ).astype(jnp.float32),
        lax.psum_scatter(
            grad_w_up.astype(jnp.bfloat16), "uly", scatter_dimension=1, tiled=True
        ).astype(jnp.float32),
        lax.psum_scatter(
            grad_w_down.astype(jnp.bfloat16), "uly", scatter_dimension=1, tiled=True
        ).astype(jnp.float32),
        lax.psum_scatter(
            jnp.tile(grad_gain_one, groups).astype(jnp.bfloat16),
            "uly",
            scatter_dimension=0,
            tiled=True,
        ).astype(jnp.float32),
        lax.psum_scatter(
            jnp.tile(grad_bias_one, groups).astype(jnp.bfloat16),
            "uly",
            scatter_dimension=0,
            tiled=True,
        ).astype(jnp.float32),
        lax.psum_scatter(
            jnp.tile(grad_gain_two, groups).astype(jnp.bfloat16),
            "uly",
            scatter_dimension=0,
            tiled=True,
        ).astype(jnp.float32),
        lax.psum_scatter(
            jnp.tile(grad_bias_two, groups).astype(jnp.bfloat16),
            "uly",
            scatter_dimension=0,
            tiled=True,
        ).astype(jnp.float32),
    )
    owned = (
        lax.psum_scatter(column_sums[0], "blk", scatter_dimension=0, tiled=True),
        lax.psum_scatter(column_sums[1], "blk", scatter_dimension=0, tiled=True),
        lax.psum_scatter(column_sums[2], "blk", scatter_dimension=0, tiled=True),
        lax.psum_scatter(column_sums[3], "blk", scatter_dimension=0, tiled=True),
        lax.psum_scatter(column_sums[4], "blk", scatter_dimension=0, tiled=True),
        lax.psum_scatter(column_sums[5], "blk", scatter_dimension=0, tiled=True),
        lax.psum_scatter(column_sums[6], "blk", scatter_dimension=0, tiled=True),
        lax.psum_scatter(column_sums[7], "blk", scatter_dimension=0, tiled=True),
    )
    return (
        output,
        grad_inputs,
        owned[4],
        owned[5],
        owned[0],
        owned[1],
        owned[6],
        owned[7],
        owned[2],
        owned[3],
    )


FULL_TOK = 2048
TILE = 256
TILES = FULL_TOK // TILE
LOG2E = 1.4426950408889634
WIDE = 768
PACK = 400
ACROSS = (((1,), (1,)), ((), ()))


def fits_fast(mesh):
    return dict(mesh.shape) == {"blk": 8, "uly": 4}


def halves_in(rows):
    half = rows.shape[-2] // 2
    return jnp.concatenate([rows[..., :half, :], rows[..., half:, :]], axis=-1)


def halves_out(packed):
    half = packed.shape[-1] // 2
    return jnp.concatenate([packed[..., :half], packed[..., half:]], axis=-2)


def in_f32(value):
    return value.astype(jnp.float32)


def in_bf16(value):
    return value.astype(jnp.bfloat16)


def norm_stats(values):
    center = values - jnp.mean(values, axis=-1, keepdims=True)
    scale = lax.rsqrt(jnp.mean(center * center, axis=-1, keepdims=True) + norm_epsilon)
    return center * scale, scale


def norm_back(grad_out, normal, scale, gain):
    grad_normal = grad_out * gain
    mean_one = jnp.mean(grad_normal, axis=-1, keepdims=True)
    mean_two = jnp.mean(grad_normal * normal, axis=-1, keepdims=True)
    return (grad_normal - mean_one - normal * mean_two) * scale


def mul(left, right):
    return jnp.dot(left, right, preferred_element_type=jnp.float32)


def mul_t(left, right):
    return lax.dot_general(left, right, ACROSS, preferred_element_type=jnp.float32)


def copies(sems, *pairs):
    moves = [pltpu.make_async_copy(source, target, sems.at[n]) for n, (source, target) in enumerate(pairs)]
    for move in moves:
        move.start()
    return moves


def finish(*moves):
    for move in moves:
        move.wait()


def group_places(uly):
    query = jnp.minimum(uly, 2)
    key = 1 - lax.rem((uly + 1) // 2, 2)
    return query, key, 3 - query - key


def send_kernel(place, weight_in, out_in, starts_in, to_one, to_two, shared, weight, out_weight, doc_starts, sems):
    finish(*copies(sems, (weight_in, weight), (out_in, out_weight), (starts_in, doc_starts)))
    even = lax.rem(place[1], 2) == 0
    groups = [weight[:, 192 * number : 192 * (number + 1)] for number in range(3)]
    starts = doc_starts[...]
    starts = in_f32(jnp.concatenate([starts // 128, lax.rem(starts, 128), jnp.zeros_like(starts)], axis=1))
    lines = jnp.concatenate([in_f32(out_weight[...]), starts, jnp.zeros((30, 192), jnp.float32)], axis=0)
    lines = in_bf16(lines)
    to_one[:96, :] = groups[1]
    to_two[:96, :] = jnp.where(even, groups[2], groups[0])
    to_one[96:, :] = lines[:112]
    to_two[96:, :] = lines[:112]
    shared[...] = lines


def third_kernel(inputs, shared, to_three, sems):
    moves = copies(
        sems,
        (inputs.at[0], to_three.at[pl.ds(0, 64)]),
        (inputs.at[1], to_three.at[pl.ds(64, 64)]),
    )
    for number in range(4):
        to_three[128:, 192 * number : 192 * (number + 1)] = shared[32 * number : 32 * (number + 1)]
    finish(*moves)


def shard_kernel(place, weight, got_one, got_two, vectors, shard):
    even = lax.rem(place[1], 2) == 0
    shard[:, :192] = jnp.where(even, weight[:, :192], weight[:, 384:])
    shard[:, 192:384] = got_one[:96, :]
    shard[:, 384:576] = got_two[:96, :]
    lines = jnp.concatenate([in_f32(vectors[...]), jnp.zeros((60, 96), jnp.float32)], axis=0)
    shard[:, 576:] = in_bf16(lines.T)


def weights_kernel(down, out_weight, got_one, got_two, got_three, weights):
    for number in range(4):
        at = slice(192 * number, 192 * (number + 1))
        weights[:, at] = down[96 * number : 96 * (number + 1), :]
        at = slice(WIDE + 192 * number, WIDE + 192 * (number + 1))
        if number < 3:
            weights[:, at] = (out_weight[...], got_one[96:192, :], got_two[96:192, :])[number]
        else:
            for part in range(3):
                weights[32 * part : 32 * (part + 1), at] = got_three[128:, 192 * part : 192 * (part + 1)]


def first_kernel(place, x0, x1, x2, x3, got_one, got_two, doc_starts, weight, pack, normed, rows, vectors, parts):
    uly = place[1]
    for shift, part in enumerate((x0, x1, x2, x3)):
        for seq in range(2):
            rows[seq, uly ^ shift] = part[64 * seq : 64 * (seq + 1)] if shift == 3 else part[seq]
    full = weight[...].reshape(WIDE, 640)
    own = doc_starts[...]
    known = jnp.concatenate(
        [
            in_f32(jnp.concatenate([own // 128, lax.rem(own, 128)], axis=1)),
            in_f32(got_one[192:208, :128])[:2],
            in_f32(got_two[192:208, :128])[:2],
            in_f32(x3[128:144, 576:704])[:2],
        ],
        axis=0,
    )
    even, low_half = lax.rem(uly, 2) == 0, uly < 2
    for seq in range(2):
        chunks = [known[2 * shift + seq : 2 * shift + seq + 1] for shift in range(4)]
        lines = []
        for part in (slice(0, 64), slice(64, 128)):
            near, next_to, far, far_next = (chunk[:, part] for chunk in chunks)
            near = jnp.where(
                even, jnp.concatenate([near, next_to], axis=1), jnp.concatenate([next_to, near], axis=1)
            )
            far = jnp.where(
                even, jnp.concatenate([far, far_next], axis=1), jnp.concatenate([far_next, far], axis=1)
            )
            lines += [jnp.where(low_half, near, far), jnp.where(low_half, far, near)]
        lines = in_bf16(jnp.concatenate(lines + [jnp.zeros((12, 128), jnp.float32)], axis=0))
        for head in range(3):
            pack[4 * seq + head, 384:, :] = lines
        pack[4 * seq + 3] = jnp.zeros((PACK, 128), jnp.bfloat16)
    vector_rows = in_f32(full[:, 512:640]).T[64:72]
    vectors[...] = vector_rows
    normal, unused = norm_stats(in_f32(rows[...].reshape(512, WIDE)))
    value = in_bf16(normal * vector_rows[0:1] + vector_rows[1:2])
    normed[...] = value
    product = in_bf16(mul(value, full[:, :576]))
    for number in range(3):
        parts[number] = product[:, 192 * number : 192 * (number + 1)]
    queries, keys, values = (parts[at] for at in group_places(uly))
    for seq in range(2):
        at_rows = slice(256 * seq, 256 * (seq + 1))
        for head in range(3):
            at = slice(HEAD_DIM * head, HEAD_DIM * (head + 1))
            pack[4 * seq + head, :256, :] = jnp.concatenate([queries[at_rows, at], keys[at_rows, at]], axis=1)
            pack[4 * seq + head, 256:384, :] = halves_in(values[at_rows, at])


def first_row(pack, tile):
    high, low = (
        jnp.concatenate([rows[0:1], rows[1:2]], axis=1)
        for rows in (in_f32(pack[tile, 384:386, :]), in_f32(pack[tile, 386:388, :]))
    )
    return high * 128.0 + low


def iotas():
    key_at = lax.broadcasted_iota(jnp.int32, (TILE, TILE), 0)
    query_at = lax.broadcasted_iota(jnp.int32, (TILE, TILE), 1)
    return in_f32(key_at), key_at <= query_at


def attn_forward_kernel(pack, packed_out, out_cols, log_row, q_rows, k_rows, v_cols, held, probs):
    scale = LOG2E * HEAD_DIM**-0.5
    for t in range(TILES):
        rows = pl.ds(t * TILE, TILE)
        pair = pack[t, :TILE, :]
        q_rows[rows, :] = pair[:, :HEAD_DIM]
        k_rows[rows, :] = pair[:, HEAD_DIM:]
        v_cols[:, rows] = halves_out(pack[t, TILE:384, :]).T
    key_at, causal = iotas()
    for i in range(TILES):
        q_at = pl.ds(i * TILE, TILE)
        queries = q_rows[q_at, :]
        first = first_row(pack, i)
        top = None
        for j in range(i + 1):
            scores = mul_t(k_rows[pl.ds(j * TILE, TILE), :], queries)
            allowed = key_at >= first - float(j * TILE)
            if j == i:
                allowed = allowed & causal
            scores = jnp.where(allowed, scores * scale, neg_large)
            held[i % 2, j] = scores
            tile_top = jnp.max(scores.reshape(TILE // 8, 8, TILE), axis=0)
            top = tile_top if top is None else jnp.maximum(top, tile_top)
        top = jnp.max(top, axis=0, keepdims=True)
        total = None
        for j in range(i + 1):
            weights = jnp.exp2(held[i % 2, j] - top)
            tile_sum = jnp.sum(weights.reshape(TILE // 8, 8, TILE), axis=0)
            total = tile_sum if total is None else total + tile_sum
            probs[i % 2, pl.ds(j * TILE, TILE), :] = in_bf16(weights)
        seen = pl.ds(0, (i + 1) * TILE)
        acc = mul(v_cols[:, seen], probs[i % 2, seen, :])
        total = jnp.sum(total, axis=0, keepdims=True)
        acc = acc / total
        out_cols[:, q_at] = acc
        log_row[:, q_at] = top + jnp.log2(total)
        packed_out[i] = in_bf16(halves_in(acc.T))


def attn_backward_kernel(
    pack, grad, out_cols, log_row, dpack, q_rows, k_rows, v_rows, g_rows, k_cols, delta, firsts, dq_cols, probs, dscores
):
    scale = LOG2E * HEAD_DIM**-0.5
    for t in range(TILES):
        rows = pl.ds(t * TILE, TILE)
        pair = pack[t, :TILE, :]
        q_rows[rows, :] = pair[:, :HEAD_DIM]
        keys = pair[:, HEAD_DIM:]
        k_rows[rows, :] = keys
        k_cols[:, rows] = keys.T
        v_rows[rows, :] = halves_out(pack[t, TILE:384, :])
        g_tile = halves_out(grad[pl.ds(4 * t, 4)]).reshape(TILE, HEAD_DIM)
        g_rows[rows, :] = g_tile
        delta[:, rows] = jnp.sum(in_f32(g_tile.T) * out_cols[:, rows], axis=0, keepdims=True)
        firsts[:, rows] = first_row(pack, t)
    key_at, causal = iotas()
    for j in range(TILES):
        k_at = pl.ds(j * TILE, TILE)
        keys, values, keys_t = k_rows[k_at, :], v_rows[k_at, :], k_cols[:, k_at]
        for i in range(j, TILES):
            q_at = pl.ds(i * TILE, TILE)
            allowed = key_at >= firsts[:, q_at] - float(j * TILE)
            if i == j:
                allowed = allowed & causal
            scores = mul_t(keys, q_rows[q_at, :]) * scale - log_row[:, q_at]
            weights = jnp.exp2(jnp.where(allowed, scores, neg_large))
            probs[j % 2, :, q_at] = in_bf16(weights)
            dscores[j % 2, :, q_at] = in_bf16(weights * (mul_t(values, g_rows[q_at, :]) - delta[:, q_at]))
        later = pl.ds(j * TILE, FULL_TOK - j * TILE)
        dv = mul(probs[j % 2, :, later], g_rows[later, :])
        dk = mul(dscores[j % 2, :, later], q_rows[later, :])
        dq = mul(keys_t, dscores[j % 2, :, later])
        if j == 0:
            dq_cols[...] = dq
        else:
            dq_cols[:, later] += dq
        dq = (dq_cols[:, k_at] * HEAD_DIM**-0.5).T
        dk = dk * HEAD_DIM**-0.5
        dpack[j, :TILE, :] = in_bf16(jnp.concatenate([dq, dk], axis=1))
        dpack[j, TILE:, :] = halves_in(in_bf16(dv))


def middle_kernel(place, mixed_pack, rows_in, weights_in, up_in, g0, g1, g2, g3, vectors, *refs):
    grad_outs, (mixed_to, middle_to, normed_to, act_to, pre_to) = refs[:4], refs[4:9]
    w_out_to, w_down_to, branch_to = refs[9:12]
    slots, mixed, rows, weights, up, parts, columns, w_out, w_down, grad_branch = refs[12:22]
    middle_own, normed, act_out, pre_out, sems = refs[22:]
    uly = place[1]
    moves = copies(
        sems.at[pl.ds(0, 4)],
        (weights_in.at[:, :, pl.ds(WIDE, WIDE)], weights.at[1]),
        (rows_in, rows),
        (up_in, up),
        (weights_in.at[:, :, pl.ds(0, WIDE)], weights.at[0]),
    )
    for group in range(4):
        for seq in range(2):
            for head in range(3):
                at = 192 * group + HEAD_DIM * head
                mixed[pl.ds(256 * seq, 256), at : at + HEAD_DIM] = halves_out(mixed_pack[group, seq, head])
    out_moves = copies(sems.at[pl.ds(4, 1)], (mixed, mixed_to))
    for shift, part in enumerate((g0, g1, g2, g3)):
        for seq in range(2):
            parts[seq, uly ^ shift] = in_bf16(branch_scale * in_f32(part[seq]))
    grad_branch[...] = parts[...].reshape(512, WIDE)
    out_moves += copies(sems.at[pl.ds(5, 1)], (grad_branch, branch_to))
    finish(moves[0])
    for shift in range(4):
        columns[0, uly ^ shift] = weights[1, :, :, 192 * shift : 192 * (shift + 1)].reshape(WIDE, 192)
    for group in range(4):
        w_out[:, 192 * group : 192 * (group + 1)] = columns[0, group]
    out_moves += copies(sems.at[pl.ds(6, 1)], (w_out, w_out_to))
    projected = mul(mixed[...], w_out[...])
    finish(moves[1])
    middle = in_f32(rows[...].reshape(512, WIDE)) + branch_scale * projected
    normal, unused = norm_stats(middle)
    normed[...] = in_bf16(normal * vectors[2:3] + vectors[3:4])
    chunks = middle.reshape(2, 4, 64, WIDE)
    middle_own[...] = jnp.where(
        uly < 2,
        jnp.where(uly == 0, chunks[:, 0], chunks[:, 1]),
        jnp.where(uly == 2, chunks[:, 2], chunks[:, 3]),
    )
    out_moves += copies(sems.at[pl.ds(8, 2)], (normed, normed_to), (middle_own, middle_to))
    finish(moves[2])
    w_up = up[...].reshape(WIDE, WIDE)
    pre = mul(normed[...], w_up)
    finish(moves[3])
    for at in range(8):
        for number in range(4):
            columns[1, (at // 2) ^ uly, pl.ds(384 * (at % 2) + 96 * number, 96), :] = weights[
                0, at, :, 192 * number : 192 * (number + 1)
            ]
    for group in range(4):
        w_down[:, 192 * group : 192 * (group + 1)] = columns[1, group]
    out_moves += copies(sems.at[pl.ds(7, 1)], (w_down, w_down_to))
    grad_act = mul_t(grad_branch[...], w_down[...])
    square = pre * pre
    bend = jnp.tanh(math.sqrt(2.0 / math.pi) * pre * (1.0 + 0.044715 * square))
    half = 0.5 * (1.0 + bend)
    act_out[...] = in_bf16(pre * half)
    out_moves += copies(sems.at[pl.ds(10, 1)], (act_out, act_to))
    slope = math.sqrt(2.0 / math.pi) * (1.0 + 3 * 0.044715 * square)
    gate = half + 0.5 * pre * (1.0 - bend * bend) * slope
    pre_out[...] = in_bf16(grad_act * gate)
    out_moves += copies(sems.at[pl.ds(11, 1)], (pre_out, pre_to))
    result = in_bf16(mul_t(pre_out[...], w_up)).reshape(2, 4, 64, WIDE)
    for to in range(4):
        slots[to] = result[:, to]
    out_moves += copies(sems.at[pl.ds(12, 4)], *((slots.at[uly ^ n], out) for n, out in enumerate(grad_outs)))
    finish(*out_moves)


def feed_grads_kernel(place, normed, act, grad_pre, branch_in, down_in, feed, keep, send, *refs):
    up_grad, down_grad, grad_branch, w_down, sems = refs
    moves = copies(sems, (branch_in, grad_branch), (down_in, w_down))
    blk, uly = place[0], place[1]
    chip, core = blk // 2, lax.rem(blk, 2)
    up_grad[...] = in_bf16(mul(normed[...].T, grad_pre[...])).reshape(8, 96, WIDE)
    finish(*moves)
    grad = in_bf16(mul(act[...].T, grad_branch[...]))
    for group in range(4):
        for half in range(2):
            for number in range(4):
                at = 384 * half + 96 * number
                down_grad[2 * (group ^ uly) + half, :, 192 * number : 192 * (number + 1)] = grad[
                    at : at + 96, 192 * group : 192 * (group + 1)
                ]
    for shift in range(4):
        same, other = 2 * (chip ^ shift) + core, 2 * (chip ^ shift) + 1 - core
        keep[shift, 0], keep[shift, 1] = up_grad[same], down_grad[same]
        send[shift, 0], send[shift, 1] = up_grad[other], down_grad[other]
    feed[...] = in_bf16(mul(act[...], w_down[...])).reshape(2, 256, WIDE)


def second_back_kernel(
    place, g0, g1, g2, g3, middle, out_grad, w_out_in, vectors, middle_to, pack, sums, a0, a1, a2, a3, *refs
):
    columns, grad_middle, w_out, sems = refs
    uly = place[1]
    moves = copies(sems.at[pl.ds(0, 1)], (w_out_in, w_out))
    grad = in_f32(g0[...]) + in_f32(g1[...]) + in_f32(g2[...]) + in_f32(g3[...])
    grad = grad.reshape(128, WIDE)
    normal, scale = norm_stats(middle[...].reshape(128, WIDE))
    sums[...] = jnp.concatenate(
        [
            jnp.sum(grad * normal, axis=0, keepdims=True),
            jnp.sum(grad, axis=0, keepdims=True),
            jnp.zeros((6, WIDE), jnp.float32),
        ],
        axis=0,
    )
    result = in_f32(out_grad[...].reshape(128, WIDE)) + norm_back(grad, normal, scale, vectors[2:3])
    grad_middle[...] = result.reshape(2, 64, WIDE)
    low = in_bf16(branch_scale * result)
    for group in range(4):
        columns[group] = low[:, 192 * group : 192 * (group + 1)]
    outs = copies(sems.at[pl.ds(1, 1)], (grad_middle, middle_to))
    outs += copies(sems.at[pl.ds(2, 4)], *((columns.at[uly ^ n], out) for n, out in enumerate((a0, a1, a2, a3))))
    finish(*moves)
    mixed = in_bf16(mul_t(low, w_out[...]))
    for group in range(4):
        for seq in range(2):
            rows = mixed[64 * seq : 64 * (seq + 1)]
            for head in range(3):
                at = 192 * group + HEAD_DIM * head
                pack[4 * seq + head, group] = halves_in(rows[:, at : at + HEAD_DIM])
            pack[4 * seq + 3, group] = jnp.zeros((32, 128), jnp.bfloat16)
    finish(*outs)


TAIL = 832


def last_kernel(place, dpack, weight_in, rows_from, normed_from, sums_two, mixed_from, a0, a1, a2, a3, *refs):
    grad_to, keep, send, grad_qkv, parts, slots, full, columns, weight, rows_in, normed, mixed, sems = refs
    blk, uly = place[0], place[1]
    moves = copies(
        sems.at[pl.ds(0, 4)],
        (weight_in, weight),
        (rows_from, rows_in),
        (normed_from, normed),
        (mixed_from, mixed),
    )
    chip, core = blk // 2, lax.rem(blk, 2)
    for seq in range(2):
        rows = pl.ds(256 * seq, 256)
        for head in range(3):
            at = slice(HEAD_DIM * head, HEAD_DIM * (head + 1))
            pair = dpack[4 * seq + head, :256, :]
            parts[0, rows, at] = pair[:, :HEAD_DIM]
            parts[1, rows, at] = pair[:, HEAD_DIM:]
            parts[2, rows, at] = halves_out(dpack[4 * seq + head, 256:, :])
        for shift, part in enumerate((a0, a1, a2, a3)):
            columns[seq, uly ^ shift] = part[64 * seq : 64 * (seq + 1)]
    query, key, value = group_places(uly)
    for number in range(3):
        part = jnp.where(query == number, 0, jnp.where(key == number, 1, 2))
        grad_qkv[:, 192 * number : 192 * (number + 1)] = parts[part]
    finish(moves[0])
    grad = mul_t(grad_qkv[...], weight[...].reshape(WIDE, 640)[:, :576])
    result = in_bf16(grad).reshape(2, 4, 64, WIDE)
    for to in range(4):
        slots[to] = result[:, to]
    out_moves = copies(sems.at[pl.ds(4, 1)], (slots, grad_to))
    finish(moves[1])
    normal, unused = norm_stats(in_f32(rows_in[...].reshape(512, WIDE)))
    sums = jnp.concatenate(
        [
            jnp.sum(grad * normal, axis=0, keepdims=True),
            jnp.sum(grad, axis=0, keepdims=True),
            sums_two[0:2],
            jnp.zeros((60, WIDE), jnp.float32),
        ],
        axis=0,
    )
    finish(moves[2], moves[3])
    grad_weight = mul(normed[...].T, grad_qkv[...])
    grad_out_weight = mul(mixed[...].T, columns[...].reshape(512, 192))
    full[...] = in_bf16(jnp.concatenate([grad_weight, sums.T, grad_out_weight], axis=1)).reshape(8, 96, TAIL)
    for shift in range(4):
        keep[shift] = full[2 * (chip ^ shift) + core]
        send[shift] = full[2 * (chip ^ shift) + 1 - core]
    finish(*out_moves)


def join_ud_kernel(own, from_x, from_y, from_xy, up, down):
    total = own[...] + in_f32(from_x[...]) + in_f32(from_y[...]) + in_f32(from_xy[...])
    up[...] = total[0]
    for number in range(4):
        down[96 * number : 96 * (number + 1), :] = in_bf16(total[1, :, 192 * number : 192 * (number + 1)])


def join_tail_kernel(place, own, from_x, from_y, from_xy, kept, sums, w_out, to_one, to_two, to_three):
    even = lax.rem(place[1], 2) == 0
    total = own[...] + in_f32(from_x[...]) + in_f32(from_y[...]) + in_f32(from_xy[...])
    low = in_bf16(total)
    line = total[:, 512:640].T[64:72]
    kept[...] = total[:, :192]
    w_out[...] = total[:, 640:]
    sums[...] = line
    to_one[:, :192], to_one[:, 192:] = low[:, 192:384], low[:, 576:640]
    to_two[:, :192], to_two[:, 192:] = low[:, 384:576], low[:, 576:640]
    to_three[...] = line


def finish_tail_kernel(place, kept, sums, got_one, got_two, got_three, w_qkv, vectors):
    even = lax.rem(place[1], 2) == 0
    own, one, two = kept[...], in_f32(got_one[:, :192]), in_f32(got_two[:, :192])
    w_qkv[:, :192] = jnp.where(even, own, two)
    w_qkv[:, 192:384] = one
    w_qkv[:, 384:] = jnp.where(even, two, own)
    lines = in_f32(got_one[:, 128:256]) + in_f32(got_two[:, 128:256])
    vectors[...] = lines.T[64:72] + sums[...] + got_three[...]


def finish_rows_kernel(grads, inputs, grad_middle, vectors, grad_inputs):
    grad = in_f32(grads[0]) + in_f32(grads[1]) + in_f32(grads[2]) + in_f32(grads[3])
    normal, scale = norm_stats(in_f32(inputs[...].reshape(128, WIDE)))
    result = norm_back(grad.reshape(128, WIDE), normal, scale, vectors[0:1])
    grad_inputs[...] = grad_middle[...] + result.reshape(2, 64, WIDE)


def chip_sum_kernel(keep, got, own, to_x, to_y, to_xy):
    own[...] = in_f32(keep[0]) + in_f32(got[0])
    for shift, out in ((1, to_x), (2, to_y), (3, to_xy)):
        out[...] = in_bf16(in_f32(keep[shift]) + in_f32(got[shift]))


VMEM_SPEC = pl.BlockSpec(memory_space=pltpu.VMEM)


FAR_SPEC = pl.BlockSpec(memory_space=pltpu.HBM)


def on_core(kernel, outs, operands, scratch=(), grant=16, cost=0, place=False, far=(), far_outs=(), sems=0):
    shapes = [jax.ShapeDtypeStruct(shape, dtype) for shape, dtype in outs]
    specs = [FAR_SPEC if n in far else VMEM_SPEC for n in range(len(operands))]
    if place:
        specs[0] = pl.BlockSpec(memory_space=pltpu.SMEM)
    scratch = [pltpu.VMEM(shape, dtype) for shape, dtype in scratch]
    if sems:
        scratch.append(pltpu.SemaphoreType.DMA((sems,)))
    return pl.pallas_call(
        kernel,
        out_shape=shapes,
        in_specs=specs,
        out_specs=[FAR_SPEC if n in far_outs else VMEM_SPEC for n in range(len(shapes))],
        scratch_shapes=scratch,
        compiler_params=pltpu.CompilerParams(vmem_limit_bytes=(56 if far or far_outs else grant) * 2**20),
        cost_estimate=pl.CostEstimate(flops=int(cost * 10**9), bytes_accessed=0, transcendentals=0),
        name=kernel.__name__,
    )(*operands)


def swap_z(value, shift):
    return lax.ppermute(value, "uly", [(i, i ^ shift) for i in range(4)])


def swap_blk(value, mask):
    return lax.ppermute(value, "blk", [(i, i ^ mask) for i in range(8)])


def swap_parts(parts):
    return [parts[0]] + [swap_z(parts[shift], shift) for shift in (1, 2, 3)]


def sum_blk(keep, send):
    got = swap_blk(send, 1)
    shape = keep.shape[1:]
    own, to_x, to_y, to_xy = on_core(
        chip_sum_kernel, [(shape, jnp.float32)] + [(shape, jnp.bfloat16)] * 3, (keep, got)
    )
    return own, to_x, to_y, to_xy


def swap_sums(own, to_x, to_y, to_xy):
    return own, swap_blk(to_x, 2), swap_blk(to_y, 4), swap_blk(to_xy, 6)


def after(value, *others):
    return lax.optimization_barrier((value,) + others)[0]


DOWN_MOVES = [(b * 4 + u, (2 * (u ^ (b // 2)) + b % 2) * 4 + b // 2) for b in range(8) for u in range(4)]


def local_fast(
    inputs,
    doc_starts,
    out_grad,
    first_gain,
    first_bias,
    query_key_value_weight,
    attention_out_weight,
    second_gain,
    second_bias,
    up_weight,
    down_weight,
):
    bf16, f32 = jnp.bfloat16, jnp.float32
    blk, uly = lax.axis_index("blk"), lax.axis_index("uly")
    place = jnp.stack([blk, uly]).astype(jnp.int32)
    square = (WIDE, WIDE)

    to_one, to_two, shared = on_core(
        send_kernel,
        [((208, 192), bf16), ((208, 192), bf16), ((128, 192), bf16)],
        [place, query_key_value_weight, attention_out_weight, doc_starts],
        scratch=[((96, 576), bf16), ((96, 192), bf16), ((2, 64), jnp.int32)],
        place=True,
        far=(1, 2, 3),
        sems=3,
    )
    got_one, got_two = swap_z(to_one, 1), swap_z(to_two, 2)
    x_own = after(inputs, to_one, to_two)
    (to_three,) = on_core(third_kernel, [((160, WIDE), bf16)], [x_own, shared], far=(0,), sems=2)
    x_parts = [inputs, swap_z(x_own, 1), swap_z(x_own, 2), swap_z(to_three, 3)]
    (qkv_shard,) = on_core(
        shard_kernel,
        [((96, 640), bf16)],
        [place, query_key_value_weight, got_one, got_two]
        + [jnp.stack([first_gain, first_bias, second_gain, second_bias])],
        place=True,
    )
    w_qkv = lax.all_gather(qkv_shard, "blk", axis=0)
    down_shard = lax.ppermute(down_weight, ("blk", "uly"), DOWN_MOVES)
    x_parts[0], down_shard = lax.optimization_barrier((inputs, down_shard))

    pack, normed_one, rows, vectors = on_core(
        first_kernel,
        [((8, PACK, 128), bf16), ((512, WIDE), bf16), ((2, 4, 64, WIDE), bf16), ((8, WIDE), f32)],
        [place] + x_parts + [got_one, got_two, doc_starts, w_qkv],
        scratch=[((3, 512, 192), bf16)],
        place=True,
    )
    g_own = after(out_grad, normed_one)
    g_one, g_three = swap_z(g_own, 1), swap_z(g_own, 3)
    (weights,) = on_core(
        weights_kernel,
        [((96, 2 * WIDE), bf16)],
        [down_shard, attention_out_weight, after(got_one, pack), got_two, x_parts[3]],
    )
    ups = lax.all_gather(up_weight, "blk", axis=0)
    pack = lax.all_to_all(pack, "blk", 0, 0, tiled=True)
    pack, g_one, g_three = lax.optimization_barrier((pack, g_one, g_three))

    head_rows = ((FULL_TOK, HEAD_DIM), bf16)
    head_cols = ((HEAD_DIM, FULL_TOK), bf16)
    attn_pack, out_cols, log_row = on_core(
        attn_forward_kernel,
        [((8, 128, 128), bf16), ((HEAD_DIM, FULL_TOK), f32), ((1, FULL_TOK), f32)],
        [pack],
        scratch=[head_rows, head_rows, head_cols, ((2, TILES, TILE, TILE), f32), ((2, FULL_TOK, TILE), bf16)],
    )
    weights, g_own = lax.optimization_barrier((weights, out_grad, attn_pack))[:2]
    weights = lax.all_gather(weights, "blk", axis=0)
    attn_pack = lax.all_to_all(attn_pack, "blk", 0, 0, tiled=True)
    g_two = swap_z(g_own, 2)
    g_parts = [out_grad, g_one, g_two, g_three]

    tok_rows = ((512, WIDE), bf16)
    own_rows = ((2, 64, WIDE), bf16)
    attn_pack = lax.all_gather(attn_pack.reshape(2, 4, 128, 128)[:, :3], "uly", axis=0)
    *grad_norm, mixed, middle_own, normed_two, act, grad_pre, w_out, w_down, grad_branch = on_core(
        middle_kernel,
        [own_rows] * 4 + [tok_rows, ((2, 64, WIDE), f32)] + [tok_rows] * 3 + [(square, bf16)] * 2 + [tok_rows],
        [place, attn_pack, rows, weights, ups] + g_parts + [vectors],
        scratch=[
            ((4, 2, 64, WIDE), bf16),
            tok_rows,
            ((2, 4, 64, WIDE), bf16),
            ((2, 8, 96, WIDE), bf16),
            ((8, 96, WIDE), bf16),
            ((2, 4, 64, WIDE), bf16),
            ((2, 4, WIDE, 192), bf16),
            (square, bf16),
            (square, bf16),
            tok_rows,
            ((2, 64, WIDE), f32),
            tok_rows,
            tok_rows,
            tok_rows,
        ],
        cost=5,
        place=True,
        far=(2, 3, 4),
        far_outs=tuple(range(12)),
        sems=16,
    )
    grad_norm = swap_parts(grad_norm)
    feed, keep, send = on_core(
        feed_grads_kernel,
        [((2, 256, WIDE), bf16), ((4, 2, 96, WIDE), bf16), ((4, 2, 96, WIDE), bf16)],
        [place, normed_two, act, grad_pre, grad_branch, w_down],
        scratch=[((8, 96, WIDE), bf16), ((8, 96, WIDE), bf16), tok_rows, (square, bf16)],
        place=True,
        cost=4,
        far=(4, 5),
        sems=2,
    )
    grad_norm[0], keep, send = lax.optimization_barrier((grad_norm[0], keep, send))
    grad_middle, grad_pack, sums_two, *grad_cols = on_core(
        second_back_kernel,
        [((2, 64, WIDE), f32), ((8, 4, 32, 128), bf16), ((8, WIDE), f32)] + [((128, 192), bf16)] * 4,
        [place] + grad_norm + [middle_own, out_grad, w_out, vectors],
        scratch=[((4, 128, 192), bf16), ((2, 64, WIDE), f32), (square, bf16)],
        place=True,
        cost=2,
        far=(7,),
        far_outs=(0, 3, 4, 5, 6),
        sems=6,
    )
    grad_pack = lax.all_to_all(grad_pack.reshape(32, 32, 128), ("blk", "uly"), 0, 0, tiled=True)
    feed = in_f32(lax.psum_scatter(after(feed, grad_pack), "uly", scatter_dimension=1, tiled=True))
    output = in_bf16(middle_own + branch_scale * feed)
    sums = sum_blk(keep, send)
    grad_pack = after(grad_pack, *sums)
    sums = swap_sums(*sums)

    (dpack,) = on_core(
        attn_backward_kernel,
        [((8, 384, 128), bf16)],
        [pack, grad_pack, out_cols, log_row],
        scratch=[head_rows] * 4 + [head_cols] + [((1, FULL_TOK), f32)] * 2 + [((HEAD_DIM, FULL_TOK), f32)] + [((2, TILE, FULL_TOK), bf16)] * 2,
    )
    dpack, *sums = lax.optimization_barrier([dpack] + list(sums))
    g_w_up, g_w_down = on_core(join_ud_kernel, [((96, WIDE), f32), ((384, 192), bf16)], sums)
    grad_cols = swap_parts([after(part, dpack) for part in grad_cols])
    dpack = lax.all_to_all(dpack, "blk", 0, 0, tiled=True)
    grad_norm, keep, send = on_core(
        last_kernel,
        [((4, 2, 64, WIDE), bf16)] + [((4, 96, TAIL), bf16)] * 2,
        [place, dpack, w_qkv, rows, normed_one, sums_two, mixed] + grad_cols,
        scratch=[
            ((512, 576), bf16),
            ((3, 512, 192), bf16),
            ((4, 2, 64, WIDE), bf16),
            ((8, 96, TAIL), bf16),
            ((2, 4, 64, 192), bf16),
            ((8, 96, 640), bf16),
            ((2, 4, 64, WIDE), bf16),
            tok_rows,
            tok_rows,
        ],
        grant=24,
        place=True,
        far=(2, 3, 4, 6),
        far_outs=(0,),
        sems=5,
        cost=3,
    )
    grad_norm = lax.all_to_all(grad_norm, "uly", 0, 0, tiled=True)
    kept, sums, g_w_out, to_one, to_two, to_three = on_core(
        join_tail_kernel,
        [((96, 192), f32), ((8, 96), f32), ((96, 192), f32), ((96, 256), bf16), ((96, 256), bf16), ((8, 96), f32)],
        [place] + list(swap_sums(*sum_blk(keep, send))),
        place=True,
    )
    g_w_down = lax.ppermute(after(g_w_down, to_one), ("blk", "uly"), [(to, at) for at, to in DOWN_MOVES])
    g_w_qkv, d_vectors = on_core(
        finish_tail_kernel,
        [((96, 576), f32), ((8, 96), f32)],
        [place, kept, sums, swap_z(to_one, 1), swap_z(to_two, 2), swap_z(to_three, 3)],
        place=True,
    )
    (grad_inputs,) = on_core(
        finish_rows_kernel, [((2, 64, WIDE), f32)], [grad_norm, inputs, grad_middle, vectors]
    )
    return (
        output,
        grad_inputs,
        d_vectors[0],
        d_vectors[1],
        g_w_qkv,
        g_w_out,
        d_vectors[2],
        d_vectors[3],
        g_w_up,
        in_f32(g_w_down),
    )


def solution(mesh):
    local = local_fast if fits_fast(mesh) else local_general
    placed = (
        P(None, ("blk", "uly"), None),
        P(None, ("blk", "uly")),
        P(None, ("blk", "uly"), None),
        P("blk"),
        P("blk"),
        P("blk", "uly"),
        P("blk", "uly"),
        P("blk"),
        P("blk"),
        P("blk", "uly"),
        P("blk", "uly"),
    )
    return jax.shard_map(
        local,
        mesh=mesh,
        in_specs=placed,
        out_specs=(
            P(None, ("blk", "uly"), None),
            P(None, ("blk", "uly"), None),
            P("blk"),
            P("blk"),
            P("blk", "uly"),
            P("blk", "uly"),
            P("blk"),
            P("blk"),
            P("blk", "uly"),
            P("blk", "uly"),
        ),
        check_vma=False,
    )
```

```python
import functools
import math

import jax
import jax.numpy as jnp
from jax import lax
from jax.experimental import pallas as pl
from jax.experimental.pallas import tpu as pltpu
from jax.sharding import PartitionSpec as P

HEAD_DIM = 64


branch_scale = 48.0 ** (-0.5)
norm_epsilon = 1e-05
neg_large = -1e30


def layer_norm(values, gain_vec, shift_vec):
    center = values - jnp.mean(values, axis=-1, keepdims=True)
    spread = jnp.mean(center * center, axis=-1, keepdims=True)
    return center * lax.rsqrt(spread + norm_epsilon) * gain_vec + shift_vec


def smooth_gate(values):
    return jax.nn.gelu(values, approximate=True)


def project(left, right):
    return jnp.einsum("stk,kn->stn", left, right, preferred_element_type=jnp.float32)


def project_back(left, right):
    return jnp.einsum("stn,kn->stk", left, right, preferred_element_type=jnp.float32)


def weight_grad(left, right):
    return jnp.einsum("stk,stn->kn", left, right, preferred_element_type=jnp.float32)


def visible(query_pos, query_first, key_pos):
    return (key_pos[None, :] <= query_pos[:, None]) & (key_pos[None, :] >= query_first[:, None])


def live_pair(query_pos, query_first, key_pos):
    return (key_pos[0] <= query_pos[-1]) & (key_pos[-1] >= query_first[0])


def forward_pair(carried, queries, key_rows, value_rows, query_pos, query_first, key_pos):
    run_max, run_sum, run_acc = carried
    score_scale = queries.shape[-1] ** (-0.5)
    scores = (
        jnp.einsum("qhd,khd->hqk", queries, key_rows, preferred_element_type=jnp.float32)
        * score_scale
    )
    allowed = visible(query_pos, query_first, key_pos)[None]
    scores = jnp.where(allowed, scores, neg_large)
    new_max = jnp.maximum(run_max, jnp.max(scores, axis=-1))
    weights = jnp.where(allowed, jnp.exp(scores - new_max[..., None]), 0.0)
    factor = jnp.exp(run_max - new_max)
    new_sum = factor * run_sum + jnp.sum(weights, axis=-1)
    attention_mixed = jnp.einsum(
        "hqk,khd->hqd", weights.astype(jnp.bfloat16), value_rows, preferred_element_type=jnp.float32
    )
    return (new_max, new_sum, factor[..., None] * run_acc + attention_mixed)


def backward_pair(
    queries,
    grad_rows,
    log_sum,
    delta_rows,
    key_rows,
    value_rows,
    query_pos,
    query_first,
    key_pos,
    want_query,
    want_keys,
):
    score_scale = queries.shape[-1] ** (-0.5)
    scores = (
        jnp.einsum("qhd,khd->hqk", queries, key_rows, preferred_element_type=jnp.float32)
        * score_scale
    )
    allowed = visible(query_pos, query_first, key_pos)[None]
    probs = jnp.where(
        allowed, jnp.exp(jnp.where(allowed, scores, neg_large) - log_sum[..., None]), 0.0
    )
    grad_probs = jnp.einsum(
        "qhd,khd->hqk", grad_rows, value_rows, preferred_element_type=jnp.float32
    )
    grad_scores = (probs * (grad_probs - delta_rows[..., None])).astype(jnp.bfloat16)
    results = ()
    if want_query:
        results = results + (
            jnp.einsum("hqk,khd->qhd", grad_scores, key_rows, preferred_element_type=jnp.float32)
            * score_scale,
        )
    if want_keys:
        grad_key_rows = (
            jnp.einsum("hqk,qhd->khd", grad_scores, queries, preferred_element_type=jnp.float32)
            * score_scale
        )
        grad_value_rows = jnp.einsum(
            "hqk,qhd->khd",
            probs.astype(jnp.bfloat16),
            grad_rows,
            preferred_element_type=jnp.float32,
        )
        results = results + (grad_key_rows, grad_value_rows)
    return results


def each_block(update, carried, arrays, row_limit):
    total_rows = arrays[0].shape[1]
    span_rows = math.gcd(total_rows, row_limit)
    block_count = total_rows // span_rows
    split_arrays = tuple(
        (
            jnp.swapaxes(
                member.reshape((member.shape[0], block_count, span_rows) + member.shape[2:]), 0, 1
            )
            for member in arrays
        )
    )

    def advance(running, inputs):
        number, blocks = inputs
        return (update(running, blocks, number * span_rows), None)

    result, unused = lax.scan(
        advance, carried, (jnp.arange(block_count, dtype=jnp.int32), split_arrays)
    )
    return result


def local_general(
    inputs,
    doc_starts,
    out_grad,
    first_gain,
    first_bias,
    query_key_value_weight,
    attention_out_weight,
    second_gain,
    second_bias,
    up_weight,
    down_weight,
):
    groups = lax.axis_size("uly")
    cycle_place = lax.axis_index("blk")
    seq_count, tok_dev, model_width = inputs.shape
    block_rows = tok_dev * groups
    group_width = model_width // groups
    heads_here = group_width // HEAD_DIM
    qkv_cols, attn_cols, up_cols, down_cols = (
        lax.all_gather(query_key_value_weight, "uly", axis=1, tiled=True),
        lax.all_gather(attention_out_weight, "uly", axis=1, tiled=True),
        lax.all_gather(up_weight, "uly", axis=1, tiled=True),
        lax.all_gather(down_weight, "uly", axis=1, tiled=True),
    )
    gathered = (
        lax.all_gather(qkv_cols, "blk", axis=0, tiled=True),
        lax.all_gather(attn_cols, "blk", axis=0, tiled=True),
        lax.all_gather(up_cols, "blk", axis=0, tiled=True),
        lax.all_gather(down_cols, "blk", axis=0, tiled=True),
        lax.all_gather(first_gain, "blk", axis=0, tiled=True),
        lax.all_gather(first_bias, "blk", axis=0, tiled=True),
        lax.all_gather(second_gain, "blk", axis=0, tiled=True),
        lax.all_gather(second_bias, "blk", axis=0, tiled=True),
    )
    wide_qkv, wide_attn, wide_up, wide_down = (gathered[0], gathered[1], gathered[2], gathered[3])
    gain_one = gathered[4].astype(jnp.float32)
    bias_one = gathered[5].astype(jnp.float32)
    gain_two = gathered[6].astype(jnp.float32)
    bias_two = gathered[7].astype(jnp.float32)
    residual = inputs.astype(jnp.float32)
    first_normalized, norm_one_back = jax.vjp(layer_norm, residual, gain_one, bias_one)
    normed_low = first_normalized.astype(jnp.bfloat16)
    query_key_value = project(normed_low, wide_qkv).astype(jnp.bfloat16)
    packed = query_key_value.reshape(seq_count, tok_dev, 3, groups, group_width)
    spread = lax.all_to_all(packed, "uly", split_axis=3, concat_axis=1, tiled=True)
    query_flat = spread[:, :, 0, 0]
    key_flat = spread[:, :, 1, 0]
    value_flat = spread[:, :, 2, 0]
    queries = query_flat.reshape(seq_count, block_rows, heads_here, HEAD_DIM)
    key_heads = key_flat.reshape(seq_count, block_rows, heads_here, HEAD_DIM)
    value_heads = value_flat.reshape(seq_count, block_rows, heads_here, HEAD_DIM)
    firsts = lax.all_gather(doc_starts, "uly", axis=1, tiled=True)
    query_pos = cycle_place * block_rows + jnp.arange(block_rows, dtype=jnp.int32)

    def forward_update(carried, blocks, first_row):
        span_rows = blocks[0].shape[1]
        key_pos = first_row + jnp.arange(span_rows, dtype=jnp.int32)
        new_max, new_sum, new_acc = ([], [], [])
        for seq_index in range(seq_count):
            one_state = (carried[0][seq_index], carried[1][seq_index], carried[2][seq_index])
            key_one = blocks[0][seq_index].reshape(span_rows, heads_here, HEAD_DIM)
            value_one = blocks[1][seq_index].reshape(span_rows, heads_here, HEAD_DIM)

            def advance_state(state_in):
                return forward_pair(
                    state_in,
                    queries[seq_index],
                    key_one,
                    value_one,
                    query_pos,
                    firsts[seq_index],
                    key_pos,
                )

            def keep_state(state_in):
                return state_in

            updated = lax.cond(
                live_pair(query_pos, firsts[seq_index], key_pos),
                advance_state,
                keep_state,
                one_state,
            )
            new_max.append(updated[0])
            new_sum.append(updated[1])
            new_acc.append(updated[2])
        return (jnp.stack(new_max), jnp.stack(new_sum), jnp.stack(new_acc))

    start_state = (
        jnp.full((seq_count, heads_here, block_rows), neg_large, jnp.float32),
        jnp.zeros((seq_count, heads_here, block_rows), jnp.float32),
        jnp.zeros((seq_count, heads_here, block_rows, HEAD_DIM), jnp.float32),
    )
    run_max, run_sum, run_acc = each_block(
        forward_update,
        start_state,
        (
            lax.all_gather(key_flat, "blk", axis=1, tiled=True),
            lax.all_gather(value_flat, "blk", axis=1, tiled=True),
        ),
        block_rows,
    )
    attn_heads = jnp.swapaxes(run_acc / run_sum[..., None], 1, 2)
    log_sum = run_max + jnp.log(run_sum)
    attn_low = attn_heads.reshape(seq_count, block_rows, 1, group_width).astype(jnp.bfloat16)
    back_rows = lax.all_to_all(attn_low, "uly", split_axis=1, concat_axis=2, tiled=True).reshape(
        seq_count, tok_dev, model_width
    )
    attention_projected = project(back_rows, wide_attn)
    middle = residual + branch_scale * attention_projected
    second_normalized, norm_two_back = jax.vjp(layer_norm, middle, gain_two, bias_two)
    normed_two_low = second_normalized.astype(jnp.bfloat16)
    before_activation = project(normed_two_low, wide_up)
    act_value, gate_back = jax.vjp(smooth_gate, before_activation)
    act_low = act_value.astype(jnp.bfloat16)
    feedforward_output = project(act_low, wide_down)
    output = (middle + branch_scale * feedforward_output).astype(jnp.bfloat16)
    grad_res = out_grad.astype(jnp.float32)
    grad_branch = (branch_scale * grad_res).astype(jnp.bfloat16)
    grad_w_down = weight_grad(act_low, grad_branch)
    grad_act = project_back(grad_branch, wide_down)
    grad_pre = gate_back(grad_act)[0].astype(jnp.bfloat16)
    grad_w_up = weight_grad(normed_two_low, grad_pre)
    grad_norm_two = project_back(grad_pre, wide_up)
    grad_mid_part, grad_gain_two, grad_bias_two = norm_two_back(grad_norm_two)
    grad_middle = grad_res + grad_mid_part
    grad_attn = (branch_scale * grad_middle).astype(jnp.bfloat16)
    grad_w_attn = weight_grad(back_rows, grad_attn)
    grad_mixed = project_back(grad_attn, wide_attn).astype(jnp.bfloat16)
    grad_spread = lax.all_to_all(
        grad_mixed.reshape(seq_count, tok_dev, groups, group_width),
        "uly",
        split_axis=2,
        concat_axis=1,
        tiled=True,
    )
    grad_flat = grad_spread[:, :, 0]
    grad_heads = grad_flat.reshape(seq_count, block_rows, heads_here, HEAD_DIM)
    delta_rows = jnp.swapaxes(jnp.sum(attn_heads * grad_heads.astype(jnp.float32), axis=-1), 1, 2)

    def query_update(grad_query, blocks, first_row):
        span_rows = blocks[0].shape[1]
        key_pos = first_row + jnp.arange(span_rows, dtype=jnp.int32)
        new_terms = []
        for seq_index in range(seq_count):
            key_one = blocks[0][seq_index].reshape(span_rows, heads_here, HEAD_DIM)
            value_one = blocks[1][seq_index].reshape(span_rows, heads_here, HEAD_DIM)

            def query_compute_terms(unused):
                return backward_pair(
                    queries[seq_index],
                    grad_heads[seq_index],
                    log_sum[seq_index],
                    delta_rows[seq_index],
                    key_one,
                    value_one,
                    query_pos,
                    firsts[seq_index],
                    key_pos,
                    True,
                    False,
                )[0]

            def query_zero_terms(unused):
                return jnp.zeros((block_rows, heads_here, HEAD_DIM), jnp.float32)

            new_terms.append(
                grad_query[seq_index]
                + lax.cond(
                    live_pair(query_pos, firsts[seq_index], key_pos),
                    query_compute_terms,
                    query_zero_terms,
                    0,
                )
            )
        return jnp.stack(new_terms)

    grad_query = each_block(
        query_update,
        jnp.zeros((seq_count, block_rows, heads_here, HEAD_DIM), jnp.float32),
        (
            lax.all_gather(key_flat, "blk", axis=1, tiled=True),
            lax.all_gather(value_flat, "blk", axis=1, tiled=True),
        ),
        block_rows,
    )

    def key_update(carried, blocks, first_row):
        span_rows = blocks[0].shape[1]
        other_pos = first_row + jnp.arange(span_rows, dtype=jnp.int32)
        key_sums, value_sums = ([], [])
        for seq_index in range(seq_count):
            query_one = blocks[0][seq_index].reshape(span_rows, heads_here, HEAD_DIM)
            grad_one = blocks[1][seq_index].reshape(span_rows, heads_here, HEAD_DIM)
            lse_one = jnp.transpose(blocks[2][seq_index])
            delta_one = jnp.transpose(blocks[3][seq_index])
            first_one = blocks[4][seq_index]

            def key_compute_terms(unused):
                return backward_pair(
                    query_one,
                    grad_one,
                    lse_one,
                    delta_one,
                    key_heads[seq_index],
                    value_heads[seq_index],
                    other_pos,
                    first_one,
                    query_pos,
                    False,
                    True,
                )

            def key_zero_terms(unused):
                zero_rows = jnp.zeros((block_rows, heads_here, HEAD_DIM), jnp.float32)
                return (zero_rows, zero_rows)

            terms = lax.cond(
                live_pair(other_pos, first_one, query_pos), key_compute_terms, key_zero_terms, 0
            )
            key_sums.append(carried[0][seq_index] + terms[0])
            value_sums.append(carried[1][seq_index] + terms[1])
        return (jnp.stack(key_sums), jnp.stack(value_sums))

    zero_heads = jnp.zeros((seq_count, block_rows, heads_here, HEAD_DIM), jnp.float32)
    grad_keys, grad_values = each_block(
        key_update,
        (zero_heads, zero_heads),
        (
            lax.all_gather(query_flat, "blk", axis=1, tiled=True),
            lax.all_gather(grad_flat, "blk", axis=1, tiled=True),
            lax.all_gather(
                jnp.swapaxes(log_sum, 1, 2).astype(jnp.bfloat16), "blk", axis=1, tiled=True
            ).astype(jnp.float32),
            lax.all_gather(
                jnp.swapaxes(delta_rows, 1, 2).astype(jnp.bfloat16), "blk", axis=1, tiled=True
            ).astype(jnp.float32),
            lax.all_gather(firsts, "blk", axis=1, tiled=True),
        ),
        block_rows,
    )
    grad_query_flat = grad_query.reshape(seq_count, block_rows, group_width)
    grad_key_flat = grad_keys.reshape(seq_count, block_rows, group_width)
    grad_value_flat = grad_values.reshape(seq_count, block_rows, group_width)
    stacked = jnp.stack([grad_query_flat, grad_key_flat, grad_value_flat], axis=2).astype(
        jnp.bfloat16
    )
    stacked = stacked.reshape(seq_count, block_rows, 3, 1, group_width)
    grad_qkv = lax.all_to_all(stacked, "uly", split_axis=1, concat_axis=3, tiled=True).reshape(
        seq_count, tok_dev, 3 * model_width
    )
    grad_w_qkv = weight_grad(normed_low, grad_qkv)
    grad_norm_one = project_back(grad_qkv, wide_qkv)
    grad_in_part, grad_gain_one, grad_bias_one = norm_one_back(grad_norm_one)
    grad_inputs = grad_middle + grad_in_part
    column_sums = (
        lax.psum_scatter(
            grad_w_qkv.astype(jnp.bfloat16), "uly", scatter_dimension=1, tiled=True
        ).astype(jnp.float32),
        lax.psum_scatter(
            grad_w_attn.astype(jnp.bfloat16), "uly", scatter_dimension=1, tiled=True
        ).astype(jnp.float32),
        lax.psum_scatter(
            grad_w_up.astype(jnp.bfloat16), "uly", scatter_dimension=1, tiled=True
        ).astype(jnp.float32),
        lax.psum_scatter(
            grad_w_down.astype(jnp.bfloat16), "uly", scatter_dimension=1, tiled=True
        ).astype(jnp.float32),
        lax.psum_scatter(
            jnp.tile(grad_gain_one, groups).astype(jnp.bfloat16),
            "uly",
            scatter_dimension=0,
            tiled=True,
        ).astype(jnp.float32),
        lax.psum_scatter(
            jnp.tile(grad_bias_one, groups).astype(jnp.bfloat16),
            "uly",
            scatter_dimension=0,
            tiled=True,
        ).astype(jnp.float32),
        lax.psum_scatter(
            jnp.tile(grad_gain_two, groups).astype(jnp.bfloat16),
            "uly",
            scatter_dimension=0,
            tiled=True,
        ).astype(jnp.float32),
        lax.psum_scatter(
            jnp.tile(grad_bias_two, groups).astype(jnp.bfloat16),
            "uly",
            scatter_dimension=0,
            tiled=True,
        ).astype(jnp.float32),
    )
    owned = (
        lax.psum_scatter(column_sums[0], "blk", scatter_dimension=0, tiled=True),
        lax.psum_scatter(column_sums[1], "blk", scatter_dimension=0, tiled=True),
        lax.psum_scatter(column_sums[2], "blk", scatter_dimension=0, tiled=True),
        lax.psum_scatter(column_sums[3], "blk", scatter_dimension=0, tiled=True),
        lax.psum_scatter(column_sums[4], "blk", scatter_dimension=0, tiled=True),
        lax.psum_scatter(column_sums[5], "blk", scatter_dimension=0, tiled=True),
        lax.psum_scatter(column_sums[6], "blk", scatter_dimension=0, tiled=True),
        lax.psum_scatter(column_sums[7], "blk", scatter_dimension=0, tiled=True),
    )
    return (
        output,
        grad_inputs,
        owned[4],
        owned[5],
        owned[0],
        owned[1],
        owned[6],
        owned[7],
        owned[2],
        owned[3],
    )


FULL_TOK = 2048
TILE = 256
TILES = FULL_TOK // TILE
LOG2E = 1.4426950408889634
WIDE = 768
PACK = 400
ACROSS = (((1,), (1,)), ((), ()))


def fits_fast(mesh):
    return dict(mesh.shape) == {"blk": 8, "uly": 4}


def halves_in(rows):
    half = rows.shape[-2] // 2
    return jnp.concatenate([rows[..., :half, :], rows[..., half:, :]], axis=-1)


def halves_out(packed):
    half = packed.shape[-1] // 2
    return jnp.concatenate([packed[..., :half], packed[..., half:]], axis=-2)


def in_f32(value):
    return value.astype(jnp.float32)


def in_bf16(value):
    return value.astype(jnp.bfloat16)


def norm_stats(values):
    center = values - jnp.mean(values, axis=-1, keepdims=True)
    scale = lax.rsqrt(jnp.mean(center * center, axis=-1, keepdims=True) + norm_epsilon)
    return center * scale, scale


def norm_back(grad_out, normal, scale, gain):
    grad_normal = grad_out * gain
    mean_one = jnp.mean(grad_normal, axis=-1, keepdims=True)
    mean_two = jnp.mean(grad_normal * normal, axis=-1, keepdims=True)
    return (grad_normal - mean_one - normal * mean_two) * scale


def mul(left, right):
    return jnp.dot(left, right, preferred_element_type=jnp.float32)


def mul_t(left, right):
    return lax.dot_general(left, right, ACROSS, preferred_element_type=jnp.float32)


def copies(sems, *pairs):
    moves = [pltpu.make_async_copy(source, target, sems.at[n]) for n, (source, target) in enumerate(pairs)]
    for move in moves:
        move.start()
    return moves


def finish(*moves):
    for move in moves:
        move.wait()


def group_places(uly):
    query = jnp.minimum(uly, 2)
    key = 1 - lax.rem((uly + 1) // 2, 2)
    return query, key, 3 - query - key


def send_kernel(place, weight_in, out_in, starts_in, to_one, to_two, shared, weight, out_weight, doc_starts, sems):
    finish(*copies(sems, (weight_in, weight), (out_in, out_weight), (starts_in, doc_starts)))
    even = lax.rem(place[1], 2) == 0
    groups = [weight[:, 192 * number : 192 * (number + 1)] for number in range(3)]
    starts = doc_starts[...]
    starts = in_f32(jnp.concatenate([starts // 128, lax.rem(starts, 128), jnp.zeros_like(starts)], axis=1))
    lines = jnp.concatenate([in_f32(out_weight[...]), starts, jnp.zeros((30, 192), jnp.float32)], axis=0)
    lines = in_bf16(lines)
    to_one[:96, :] = groups[1]
    to_two[:96, :] = jnp.where(even, groups[2], groups[0])
    to_one[96:, :] = lines[:112]
    to_two[96:, :] = lines[:112]
    for number in range(4):
        shared[:, 192 * number : 192 * (number + 1)] = lines[32 * number : 32 * (number + 1)]


def shard_kernel(place, weight, got_one, got_two, vectors, shard):
    even = lax.rem(place[1], 2) == 0
    shard[:, :192] = jnp.where(even, weight[:, :192], weight[:, 384:])
    shard[:, 192:384] = got_one[:96, :]
    shard[:, 384:576] = got_two[:96, :]
    lines = jnp.concatenate([in_f32(vectors[...]), jnp.zeros((60, 96), jnp.float32)], axis=0)
    shard[:, 576:] = in_bf16(lines.T)


def weights_kernel(down, out_weight, got_one, got_two, got_three, weights):
    for number in range(4):
        at = slice(192 * number, 192 * (number + 1))
        weights[:, at] = down[96 * number : 96 * (number + 1), :]
        at = slice(WIDE + 192 * number, WIDE + 192 * (number + 1))
        if number < 3:
            weights[:, at] = (out_weight[...], got_one[96:192, :], got_two[96:192, :])[number]
        else:
            for part in range(3):
                weights[32 * part : 32 * (part + 1), at] = got_three[128:, 192 * part : 192 * (part + 1)]


def first_kernel(place, x0, x1, x2, x3, got_one, got_two, doc_starts, weight, pack, normed, rows, vectors, parts):
    uly = place[1]
    for shift, part in enumerate((x0, x1, x2, x3)):
        for seq in range(2):
            rows[seq, uly ^ shift] = part[64 * seq : 64 * (seq + 1)] if shift == 3 else part[seq]
    full = weight[...].reshape(WIDE, 640)
    own = doc_starts[...]
    known = jnp.concatenate(
        [
            in_f32(jnp.concatenate([own // 128, lax.rem(own, 128)], axis=1)),
            in_f32(got_one[192:208, :128])[:2],
            in_f32(got_two[192:208, :128])[:2],
            in_f32(x3[128:144, 576:704])[:2],
        ],
        axis=0,
    )
    even, low_half = lax.rem(uly, 2) == 0, uly < 2
    for seq in range(2):
        chunks = [known[2 * shift + seq : 2 * shift + seq + 1] for shift in range(4)]
        lines = []
        for part in (slice(0, 64), slice(64, 128)):
            near, next_to, far, far_next = (chunk[:, part] for chunk in chunks)
            near = jnp.where(
                even, jnp.concatenate([near, next_to], axis=1), jnp.concatenate([next_to, near], axis=1)
            )
            far = jnp.where(
                even, jnp.concatenate([far, far_next], axis=1), jnp.concatenate([far_next, far], axis=1)
            )
            lines += [jnp.where(low_half, near, far), jnp.where(low_half, far, near)]
        lines = in_bf16(jnp.concatenate(lines + [jnp.zeros((12, 128), jnp.float32)], axis=0))
        for head in range(3):
            pack[4 * seq + head, 384:, :] = lines
        pack[4 * seq + 3] = jnp.zeros((PACK, 128), jnp.bfloat16)
    vector_rows = in_f32(full[:, 512:640]).T[64:72]
    vectors[...] = vector_rows
    normal, unused = norm_stats(in_f32(rows[...].reshape(512, WIDE)))
    value = in_bf16(normal * vector_rows[0:1] + vector_rows[1:2])
    normed[...] = value
    product = in_bf16(mul(value, full[:, :576]))
    for number in range(3):
        parts[number] = product[:, 192 * number : 192 * (number + 1)]
    queries, keys, values = (parts[at] for at in group_places(uly))
    for seq in range(2):
        at_rows = slice(256 * seq, 256 * (seq + 1))
        for head in range(3):
            at = slice(HEAD_DIM * head, HEAD_DIM * (head + 1))
            pack[4 * seq + head, :256, :] = jnp.concatenate([queries[at_rows, at], keys[at_rows, at]], axis=1)
            pack[4 * seq + head, 256:384, :] = halves_in(values[at_rows, at])


def first_row(pack, tile):
    high, low = (
        jnp.concatenate([rows[0:1], rows[1:2]], axis=1)
        for rows in (in_f32(pack[tile, 384:386, :]), in_f32(pack[tile, 386:388, :]))
    )
    return high * 128.0 + low


def iotas():
    key_at = lax.broadcasted_iota(jnp.int32, (TILE, TILE), 0)
    query_at = lax.broadcasted_iota(jnp.int32, (TILE, TILE), 1)
    return in_f32(key_at), key_at <= query_at


def attn_forward_kernel(pack, packed_out, out_cols, log_row, q_rows, k_rows, v_cols, held, probs):
    scale = LOG2E * HEAD_DIM**-0.5
    for t in range(TILES):
        rows = pl.ds(t * TILE, TILE)
        pair = pack[t, :TILE, :]
        q_rows[rows, :] = pair[:, :HEAD_DIM]
        k_rows[rows, :] = pair[:, HEAD_DIM:]
        v_cols[:, rows] = halves_out(pack[t, TILE:384, :]).T
    key_at, causal = iotas()
    for i in range(TILES):
        q_at = pl.ds(i * TILE, TILE)
        queries = q_rows[q_at, :]
        first = first_row(pack, i)
        top = None
        for j in range(i + 1):
            scores = mul_t(k_rows[pl.ds(j * TILE, TILE), :], queries)
            allowed = key_at >= first - float(j * TILE)
            if j == i:
                allowed = allowed & causal
            scores = jnp.where(allowed, scores * scale, neg_large)
            held[i % 2, j] = scores
            tile_top = jnp.max(scores.reshape(TILE // 8, 8, TILE), axis=0)
            top = tile_top if top is None else jnp.maximum(top, tile_top)
        top = jnp.max(top, axis=0, keepdims=True)
        total = None
        for j in range(i + 1):
            weights = jnp.exp2(held[i % 2, j] - top)
            tile_sum = jnp.sum(weights.reshape(TILE // 8, 8, TILE), axis=0)
            total = tile_sum if total is None else total + tile_sum
            probs[i % 2, pl.ds(j * TILE, TILE), :] = in_bf16(weights)
        seen = pl.ds(0, (i + 1) * TILE)
        acc = mul(v_cols[:, seen], probs[i % 2, seen, :])
        total = jnp.sum(total, axis=0, keepdims=True)
        acc = acc / total
        out_cols[:, q_at] = acc
        log_row[:, q_at] = top + jnp.log2(total)
        packed_out[i] = in_bf16(halves_in(acc.T))


def attn_backward_kernel(
    pack, grad, out_cols, log_row, dpack, q_rows, k_rows, v_rows, g_rows, k_cols, delta, firsts, dq_cols, probs, dscores
):
    scale = LOG2E * HEAD_DIM**-0.5
    for t in range(TILES):
        rows = pl.ds(t * TILE, TILE)
        pair = pack[t, :TILE, :]
        q_rows[rows, :] = pair[:, :HEAD_DIM]
        keys = pair[:, HEAD_DIM:]
        k_rows[rows, :] = keys
        k_cols[:, rows] = keys.T
        v_rows[rows, :] = halves_out(pack[t, TILE:384, :])
        g_tile = halves_out(grad[pl.ds(4 * t, 4)]).reshape(TILE, HEAD_DIM)
        g_rows[rows, :] = g_tile
        delta[:, rows] = jnp.sum(in_f32(g_tile.T) * out_cols[:, rows], axis=0, keepdims=True)
        firsts[:, rows] = first_row(pack, t)
    key_at, causal = iotas()
    for j in range(TILES):
        k_at = pl.ds(j * TILE, TILE)
        keys, values, keys_t = k_rows[k_at, :], v_rows[k_at, :], k_cols[:, k_at]
        for i in range(j, TILES):
            q_at = pl.ds(i * TILE, TILE)
            allowed = key_at >= firsts[:, q_at] - float(j * TILE)
            if i == j:
                allowed = allowed & causal
            scores = mul_t(keys, q_rows[q_at, :]) * scale - log_row[:, q_at]
            weights = jnp.exp2(jnp.where(allowed, scores, neg_large))
            probs[j % 2, :, q_at] = in_bf16(weights)
            dscores[j % 2, :, q_at] = in_bf16(weights * (mul_t(values, g_rows[q_at, :]) - delta[:, q_at]))
        later = pl.ds(j * TILE, FULL_TOK - j * TILE)
        dv = mul(probs[j % 2, :, later], g_rows[later, :])
        dk = mul(dscores[j % 2, :, later], q_rows[later, :])
        dq = mul(keys_t, dscores[j % 2, :, later])
        if j == 0:
            dq_cols[...] = dq
        else:
            dq_cols[:, later] += dq
        dq = (dq_cols[:, k_at] * HEAD_DIM**-0.5).T
        dk = dk * HEAD_DIM**-0.5
        dpack[j, :TILE, :] = in_bf16(jnp.concatenate([dq, dk], axis=1))
        dpack[j, TILE:, :] = halves_in(in_bf16(dv))


def middle_kernel(place, mixed_pack, rows_in, weights_in, up_in, g0, g1, g2, g3, vectors, *refs):
    grad_outs, (mixed_to, middle_to, normed_to, act_to, pre_to) = refs[:4], refs[4:9]
    w_out_to, w_down_to, branch_to = refs[9:12]
    slots, mixed, rows, weights, up, parts, columns, w_out, w_down, grad_branch = refs[12:22]
    middle_own, normed, act_out, pre_out, sems = refs[22:]
    uly = place[1]
    moves = copies(
        sems.at[pl.ds(0, 4)],
        (weights_in.at[:, :, pl.ds(WIDE, WIDE)], weights.at[1]),
        (rows_in, rows),
        (up_in, up),
        (weights_in.at[:, :, pl.ds(0, WIDE)], weights.at[0]),
    )
    for group in range(4):
        for seq in range(2):
            for head in range(3):
                at = 192 * group + HEAD_DIM * head
                mixed[pl.ds(256 * seq, 256), at : at + HEAD_DIM] = halves_out(mixed_pack[group, seq, head])
    out_moves = copies(sems.at[pl.ds(4, 1)], (mixed, mixed_to))
    for shift, part in enumerate((g0, g1, g2, g3)):
        for seq in range(2):
            parts[seq, uly ^ shift] = in_bf16(branch_scale * in_f32(part[seq]))
    grad_branch[...] = parts[...].reshape(512, WIDE)
    out_moves += copies(sems.at[pl.ds(5, 1)], (grad_branch, branch_to))
    finish(moves[0])
    for shift in range(4):
        columns[0, uly ^ shift] = weights[1, :, :, 192 * shift : 192 * (shift + 1)].reshape(WIDE, 192)
    for group in range(4):
        w_out[:, 192 * group : 192 * (group + 1)] = columns[0, group]
    out_moves += copies(sems.at[pl.ds(6, 1)], (w_out, w_out_to))
    projected = mul(mixed[...], w_out[...])
    finish(moves[1])
    middle = in_f32(rows[...].reshape(512, WIDE)) + branch_scale * projected
    normal, unused = norm_stats(middle)
    normed[...] = in_bf16(normal * vectors[2:3] + vectors[3:4])
    chunks = middle.reshape(2, 4, 64, WIDE)
    middle_own[...] = jnp.where(
        uly < 2,
        jnp.where(uly == 0, chunks[:, 0], chunks[:, 1]),
        jnp.where(uly == 2, chunks[:, 2], chunks[:, 3]),
    )
    out_moves += copies(sems.at[pl.ds(8, 2)], (normed, normed_to), (middle_own, middle_to))
    finish(moves[2])
    w_up = up[...].reshape(WIDE, WIDE)
    pre = mul(normed[...], w_up)
    finish(moves[3])
    for at in range(8):
        for number in range(4):
            columns[1, (at // 2) ^ uly, pl.ds(384 * (at % 2) + 96 * number, 96), :] = weights[
                0, at, :, 192 * number : 192 * (number + 1)
            ]
    for group in range(4):
        w_down[:, 192 * group : 192 * (group + 1)] = columns[1, group]
    out_moves += copies(sems.at[pl.ds(7, 1)], (w_down, w_down_to))
    grad_act = mul_t(grad_branch[...], w_down[...])
    square = pre * pre
    bend = jnp.tanh(math.sqrt(2.0 / math.pi) * pre * (1.0 + 0.044715 * square))
    half = 0.5 * (1.0 + bend)
    act_out[...] = in_bf16(pre * half)
    out_moves += copies(sems.at[pl.ds(10, 1)], (act_out, act_to))
    slope = math.sqrt(2.0 / math.pi) * (1.0 + 3 * 0.044715 * square)
    gate = half + 0.5 * pre * (1.0 - bend * bend) * slope
    pre_out[...] = in_bf16(grad_act * gate)
    out_moves += copies(sems.at[pl.ds(11, 1)], (pre_out, pre_to))
    result = in_bf16(mul_t(pre_out[...], w_up)).reshape(2, 4, 64, WIDE)
    for to in range(4):
        slots[to] = result[:, to]
    out_moves += copies(sems.at[pl.ds(12, 4)], *((slots.at[uly ^ n], out) for n, out in enumerate(grad_outs)))
    finish(*out_moves)


def feed_grads_kernel(place, normed, act, grad_pre, branch_in, down_in, feed, keep, send, *refs):
    up_grad, down_grad, grad_branch, w_down, sems = refs
    moves = copies(sems, (branch_in, grad_branch), (down_in, w_down))
    blk, uly = place[0], place[1]
    chip, core = blk // 2, lax.rem(blk, 2)
    up_grad[...] = in_bf16(mul(normed[...].T, grad_pre[...])).reshape(8, 96, WIDE)
    finish(*moves)
    grad = in_bf16(mul(act[...].T, grad_branch[...]))
    for group in range(4):
        for half in range(2):
            for number in range(4):
                at = 384 * half + 96 * number
                down_grad[2 * (group ^ uly) + half, :, 192 * number : 192 * (number + 1)] = grad[
                    at : at + 96, 192 * group : 192 * (group + 1)
                ]
    for shift in range(4):
        same, other = 2 * (chip ^ shift) + core, 2 * (chip ^ shift) + 1 - core
        keep[shift, 0], keep[shift, 1] = up_grad[same], down_grad[same]
        send[shift, 0], send[shift, 1] = up_grad[other], down_grad[other]
    feed[...] = in_bf16(mul(act[...], w_down[...])).reshape(2, 256, WIDE)


def second_back_kernel(
    place, g0, g1, g2, g3, middle, out_grad, w_out_in, vectors, middle_to, pack, sums, a0, a1, a2, a3, *refs
):
    columns, grad_middle, w_out, sems = refs
    uly = place[1]
    moves = copies(sems.at[pl.ds(0, 1)], (w_out_in, w_out))
    grad = in_f32(g0[...]) + in_f32(g1[...]) + in_f32(g2[...]) + in_f32(g3[...])
    grad = grad.reshape(128, WIDE)
    normal, scale = norm_stats(middle[...].reshape(128, WIDE))
    sums[...] = jnp.concatenate(
        [
            jnp.sum(grad * normal, axis=0, keepdims=True),
            jnp.sum(grad, axis=0, keepdims=True),
            jnp.zeros((6, WIDE), jnp.float32),
        ],
        axis=0,
    )
    result = in_f32(out_grad[...].reshape(128, WIDE)) + norm_back(grad, normal, scale, vectors[2:3])
    grad_middle[...] = result.reshape(2, 64, WIDE)
    low = in_bf16(branch_scale * result)
    for group in range(4):
        columns[group] = low[:, 192 * group : 192 * (group + 1)]
    outs = copies(sems.at[pl.ds(1, 1)], (grad_middle, middle_to))
    outs += copies(sems.at[pl.ds(2, 4)], *((columns.at[uly ^ n], out) for n, out in enumerate((a0, a1, a2, a3))))
    finish(*moves)
    mixed = in_bf16(mul_t(low, w_out[...]))
    for group in range(4):
        for seq in range(2):
            rows = mixed[64 * seq : 64 * (seq + 1)]
            for head in range(3):
                at = 192 * group + HEAD_DIM * head
                pack[4 * seq + head, group] = halves_in(rows[:, at : at + HEAD_DIM])
            pack[4 * seq + 3, group] = jnp.zeros((32, 128), jnp.bfloat16)
    finish(*outs)


TAIL = 832


def last_kernel(place, dpack, weight_in, rows_from, normed_from, sums_two, mixed_from, a0, a1, a2, a3, *refs):
    grad_to, keep, send, grad_qkv, parts, slots, full, columns, weight, rows_in, normed, mixed, sems = refs
    blk, uly = place[0], place[1]
    moves = copies(
        sems.at[pl.ds(0, 4)],
        (weight_in, weight),
        (rows_from, rows_in),
        (normed_from, normed),
        (mixed_from, mixed),
    )
    chip, core = blk // 2, lax.rem(blk, 2)
    for seq in range(2):
        rows = pl.ds(256 * seq, 256)
        for head in range(3):
            at = slice(HEAD_DIM * head, HEAD_DIM * (head + 1))
            pair = dpack[4 * seq + head, :256, :]
            parts[0, rows, at] = pair[:, :HEAD_DIM]
            parts[1, rows, at] = pair[:, HEAD_DIM:]
            parts[2, rows, at] = halves_out(dpack[4 * seq + head, 256:, :])
        for shift, part in enumerate((a0, a1, a2, a3)):
            columns[seq, uly ^ shift] = part[64 * seq : 64 * (seq + 1)]
    query, key, value = group_places(uly)
    for number in range(3):
        part = jnp.where(query == number, 0, jnp.where(key == number, 1, 2))
        grad_qkv[:, 192 * number : 192 * (number + 1)] = parts[part]
    finish(moves[0])
    grad = mul_t(grad_qkv[...], weight[...].reshape(WIDE, 640)[:, :576])
    result = in_bf16(grad).reshape(2, 4, 64, WIDE)
    for to in range(4):
        slots[to] = result[:, to]
    out_moves = copies(sems.at[pl.ds(4, 1)], (slots, grad_to))
    finish(moves[1])
    normal, unused = norm_stats(in_f32(rows_in[...].reshape(512, WIDE)))
    sums = jnp.concatenate(
        [
            jnp.sum(grad * normal, axis=0, keepdims=True),
            jnp.sum(grad, axis=0, keepdims=True),
            sums_two[0:2],
            jnp.zeros((60, WIDE), jnp.float32),
        ],
        axis=0,
    )
    finish(moves[2], moves[3])
    grad_weight = mul(normed[...].T, grad_qkv[...])
    grad_out_weight = mul(mixed[...].T, columns[...].reshape(512, 192))
    full[...] = in_bf16(jnp.concatenate([grad_weight, sums.T, grad_out_weight], axis=1)).reshape(8, 96, TAIL)
    for shift in range(4):
        keep[shift] = full[2 * (chip ^ shift) + core]
        send[shift] = full[2 * (chip ^ shift) + 1 - core]
    finish(*out_moves)


def join_ud_kernel(own, from_x, from_y, from_xy, up, down):
    total = own[...] + in_f32(from_x[...]) + in_f32(from_y[...]) + in_f32(from_xy[...])
    up[...] = total[0]
    for number in range(4):
        down[96 * number : 96 * (number + 1), :] = in_bf16(total[1, :, 192 * number : 192 * (number + 1)])


def join_tail_kernel(place, own, from_x, from_y, from_xy, kept, sums, w_out, to_one, to_two, to_three):
    even = lax.rem(place[1], 2) == 0
    total = own[...] + in_f32(from_x[...]) + in_f32(from_y[...]) + in_f32(from_xy[...])
    low = in_bf16(total)
    line = total[:, 512:640].T[64:72]
    kept[...] = total[:, :192]
    w_out[...] = total[:, 640:]
    sums[...] = line
    to_one[:, :192], to_one[:, 192:] = low[:, 192:384], low[:, 576:640]
    to_two[:, :192], to_two[:, 192:] = low[:, 384:576], low[:, 576:640]
    to_three[...] = line


def finish_tail_kernel(place, kept, sums, got_one, got_two, got_three, w_qkv, vectors):
    even = lax.rem(place[1], 2) == 0
    own, one, two = kept[...], in_f32(got_one[:, :192]), in_f32(got_two[:, :192])
    w_qkv[:, :192] = jnp.where(even, own, two)
    w_qkv[:, 192:384] = one
    w_qkv[:, 384:] = jnp.where(even, two, own)
    lines = in_f32(got_one[:, 128:256]) + in_f32(got_two[:, 128:256])
    vectors[...] = lines.T[64:72] + sums[...] + got_three[...]


def finish_rows_kernel(grads, inputs, grad_middle, vectors, grad_inputs):
    grad = in_f32(grads[0]) + in_f32(grads[1]) + in_f32(grads[2]) + in_f32(grads[3])
    normal, scale = norm_stats(in_f32(inputs[...].reshape(128, WIDE)))
    result = norm_back(grad.reshape(128, WIDE), normal, scale, vectors[0:1])
    grad_inputs[...] = grad_middle[...] + result.reshape(2, 64, WIDE)


def chip_sum_kernel(keep, got, own, to_x, to_y, to_xy):
    own[...] = in_f32(keep[0]) + in_f32(got[0])
    for shift, out in ((1, to_x), (2, to_y), (3, to_xy)):
        out[...] = in_bf16(in_f32(keep[shift]) + in_f32(got[shift]))


VMEM_SPEC = pl.BlockSpec(memory_space=pltpu.VMEM)


FAR_SPEC = pl.BlockSpec(memory_space=pltpu.HBM)


def on_core(kernel, outs, operands, scratch=(), grant=16, cost=0, place=False, far=(), far_outs=(), sems=0):
    shapes = [jax.ShapeDtypeStruct(shape, dtype) for shape, dtype in outs]
    specs = [FAR_SPEC if n in far else VMEM_SPEC for n in range(len(operands))]
    if place:
        specs[0] = pl.BlockSpec(memory_space=pltpu.SMEM)
    scratch = [pltpu.VMEM(shape, dtype) for shape, dtype in scratch]
    if sems:
        scratch.append(pltpu.SemaphoreType.DMA((sems,)))
    return pl.pallas_call(
        kernel,
        out_shape=shapes,
        in_specs=specs,
        out_specs=[FAR_SPEC if n in far_outs else VMEM_SPEC for n in range(len(shapes))],
        scratch_shapes=scratch,
        compiler_params=pltpu.CompilerParams(vmem_limit_bytes=(56 if far or far_outs else grant) * 2**20),
        cost_estimate=pl.CostEstimate(flops=int(cost * 10**9), bytes_accessed=0, transcendentals=0),
        name=kernel.__name__,
    )(*operands)


def swap_z(value, shift):
    return lax.ppermute(value, "uly", [(i, i ^ shift) for i in range(4)])


def swap_blk(value, mask):
    return lax.ppermute(value, "blk", [(i, i ^ mask) for i in range(8)])


def swap_parts(parts):
    return [parts[0]] + [swap_z(parts[shift], shift) for shift in (1, 2, 3)]


def sum_blk(keep, send):
    got = swap_blk(send, 1)
    shape = keep.shape[1:]
    own, to_x, to_y, to_xy = on_core(
        chip_sum_kernel, [(shape, jnp.float32)] + [(shape, jnp.bfloat16)] * 3, (keep, got)
    )
    return own, to_x, to_y, to_xy


def swap_sums(own, to_x, to_y, to_xy):
    return own, swap_blk(to_x, 2), swap_blk(to_y, 4), swap_blk(to_xy, 6)


def after(value, *others):
    return lax.optimization_barrier((value,) + others)[0]


DOWN_MOVES = [(b * 4 + u, (2 * (u ^ (b // 2)) + b % 2) * 4 + b // 2) for b in range(8) for u in range(4)]


def local_fast(
    inputs,
    doc_starts,
    out_grad,
    first_gain,
    first_bias,
    query_key_value_weight,
    attention_out_weight,
    second_gain,
    second_bias,
    up_weight,
    down_weight,
):
    bf16, f32 = jnp.bfloat16, jnp.float32
    blk, uly = lax.axis_index("blk"), lax.axis_index("uly")
    place = jnp.stack([blk, uly]).astype(jnp.int32)
    square = (WIDE, WIDE)

    to_one, to_two, shared = on_core(
        send_kernel,
        [((208, 192), bf16), ((208, 192), bf16), ((32, WIDE), bf16)],
        [place, query_key_value_weight, attention_out_weight, doc_starts],
        scratch=[((96, 576), bf16), ((96, 192), bf16), ((2, 64), jnp.int32)],
        place=True,
        far=(1, 2, 3),
        sems=3,
    )
    got_one, got_two = swap_z(to_one, 1), swap_z(to_two, 2)
    x_own = after(inputs, to_one, to_two)
    to_three = jnp.concatenate([x_own.reshape(128, WIDE), shared], axis=0)
    x_parts = [inputs, swap_z(x_own, 1), swap_z(x_own, 2), swap_z(to_three, 3)]
    (qkv_shard,) = on_core(
        shard_kernel,
        [((96, 640), bf16)],
        [place, query_key_value_weight, got_one, got_two]
        + [jnp.stack([first_gain, first_bias, second_gain, second_bias])],
        place=True,
    )
    w_qkv = lax.all_gather(qkv_shard, "blk", axis=0)
    down_shard = lax.ppermute(down_weight, ("blk", "uly"), DOWN_MOVES)
    x_parts[0], down_shard = lax.optimization_barrier((inputs, down_shard))

    pack, normed_one, rows, vectors = on_core(
        first_kernel,
        [((8, PACK, 128), bf16), ((512, WIDE), bf16), ((2, 4, 64, WIDE), bf16), ((8, WIDE), f32)],
        [place] + x_parts + [got_one, got_two, doc_starts, w_qkv],
        scratch=[((3, 512, 192), bf16)],
        place=True,
    )
    g_own = after(out_grad, normed_one)
    g_one, g_three = swap_z(g_own, 1), swap_z(g_own, 3)
    (weights,) = on_core(
        weights_kernel,
        [((96, 2 * WIDE), bf16)],
        [down_shard, attention_out_weight, after(got_one, pack), got_two, x_parts[3]],
    )
    ups = lax.all_gather(up_weight, "blk", axis=0)
    pack = lax.all_to_all(pack, "blk", 0, 0, tiled=True)
    pack, g_three = lax.optimization_barrier((pack, g_three))

    head_rows = ((FULL_TOK, HEAD_DIM), bf16)
    head_cols = ((HEAD_DIM, FULL_TOK), bf16)
    attn_pack, out_cols, log_row = on_core(
        attn_forward_kernel,
        [((8, 128, 128), bf16), ((HEAD_DIM, FULL_TOK), f32), ((1, FULL_TOK), f32)],
        [pack],
        scratch=[head_rows, head_rows, head_cols, ((2, TILES, TILE, TILE), f32), ((2, FULL_TOK, TILE), bf16)],
    )
    weights, g_own = lax.optimization_barrier((weights, out_grad, attn_pack))[:2]
    weights = lax.all_gather(weights, "blk", axis=0)
    attn_pack = lax.all_to_all(attn_pack, "blk", 0, 0, tiled=True)
    g_two = swap_z(g_own, 2)
    g_parts = [out_grad, g_one, g_two, g_three]

    tok_rows = ((512, WIDE), bf16)
    own_rows = ((2, 64, WIDE), bf16)
    attn_pack = lax.all_gather(attn_pack.reshape(2, 4, 128, 128)[:, :3], "uly", axis=0)
    *grad_norm, mixed, middle_own, normed_two, act, grad_pre, w_out, w_down, grad_branch = on_core(
        middle_kernel,
        [own_rows] * 4 + [tok_rows, ((2, 64, WIDE), f32)] + [tok_rows] * 3 + [(square, bf16)] * 2 + [tok_rows],
        [place, attn_pack, rows, weights, ups] + g_parts + [vectors],
        scratch=[
            ((4, 2, 64, WIDE), bf16),
            tok_rows,
            ((2, 4, 64, WIDE), bf16),
            ((2, 8, 96, WIDE), bf16),
            ((8, 96, WIDE), bf16),
            ((2, 4, 64, WIDE), bf16),
            ((2, 4, WIDE, 192), bf16),
            (square, bf16),
            (square, bf16),
            tok_rows,
            ((2, 64, WIDE), f32),
            tok_rows,
            tok_rows,
            tok_rows,
        ],
        cost=5,
        place=True,
        far=(2, 3, 4),
        far_outs=tuple(range(12)),
        sems=16,
    )
    grad_norm = swap_parts(grad_norm)
    feed, keep, send = on_core(
        feed_grads_kernel,
        [((2, 256, WIDE), bf16), ((4, 2, 96, WIDE), bf16), ((4, 2, 96, WIDE), bf16)],
        [place, normed_two, act, grad_pre, grad_branch, w_down],
        scratch=[((8, 96, WIDE), bf16), ((8, 96, WIDE), bf16), tok_rows, (square, bf16)],
        place=True,
        cost=4,
        far=(4, 5),
        sems=2,
    )
    grad_norm[0], keep, send = lax.optimization_barrier((grad_norm[0], keep, send))
    grad_middle, grad_pack, sums_two, *grad_cols = on_core(
        second_back_kernel,
        [((2, 64, WIDE), f32), ((8, 4, 32, 128), bf16), ((8, WIDE), f32)] + [((128, 192), bf16)] * 4,
        [place] + grad_norm + [middle_own, out_grad, w_out, vectors],
        scratch=[((4, 128, 192), bf16), ((2, 64, WIDE), f32), (square, bf16)],
        place=True,
        cost=2,
        far=(7,),
        far_outs=(0, 3, 4, 5, 6),
        sems=6,
    )
    grad_pack = lax.all_to_all(grad_pack.reshape(32, 32, 128), ("blk", "uly"), 0, 0, tiled=True)
    feed = in_f32(lax.psum_scatter(after(feed, grad_pack), "uly", scatter_dimension=1, tiled=True))
    output = in_bf16(middle_own + branch_scale * feed)
    sums = sum_blk(keep, send)
    grad_pack = after(grad_pack, *sums)
    sums = swap_sums(*sums)

    (dpack,) = on_core(
        attn_backward_kernel,
        [((8, 384, 128), bf16)],
        [pack, grad_pack, out_cols, log_row],
        scratch=[head_rows] * 4 + [head_cols] + [((1, FULL_TOK), f32)] * 2 + [((HEAD_DIM, FULL_TOK), f32)] + [((2, TILE, FULL_TOK), bf16)] * 2,
    )
    dpack, *sums = lax.optimization_barrier([dpack] + list(sums))
    g_w_up, g_w_down = on_core(join_ud_kernel, [((96, WIDE), f32), ((384, 192), bf16)], sums)
    grad_cols = swap_parts([after(part, dpack) for part in grad_cols])
    dpack = lax.all_to_all(dpack, "blk", 0, 0, tiled=True)
    grad_norm, keep, send = on_core(
        last_kernel,
        [((4, 2, 64, WIDE), bf16)] + [((4, 96, TAIL), bf16)] * 2,
        [place, dpack, w_qkv, rows, normed_one, sums_two, mixed] + grad_cols,
        scratch=[
            ((512, 576), bf16),
            ((3, 512, 192), bf16),
            ((4, 2, 64, WIDE), bf16),
            ((8, 96, TAIL), bf16),
            ((2, 4, 64, 192), bf16),
            ((8, 96, 640), bf16),
            ((2, 4, 64, WIDE), bf16),
            tok_rows,
            tok_rows,
        ],
        grant=24,
        place=True,
        far=(2, 3, 4, 6),
        far_outs=(0,),
        sems=5,
        cost=3,
    )
    grad_norm = lax.all_to_all(grad_norm, "uly", 0, 0, tiled=True)
    kept, sums, g_w_out, to_one, to_two, to_three = on_core(
        join_tail_kernel,
        [((96, 192), f32), ((8, 96), f32), ((96, 192), f32), ((96, 256), bf16), ((96, 256), bf16), ((8, 96), f32)],
        [place] + list(swap_sums(*sum_blk(keep, send))),
        place=True,
    )
    g_w_down = lax.ppermute(after(g_w_down, to_one), ("blk", "uly"), [(to, at) for at, to in DOWN_MOVES])
    g_w_qkv, d_vectors = on_core(
        finish_tail_kernel,
        [((96, 576), f32), ((8, 96), f32)],
        [place, kept, sums, swap_z(to_one, 1), swap_z(to_two, 2), swap_z(to_three, 3)],
        place=True,
    )
    (grad_inputs,) = on_core(
        finish_rows_kernel, [((2, 64, WIDE), f32)], [grad_norm, inputs, grad_middle, vectors]
    )
    return (
        output,
        grad_inputs,
        d_vectors[0],
        d_vectors[1],
        g_w_qkv,
        g_w_out,
        d_vectors[2],
        d_vectors[3],
        g_w_up,
        in_f32(g_w_down),
    )


def solution(mesh):
    local = local_fast if fits_fast(mesh) else local_general
    placed = (
        P(None, ("blk", "uly"), None),
        P(None, ("blk", "uly")),
        P(None, ("blk", "uly"), None),
        P("blk"),
        P("blk"),
        P("blk", "uly"),
        P("blk", "uly"),
        P("blk"),
        P("blk"),
        P("blk", "uly"),
        P("blk", "uly"),
    )
    return jax.shard_map(
        local,
        mesh=mesh,
        in_specs=placed,
        out_specs=(
            P(None, ("blk", "uly"), None),
            P(None, ("blk", "uly"), None),
            P("blk"),
            P("blk"),
            P("blk", "uly"),
            P("blk", "uly"),
            P("blk"),
            P("blk"),
            P("blk", "uly"),
            P("blk", "uly"),
        ),
        check_vma=False,
    )
```

```python
import functools
import math

import jax
import jax.numpy as jnp
from jax import lax
from jax.experimental import pallas as pl
from jax.experimental.pallas import tpu as pltpu
from jax.sharding import PartitionSpec as P

HEAD_DIM = 64


branch_scale = 48.0 ** (-0.5)
norm_epsilon = 1e-05
neg_large = -1e30


def layer_norm(values, gain_vec, shift_vec):
    center = values - jnp.mean(values, axis=-1, keepdims=True)
    spread = jnp.mean(center * center, axis=-1, keepdims=True)
    return center * lax.rsqrt(spread + norm_epsilon) * gain_vec + shift_vec


def smooth_gate(values):
    return jax.nn.gelu(values, approximate=True)


def project(left, right):
    return jnp.einsum("stk,kn->stn", left, right, preferred_element_type=jnp.float32)


def project_back(left, right):
    return jnp.einsum("stn,kn->stk", left, right, preferred_element_type=jnp.float32)


def weight_grad(left, right):
    return jnp.einsum("stk,stn->kn", left, right, preferred_element_type=jnp.float32)


def visible(query_pos, query_first, key_pos):
    return (key_pos[None, :] <= query_pos[:, None]) & (key_pos[None, :] >= query_first[:, None])


def live_pair(query_pos, query_first, key_pos):
    return (key_pos[0] <= query_pos[-1]) & (key_pos[-1] >= query_first[0])


def forward_pair(carried, queries, key_rows, value_rows, query_pos, query_first, key_pos):
    run_max, run_sum, run_acc = carried
    score_scale = queries.shape[-1] ** (-0.5)
    scores = (
        jnp.einsum("qhd,khd->hqk", queries, key_rows, preferred_element_type=jnp.float32)
        * score_scale
    )
    allowed = visible(query_pos, query_first, key_pos)[None]
    scores = jnp.where(allowed, scores, neg_large)
    new_max = jnp.maximum(run_max, jnp.max(scores, axis=-1))
    weights = jnp.where(allowed, jnp.exp(scores - new_max[..., None]), 0.0)
    factor = jnp.exp(run_max - new_max)
    new_sum = factor * run_sum + jnp.sum(weights, axis=-1)
    attention_mixed = jnp.einsum(
        "hqk,khd->hqd", weights.astype(jnp.bfloat16), value_rows, preferred_element_type=jnp.float32
    )
    return (new_max, new_sum, factor[..., None] * run_acc + attention_mixed)


def backward_pair(
    queries,
    grad_rows,
    log_sum,
    delta_rows,
    key_rows,
    value_rows,
    query_pos,
    query_first,
    key_pos,
    want_query,
    want_keys,
):
    score_scale = queries.shape[-1] ** (-0.5)
    scores = (
        jnp.einsum("qhd,khd->hqk", queries, key_rows, preferred_element_type=jnp.float32)
        * score_scale
    )
    allowed = visible(query_pos, query_first, key_pos)[None]
    probs = jnp.where(
        allowed, jnp.exp(jnp.where(allowed, scores, neg_large) - log_sum[..., None]), 0.0
    )
    grad_probs = jnp.einsum(
        "qhd,khd->hqk", grad_rows, value_rows, preferred_element_type=jnp.float32
    )
    grad_scores = (probs * (grad_probs - delta_rows[..., None])).astype(jnp.bfloat16)
    results = ()
    if want_query:
        results = results + (
            jnp.einsum("hqk,khd->qhd", grad_scores, key_rows, preferred_element_type=jnp.float32)
            * score_scale,
        )
    if want_keys:
        grad_key_rows = (
            jnp.einsum("hqk,qhd->khd", grad_scores, queries, preferred_element_type=jnp.float32)
            * score_scale
        )
        grad_value_rows = jnp.einsum(
            "hqk,qhd->khd",
            probs.astype(jnp.bfloat16),
            grad_rows,
            preferred_element_type=jnp.float32,
        )
        results = results + (grad_key_rows, grad_value_rows)
    return results


def each_block(update, carried, arrays, row_limit):
    total_rows = arrays[0].shape[1]
    span_rows = math.gcd(total_rows, row_limit)
    block_count = total_rows // span_rows
    split_arrays = tuple(
        (
            jnp.swapaxes(
                member.reshape((member.shape[0], block_count, span_rows) + member.shape[2:]), 0, 1
            )
            for member in arrays
        )
    )

    def advance(running, inputs):
        number, blocks = inputs
        return (update(running, blocks, number * span_rows), None)

    result, unused = lax.scan(
        advance, carried, (jnp.arange(block_count, dtype=jnp.int32), split_arrays)
    )
    return result


def local_general(
    inputs,
    doc_starts,
    out_grad,
    first_gain,
    first_bias,
    query_key_value_weight,
    attention_out_weight,
    second_gain,
    second_bias,
    up_weight,
    down_weight,
):
    groups = lax.axis_size("uly")
    cycle_place = lax.axis_index("blk")
    seq_count, tok_dev, model_width = inputs.shape
    block_rows = tok_dev * groups
    group_width = model_width // groups
    heads_here = group_width // HEAD_DIM
    qkv_cols, attn_cols, up_cols, down_cols = (
        lax.all_gather(query_key_value_weight, "uly", axis=1, tiled=True),
        lax.all_gather(attention_out_weight, "uly", axis=1, tiled=True),
        lax.all_gather(up_weight, "uly", axis=1, tiled=True),
        lax.all_gather(down_weight, "uly", axis=1, tiled=True),
    )
    gathered = (
        lax.all_gather(qkv_cols, "blk", axis=0, tiled=True),
        lax.all_gather(attn_cols, "blk", axis=0, tiled=True),
        lax.all_gather(up_cols, "blk", axis=0, tiled=True),
        lax.all_gather(down_cols, "blk", axis=0, tiled=True),
        lax.all_gather(first_gain, "blk", axis=0, tiled=True),
        lax.all_gather(first_bias, "blk", axis=0, tiled=True),
        lax.all_gather(second_gain, "blk", axis=0, tiled=True),
        lax.all_gather(second_bias, "blk", axis=0, tiled=True),
    )
    wide_qkv, wide_attn, wide_up, wide_down = (gathered[0], gathered[1], gathered[2], gathered[3])
    gain_one = gathered[4].astype(jnp.float32)
    bias_one = gathered[5].astype(jnp.float32)
    gain_two = gathered[6].astype(jnp.float32)
    bias_two = gathered[7].astype(jnp.float32)
    residual = inputs.astype(jnp.float32)
    first_normalized, norm_one_back = jax.vjp(layer_norm, residual, gain_one, bias_one)
    normed_low = first_normalized.astype(jnp.bfloat16)
    query_key_value = project(normed_low, wide_qkv).astype(jnp.bfloat16)
    packed = query_key_value.reshape(seq_count, tok_dev, 3, groups, group_width)
    spread = lax.all_to_all(packed, "uly", split_axis=3, concat_axis=1, tiled=True)
    query_flat = spread[:, :, 0, 0]
    key_flat = spread[:, :, 1, 0]
    value_flat = spread[:, :, 2, 0]
    queries = query_flat.reshape(seq_count, block_rows, heads_here, HEAD_DIM)
    key_heads = key_flat.reshape(seq_count, block_rows, heads_here, HEAD_DIM)
    value_heads = value_flat.reshape(seq_count, block_rows, heads_here, HEAD_DIM)
    firsts = lax.all_gather(doc_starts, "uly", axis=1, tiled=True)
    query_pos = cycle_place * block_rows + jnp.arange(block_rows, dtype=jnp.int32)

    def forward_update(carried, blocks, first_row):
        span_rows = blocks[0].shape[1]
        key_pos = first_row + jnp.arange(span_rows, dtype=jnp.int32)
        new_max, new_sum, new_acc = ([], [], [])
        for seq_index in range(seq_count):
            one_state = (carried[0][seq_index], carried[1][seq_index], carried[2][seq_index])
            key_one = blocks[0][seq_index].reshape(span_rows, heads_here, HEAD_DIM)
            value_one = blocks[1][seq_index].reshape(span_rows, heads_here, HEAD_DIM)

            def advance_state(state_in):
                return forward_pair(
                    state_in,
                    queries[seq_index],
                    key_one,
                    value_one,
                    query_pos,
                    firsts[seq_index],
                    key_pos,
                )

            def keep_state(state_in):
                return state_in

            updated = lax.cond(
                live_pair(query_pos, firsts[seq_index], key_pos),
                advance_state,
                keep_state,
                one_state,
            )
            new_max.append(updated[0])
            new_sum.append(updated[1])
            new_acc.append(updated[2])
        return (jnp.stack(new_max), jnp.stack(new_sum), jnp.stack(new_acc))

    start_state = (
        jnp.full((seq_count, heads_here, block_rows), neg_large, jnp.float32),
        jnp.zeros((seq_count, heads_here, block_rows), jnp.float32),
        jnp.zeros((seq_count, heads_here, block_rows, HEAD_DIM), jnp.float32),
    )
    run_max, run_sum, run_acc = each_block(
        forward_update,
        start_state,
        (
            lax.all_gather(key_flat, "blk", axis=1, tiled=True),
            lax.all_gather(value_flat, "blk", axis=1, tiled=True),
        ),
        block_rows,
    )
    attn_heads = jnp.swapaxes(run_acc / run_sum[..., None], 1, 2)
    log_sum = run_max + jnp.log(run_sum)
    attn_low = attn_heads.reshape(seq_count, block_rows, 1, group_width).astype(jnp.bfloat16)
    back_rows = lax.all_to_all(attn_low, "uly", split_axis=1, concat_axis=2, tiled=True).reshape(
        seq_count, tok_dev, model_width
    )
    attention_projected = project(back_rows, wide_attn)
    middle = residual + branch_scale * attention_projected
    second_normalized, norm_two_back = jax.vjp(layer_norm, middle, gain_two, bias_two)
    normed_two_low = second_normalized.astype(jnp.bfloat16)
    before_activation = project(normed_two_low, wide_up)
    act_value, gate_back = jax.vjp(smooth_gate, before_activation)
    act_low = act_value.astype(jnp.bfloat16)
    feedforward_output = project(act_low, wide_down)
    output = (middle + branch_scale * feedforward_output).astype(jnp.bfloat16)
    grad_res = out_grad.astype(jnp.float32)
    grad_branch = (branch_scale * grad_res).astype(jnp.bfloat16)
    grad_w_down = weight_grad(act_low, grad_branch)
    grad_act = project_back(grad_branch, wide_down)
    grad_pre = gate_back(grad_act)[0].astype(jnp.bfloat16)
    grad_w_up = weight_grad(normed_two_low, grad_pre)
    grad_norm_two = project_back(grad_pre, wide_up)
    grad_mid_part, grad_gain_two, grad_bias_two = norm_two_back(grad_norm_two)
    grad_middle = grad_res + grad_mid_part
    grad_attn = (branch_scale * grad_middle).astype(jnp.bfloat16)
    grad_w_attn = weight_grad(back_rows, grad_attn)
    grad_mixed = project_back(grad_attn, wide_attn).astype(jnp.bfloat16)
    grad_spread = lax.all_to_all(
        grad_mixed.reshape(seq_count, tok_dev, groups, group_width),
        "uly",
        split_axis=2,
        concat_axis=1,
        tiled=True,
    )
    grad_flat = grad_spread[:, :, 0]
    grad_heads = grad_flat.reshape(seq_count, block_rows, heads_here, HEAD_DIM)
    delta_rows = jnp.swapaxes(jnp.sum(attn_heads * grad_heads.astype(jnp.float32), axis=-1), 1, 2)

    def query_update(grad_query, blocks, first_row):
        span_rows = blocks[0].shape[1]
        key_pos = first_row + jnp.arange(span_rows, dtype=jnp.int32)
        new_terms = []
        for seq_index in range(seq_count):
            key_one = blocks[0][seq_index].reshape(span_rows, heads_here, HEAD_DIM)
            value_one = blocks[1][seq_index].reshape(span_rows, heads_here, HEAD_DIM)

            def query_compute_terms(unused):
                return backward_pair(
                    queries[seq_index],
                    grad_heads[seq_index],
                    log_sum[seq_index],
                    delta_rows[seq_index],
                    key_one,
                    value_one,
                    query_pos,
                    firsts[seq_index],
                    key_pos,
                    True,
                    False,
                )[0]

            def query_zero_terms(unused):
                return jnp.zeros((block_rows, heads_here, HEAD_DIM), jnp.float32)

            new_terms.append(
                grad_query[seq_index]
                + lax.cond(
                    live_pair(query_pos, firsts[seq_index], key_pos),
                    query_compute_terms,
                    query_zero_terms,
                    0,
                )
            )
        return jnp.stack(new_terms)

    grad_query = each_block(
        query_update,
        jnp.zeros((seq_count, block_rows, heads_here, HEAD_DIM), jnp.float32),
        (
            lax.all_gather(key_flat, "blk", axis=1, tiled=True),
            lax.all_gather(value_flat, "blk", axis=1, tiled=True),
        ),
        block_rows,
    )

    def key_update(carried, blocks, first_row):
        span_rows = blocks[0].shape[1]
        other_pos = first_row + jnp.arange(span_rows, dtype=jnp.int32)
        key_sums, value_sums = ([], [])
        for seq_index in range(seq_count):
            query_one = blocks[0][seq_index].reshape(span_rows, heads_here, HEAD_DIM)
            grad_one = blocks[1][seq_index].reshape(span_rows, heads_here, HEAD_DIM)
            lse_one = jnp.transpose(blocks[2][seq_index])
            delta_one = jnp.transpose(blocks[3][seq_index])
            first_one = blocks[4][seq_index]

            def key_compute_terms(unused):
                return backward_pair(
                    query_one,
                    grad_one,
                    lse_one,
                    delta_one,
                    key_heads[seq_index],
                    value_heads[seq_index],
                    other_pos,
                    first_one,
                    query_pos,
                    False,
                    True,
                )

            def key_zero_terms(unused):
                zero_rows = jnp.zeros((block_rows, heads_here, HEAD_DIM), jnp.float32)
                return (zero_rows, zero_rows)

            terms = lax.cond(
                live_pair(other_pos, first_one, query_pos), key_compute_terms, key_zero_terms, 0
            )
            key_sums.append(carried[0][seq_index] + terms[0])
            value_sums.append(carried[1][seq_index] + terms[1])
        return (jnp.stack(key_sums), jnp.stack(value_sums))

    zero_heads = jnp.zeros((seq_count, block_rows, heads_here, HEAD_DIM), jnp.float32)
    grad_keys, grad_values = each_block(
        key_update,
        (zero_heads, zero_heads),
        (
            lax.all_gather(query_flat, "blk", axis=1, tiled=True),
            lax.all_gather(grad_flat, "blk", axis=1, tiled=True),
            lax.all_gather(
                jnp.swapaxes(log_sum, 1, 2).astype(jnp.bfloat16), "blk", axis=1, tiled=True
            ).astype(jnp.float32),
            lax.all_gather(
                jnp.swapaxes(delta_rows, 1, 2).astype(jnp.bfloat16), "blk", axis=1, tiled=True
            ).astype(jnp.float32),
            lax.all_gather(firsts, "blk", axis=1, tiled=True),
        ),
        block_rows,
    )
    grad_query_flat = grad_query.reshape(seq_count, block_rows, group_width)
    grad_key_flat = grad_keys.reshape(seq_count, block_rows, group_width)
    grad_value_flat = grad_values.reshape(seq_count, block_rows, group_width)
    stacked = jnp.stack([grad_query_flat, grad_key_flat, grad_value_flat], axis=2).astype(
        jnp.bfloat16
    )
    stacked = stacked.reshape(seq_count, block_rows, 3, 1, group_width)
    grad_qkv = lax.all_to_all(stacked, "uly", split_axis=1, concat_axis=3, tiled=True).reshape(
        seq_count, tok_dev, 3 * model_width
    )
    grad_w_qkv = weight_grad(normed_low, grad_qkv)
    grad_norm_one = project_back(grad_qkv, wide_qkv)
    grad_in_part, grad_gain_one, grad_bias_one = norm_one_back(grad_norm_one)
    grad_inputs = grad_middle + grad_in_part
    column_sums = (
        lax.psum_scatter(
            grad_w_qkv.astype(jnp.bfloat16), "uly", scatter_dimension=1, tiled=True
        ).astype(jnp.float32),
        lax.psum_scatter(
            grad_w_attn.astype(jnp.bfloat16), "uly", scatter_dimension=1, tiled=True
        ).astype(jnp.float32),
        lax.psum_scatter(
            grad_w_up.astype(jnp.bfloat16), "uly", scatter_dimension=1, tiled=True
        ).astype(jnp.float32),
        lax.psum_scatter(
            grad_w_down.astype(jnp.bfloat16), "uly", scatter_dimension=1, tiled=True
        ).astype(jnp.float32),
        lax.psum_scatter(
            jnp.tile(grad_gain_one, groups).astype(jnp.bfloat16),
            "uly",
            scatter_dimension=0,
            tiled=True,
        ).astype(jnp.float32),
        lax.psum_scatter(
            jnp.tile(grad_bias_one, groups).astype(jnp.bfloat16),
            "uly",
            scatter_dimension=0,
            tiled=True,
        ).astype(jnp.float32),
        lax.psum_scatter(
            jnp.tile(grad_gain_two, groups).astype(jnp.bfloat16),
            "uly",
            scatter_dimension=0,
            tiled=True,
        ).astype(jnp.float32),
        lax.psum_scatter(
            jnp.tile(grad_bias_two, groups).astype(jnp.bfloat16),
            "uly",
            scatter_dimension=0,
            tiled=True,
        ).astype(jnp.float32),
    )
    owned = (
        lax.psum_scatter(column_sums[0], "blk", scatter_dimension=0, tiled=True),
        lax.psum_scatter(column_sums[1], "blk", scatter_dimension=0, tiled=True),
        lax.psum_scatter(column_sums[2], "blk", scatter_dimension=0, tiled=True),
        lax.psum_scatter(column_sums[3], "blk", scatter_dimension=0, tiled=True),
        lax.psum_scatter(column_sums[4], "blk", scatter_dimension=0, tiled=True),
        lax.psum_scatter(column_sums[5], "blk", scatter_dimension=0, tiled=True),
        lax.psum_scatter(column_sums[6], "blk", scatter_dimension=0, tiled=True),
        lax.psum_scatter(column_sums[7], "blk", scatter_dimension=0, tiled=True),
    )
    return (
        output,
        grad_inputs,
        owned[4],
        owned[5],
        owned[0],
        owned[1],
        owned[6],
        owned[7],
        owned[2],
        owned[3],
    )


FULL_TOK = 2048
TILE = 256
TILES = FULL_TOK // TILE
LOG2E = 1.4426950408889634
WIDE = 768
PACK = 400
ACROSS = (((1,), (1,)), ((), ()))


def fits_fast(mesh):
    return dict(mesh.shape) == {"blk": 8, "uly": 4}


def halves_in(rows):
    half = rows.shape[-2] // 2
    return jnp.concatenate([rows[..., :half, :], rows[..., half:, :]], axis=-1)


def halves_out(packed):
    half = packed.shape[-1] // 2
    return jnp.concatenate([packed[..., :half], packed[..., half:]], axis=-2)


def in_f32(value):
    return value.astype(jnp.float32)


def in_bf16(value):
    return value.astype(jnp.bfloat16)


def norm_stats(values):
    center = values - jnp.mean(values, axis=-1, keepdims=True)
    scale = lax.rsqrt(jnp.mean(center * center, axis=-1, keepdims=True) + norm_epsilon)
    return center * scale, scale


def norm_back(grad_out, normal, scale, gain):
    grad_normal = grad_out * gain
    mean_one = jnp.mean(grad_normal, axis=-1, keepdims=True)
    mean_two = jnp.mean(grad_normal * normal, axis=-1, keepdims=True)
    return (grad_normal - mean_one - normal * mean_two) * scale


def mul(left, right):
    return jnp.dot(left, right, preferred_element_type=jnp.float32)


def mul_t(left, right):
    return lax.dot_general(left, right, ACROSS, preferred_element_type=jnp.float32)


def copies(sems, *pairs):
    moves = [pltpu.make_async_copy(source, target, sems.at[n]) for n, (source, target) in enumerate(pairs)]
    for move in moves:
        move.start()
    return moves


def finish(*moves):
    for move in moves:
        move.wait()


def group_places(uly):
    query = jnp.minimum(uly, 2)
    key = 1 - lax.rem((uly + 1) // 2, 2)
    return query, key, 3 - query - key


def send_kernel(place, weight_in, out_in, starts_in, to_one, to_two, shared, weight, out_weight, doc_starts, sems):
    finish(*copies(sems, (weight_in, weight), (out_in, out_weight), (starts_in, doc_starts)))
    even = lax.rem(place[1], 2) == 0
    groups = [weight[:, 192 * number : 192 * (number + 1)] for number in range(3)]
    starts = doc_starts[...]
    starts = in_f32(jnp.concatenate([starts // 128, lax.rem(starts, 128), jnp.zeros_like(starts)], axis=1))
    lines = jnp.concatenate([in_f32(out_weight[...]), starts, jnp.zeros((30, 192), jnp.float32)], axis=0)
    lines = in_bf16(lines)
    to_one[:96, :] = groups[1]
    to_two[:96, :] = jnp.where(even, groups[2], groups[0])
    to_one[96:, :] = lines[:112]
    to_two[96:, :] = lines[:112]
    for number in range(4):
        shared[:, 192 * number : 192 * (number + 1)] = lines[32 * number : 32 * (number + 1)]


def shard_kernel(place, weight, got_one, got_two, vectors, shard):
    even = lax.rem(place[1], 2) == 0
    shard[:, :192] = jnp.where(even, weight[:, :192], weight[:, 384:])
    shard[:, 192:384] = got_one[:96, :]
    shard[:, 384:576] = got_two[:96, :]
    lines = jnp.concatenate([in_f32(vectors[...]), jnp.zeros((60, 96), jnp.float32)], axis=0)
    shard[:, 576:] = in_bf16(lines.T)


def weights_kernel(down, out_weight, got_one, got_two, got_three, weights):
    for number in range(4):
        at = slice(192 * number, 192 * (number + 1))
        weights[:, at] = down[96 * number : 96 * (number + 1), :]
        at = slice(WIDE + 192 * number, WIDE + 192 * (number + 1))
        if number < 3:
            weights[:, at] = (out_weight[...], got_one[96:192, :], got_two[96:192, :])[number]
        else:
            for part in range(3):
                weights[32 * part : 32 * (part + 1), at] = got_three[128:, 192 * part : 192 * (part + 1)]


def first_kernel(place, x0, x1, x2, x3, got_one, got_two, doc_starts, weight, pack, normed, rows, vectors, parts):
    uly = place[1]
    for shift, part in enumerate((x0, x1, x2, x3)):
        for seq in range(2):
            rows[seq, uly ^ shift] = part[64 * seq : 64 * (seq + 1)] if shift == 3 else part[seq]
    full = weight[...].reshape(WIDE, 640)
    own = doc_starts[...]
    known = jnp.concatenate(
        [
            in_f32(jnp.concatenate([own // 128, lax.rem(own, 128)], axis=1)),
            in_f32(got_one[192:208, :128])[:2],
            in_f32(got_two[192:208, :128])[:2],
            in_f32(x3[128:144, 576:704])[:2],
        ],
        axis=0,
    )
    even, low_half = lax.rem(uly, 2) == 0, uly < 2
    for seq in range(2):
        chunks = [known[2 * shift + seq : 2 * shift + seq + 1] for shift in range(4)]
        lines = []
        for part in (slice(0, 64), slice(64, 128)):
            near, next_to, far, far_next = (chunk[:, part] for chunk in chunks)
            near = jnp.where(
                even, jnp.concatenate([near, next_to], axis=1), jnp.concatenate([next_to, near], axis=1)
            )
            far = jnp.where(
                even, jnp.concatenate([far, far_next], axis=1), jnp.concatenate([far_next, far], axis=1)
            )
            lines += [jnp.where(low_half, near, far), jnp.where(low_half, far, near)]
        lines = in_bf16(jnp.concatenate(lines + [jnp.zeros((12, 128), jnp.float32)], axis=0))
        for head in range(3):
            pack[4 * seq + head, 384:, :] = lines
        pack[4 * seq + 3] = jnp.zeros((PACK, 128), jnp.bfloat16)
    vector_rows = in_f32(full[:, 512:640]).T[64:72]
    vectors[...] = vector_rows
    normal, unused = norm_stats(in_f32(rows[...].reshape(512, WIDE)))
    value = in_bf16(normal * vector_rows[0:1] + vector_rows[1:2])
    normed[...] = value
    product = in_bf16(mul(value, full[:, :576]))
    for number in range(3):
        parts[number] = product[:, 192 * number : 192 * (number + 1)]
    queries, keys, values = (parts[at] for at in group_places(uly))
    for seq in range(2):
        at_rows = slice(256 * seq, 256 * (seq + 1))
        for head in range(3):
            at = slice(HEAD_DIM * head, HEAD_DIM * (head + 1))
            pack[4 * seq + head, :256, :] = jnp.concatenate([queries[at_rows, at], keys[at_rows, at]], axis=1)
            pack[4 * seq + head, 256:384, :] = halves_in(values[at_rows, at])


def first_row(pack, tile):
    lines = in_f32(pack[tile, 384:, :])
    high, low = (jnp.concatenate([lines[at : at + 1], lines[at + 1 : at + 2]], axis=1) for at in (0, 2))
    return high * 128.0 + low


def iotas():
    key_at = lax.broadcasted_iota(jnp.int32, (TILE, TILE), 0)
    query_at = lax.broadcasted_iota(jnp.int32, (TILE, TILE), 1)
    return in_f32(key_at), key_at <= query_at


def attn_forward_kernel(pack, packed_out, out_cols, log_row, q_rows, k_rows, v_cols, held, probs):
    scale = LOG2E * HEAD_DIM**-0.5
    for t in range(TILES):
        rows = pl.ds(t * TILE, TILE)
        pair = pack[t, :TILE, :]
        q_rows[rows, :] = pair[:, :HEAD_DIM]
        k_rows[rows, :] = pair[:, HEAD_DIM:]
        v_cols[:, rows] = halves_out(pack[t, TILE:384, :]).T
    key_at, causal = iotas()
    for i in range(TILES):
        q_at = pl.ds(i * TILE, TILE)
        queries = q_rows[q_at, :]
        first = first_row(pack, i)
        top = None
        for j in range(i + 1):
            scores = mul_t(k_rows[pl.ds(j * TILE, TILE), :], queries)
            allowed = key_at >= first - float(j * TILE)
            if j == i:
                allowed = allowed & causal
            scores = jnp.where(allowed, scores * scale, neg_large)
            held[i % 2, j] = scores
            tile_top = jnp.max(scores.reshape(TILE // 8, 8, TILE), axis=0)
            top = tile_top if top is None else jnp.maximum(top, tile_top)
        top = jnp.max(top, axis=0, keepdims=True)
        total = None
        for j in range(i + 1):
            weights = jnp.exp2(held[i % 2, j] - top)
            tile_sum = jnp.sum(weights.reshape(TILE // 8, 8, TILE), axis=0)
            total = tile_sum if total is None else total + tile_sum
            probs[i % 2, pl.ds(j * TILE, TILE), :] = in_bf16(weights)
        seen = pl.ds(0, (i + 1) * TILE)
        acc = mul(v_cols[:, seen], probs[i % 2, seen, :])
        total = jnp.sum(total, axis=0, keepdims=True)
        acc = acc / total
        out_cols[:, q_at] = acc
        log_row[:, q_at] = top + jnp.log2(total)
        packed_out[i] = in_bf16(halves_in(acc.T))


def attn_backward_kernel(
    pack, grad, out_cols, log_row, dpack, q_rows, k_rows, v_rows, g_rows, k_cols, delta, firsts, dq_cols, probs, dscores
):
    scale = LOG2E * HEAD_DIM**-0.5
    for t in range(TILES):
        rows = pl.ds(t * TILE, TILE)
        pair = pack[t, :TILE, :]
        q_rows[rows, :] = pair[:, :HEAD_DIM]
        keys = pair[:, HEAD_DIM:]
        k_rows[rows, :] = keys
        k_cols[:, rows] = keys.T
        v_rows[rows, :] = halves_out(pack[t, TILE:384, :])
        g_tile = halves_out(grad[pl.ds(4 * t, 4)]).reshape(TILE, HEAD_DIM)
        g_rows[rows, :] = g_tile
        delta[:, rows] = jnp.sum(in_f32(g_tile.T) * out_cols[:, rows], axis=0, keepdims=True)
        firsts[:, rows] = first_row(pack, t)
    key_at, causal = iotas()
    for j in range(TILES):
        k_at = pl.ds(j * TILE, TILE)
        keys, values, keys_t = k_rows[k_at, :], v_rows[k_at, :], k_cols[:, k_at]
        for i in range(j, TILES):
            q_at = pl.ds(i * TILE, TILE)
            allowed = key_at >= firsts[:, q_at] - float(j * TILE)
            if i == j:
                allowed = allowed & causal
            scores = mul_t(keys, q_rows[q_at, :]) * scale - log_row[:, q_at]
            weights = jnp.exp2(jnp.where(allowed, scores, neg_large))
            probs[j % 2, :, q_at] = in_bf16(weights)
            dscores[j % 2, :, q_at] = in_bf16(weights * (mul_t(values, g_rows[q_at, :]) - delta[:, q_at]))
        later = pl.ds(j * TILE, FULL_TOK - j * TILE)
        dv = mul(probs[j % 2, :, later], g_rows[later, :])
        dk = mul(dscores[j % 2, :, later], q_rows[later, :])
        dq = mul(keys_t, dscores[j % 2, :, later])
        if j == 0:
            dq_cols[...] = dq
        else:
            dq_cols[:, later] += dq
        dq = (dq_cols[:, k_at] * HEAD_DIM**-0.5).T
        dk = dk * HEAD_DIM**-0.5
        dpack[j, :TILE, :] = in_bf16(jnp.concatenate([dq, dk], axis=1))
        dpack[j, TILE:, :] = halves_in(in_bf16(dv))


def middle_kernel(place, mixed_pack, rows_in, weights_in, up_in, g0, g1, g2, g3, vectors, *refs):
    grad_outs, (mixed_to, middle_to, normed_to, act_to, pre_to) = refs[:4], refs[4:9]
    w_out_to, w_down_to, branch_to = refs[9:12]
    slots, mixed, rows, weights, up, parts, columns, w_out, w_down, grad_branch = refs[12:22]
    middle_own, normed, act_out, pre_out, sems = refs[22:]
    uly = place[1]
    moves = copies(
        sems.at[pl.ds(0, 4)],
        (weights_in.at[:, :, pl.ds(WIDE, WIDE)], weights.at[1]),
        (rows_in, rows),
        (up_in, up),
        (weights_in.at[:, :, pl.ds(0, WIDE)], weights.at[0]),
    )
    for group in range(4):
        for seq in range(2):
            for head in range(3):
                at = 192 * group + HEAD_DIM * head
                mixed[pl.ds(256 * seq, 256), at : at + HEAD_DIM] = halves_out(mixed_pack[group, seq, head])
    out_moves = copies(sems.at[pl.ds(4, 1)], (mixed, mixed_to))
    for shift, part in enumerate((g0, g1, g2, g3)):
        for seq in range(2):
            parts[seq, uly ^ shift] = in_bf16(branch_scale * in_f32(part[seq]))
    grad_branch[...] = parts[...].reshape(512, WIDE)
    out_moves += copies(sems.at[pl.ds(5, 1)], (grad_branch, branch_to))
    finish(moves[0])
    for shift in range(4):
        columns[0, uly ^ shift] = weights[1, :, :, 192 * shift : 192 * (shift + 1)].reshape(WIDE, 192)
    for group in range(4):
        w_out[:, 192 * group : 192 * (group + 1)] = columns[0, group]
    out_moves += copies(sems.at[pl.ds(6, 1)], (w_out, w_out_to))
    projected = mul(mixed[...], w_out[...])
    finish(moves[1])
    middle = in_f32(rows[...].reshape(512, WIDE)) + branch_scale * projected
    normal, unused = norm_stats(middle)
    normed[...] = in_bf16(normal * vectors[2:3] + vectors[3:4])
    chunks = middle.reshape(2, 4, 64, WIDE)
    middle_own[...] = jnp.where(
        uly < 2,
        jnp.where(uly == 0, chunks[:, 0], chunks[:, 1]),
        jnp.where(uly == 2, chunks[:, 2], chunks[:, 3]),
    )
    out_moves += copies(sems.at[pl.ds(8, 2)], (normed, normed_to), (middle_own, middle_to))
    finish(moves[2])
    w_up = up[...].reshape(WIDE, WIDE)
    pre = mul(normed[...], w_up)
    finish(moves[3])
    for at in range(8):
        for number in range(4):
            columns[1, (at // 2) ^ uly, pl.ds(384 * (at % 2) + 96 * number, 96), :] = weights[
                0, at, :, 192 * number : 192 * (number + 1)
            ]
    for group in range(4):
        w_down[:, 192 * group : 192 * (group + 1)] = columns[1, group]
    out_moves += copies(sems.at[pl.ds(7, 1)], (w_down, w_down_to))
    grad_act = mul_t(grad_branch[...], w_down[...])
    square = pre * pre
    bend = jnp.tanh(math.sqrt(2.0 / math.pi) * pre * (1.0 + 0.044715 * square))
    half = 0.5 * (1.0 + bend)
    act_out[...] = in_bf16(pre * half)
    out_moves += copies(sems.at[pl.ds(10, 1)], (act_out, act_to))
    slope = math.sqrt(2.0 / math.pi) * (1.0 + 3 * 0.044715 * square)
    gate = half + 0.5 * pre * (1.0 - bend * bend) * slope
    pre_out[...] = in_bf16(grad_act * gate)
    out_moves += copies(sems.at[pl.ds(11, 1)], (pre_out, pre_to))
    result = in_bf16(mul_t(pre_out[...], w_up)).reshape(2, 4, 64, WIDE)
    for to in range(4):
        slots[to] = result[:, to]
    out_moves += copies(sems.at[pl.ds(12, 4)], *((slots.at[uly ^ n], out) for n, out in enumerate(grad_outs)))
    finish(*out_moves)


def feed_grads_kernel(place, normed, act, grad_pre, branch_in, down_in, feed, keep, send, *refs):
    up_grad, down_grad, grad_branch, w_down, sems = refs
    moves = copies(sems, (branch_in, grad_branch), (down_in, w_down))
    blk, uly = place[0], place[1]
    chip, core = blk // 2, lax.rem(blk, 2)
    up_grad[...] = in_bf16(mul(normed[...].T, grad_pre[...])).reshape(8, 96, WIDE)
    finish(*moves)
    grad = in_bf16(mul(act[...].T, grad_branch[...]))
    for group in range(4):
        for half in range(2):
            for number in range(4):
                at = 384 * half + 96 * number
                down_grad[2 * (group ^ uly) + half, :, 192 * number : 192 * (number + 1)] = grad[
                    at : at + 96, 192 * group : 192 * (group + 1)
                ]
    for shift in range(4):
        same, other = 2 * (chip ^ shift) + core, 2 * (chip ^ shift) + 1 - core
        keep[shift, 0], keep[shift, 1] = up_grad[same], down_grad[same]
        send[shift, 0], send[shift, 1] = up_grad[other], down_grad[other]
    feed[...] = in_bf16(mul(act[...], w_down[...])).reshape(2, 256, WIDE)


def second_back_kernel(
    place, g0, g1, g2, g3, middle, out_grad, w_out_in, vectors, middle_to, pack, sums, a0, a1, a2, a3, *refs
):
    columns, grad_middle, w_out, sems = refs
    uly = place[1]
    moves = copies(sems.at[pl.ds(0, 1)], (w_out_in, w_out))
    grad = in_f32(g0[...]) + in_f32(g1[...]) + in_f32(g2[...]) + in_f32(g3[...])
    grad = grad.reshape(128, WIDE)
    normal, scale = norm_stats(middle[...].reshape(128, WIDE))
    sums[...] = jnp.concatenate(
        [
            jnp.sum(grad * normal, axis=0, keepdims=True),
            jnp.sum(grad, axis=0, keepdims=True),
            jnp.zeros((6, WIDE), jnp.float32),
        ],
        axis=0,
    )
    result = in_f32(out_grad[...].reshape(128, WIDE)) + norm_back(grad, normal, scale, vectors[2:3])
    grad_middle[...] = result.reshape(2, 64, WIDE)
    low = in_bf16(branch_scale * result)
    for group in range(4):
        columns[group] = low[:, 192 * group : 192 * (group + 1)]
    outs = copies(sems.at[pl.ds(1, 1)], (grad_middle, middle_to))
    outs += copies(sems.at[pl.ds(2, 4)], *((columns.at[uly ^ n], out) for n, out in enumerate((a0, a1, a2, a3))))
    finish(*moves)
    mixed = in_bf16(mul_t(low, w_out[...]))
    for group in range(4):
        for seq in range(2):
            rows = mixed[64 * seq : 64 * (seq + 1)]
            for head in range(3):
                at = 192 * group + HEAD_DIM * head
                pack[4 * seq + head, group] = halves_in(rows[:, at : at + HEAD_DIM])
            pack[4 * seq + 3, group] = jnp.zeros((32, 128), jnp.bfloat16)
    finish(*outs)


TAIL = 832


def last_kernel(place, dpack, weight_in, rows_from, normed_from, sums_two, mixed_from, a0, a1, a2, a3, *refs):
    grad_to, keep, send, grad_qkv, parts, slots, full, columns, weight, rows_in, normed, mixed, sems = refs
    blk, uly = place[0], place[1]
    moves = copies(
        sems.at[pl.ds(0, 4)],
        (weight_in, weight),
        (rows_from, rows_in),
        (normed_from, normed),
        (mixed_from, mixed),
    )
    chip, core = blk // 2, lax.rem(blk, 2)
    for seq in range(2):
        rows = pl.ds(256 * seq, 256)
        for head in range(3):
            at = slice(HEAD_DIM * head, HEAD_DIM * (head + 1))
            pair = dpack[4 * seq + head, :256, :]
            parts[0, rows, at] = pair[:, :HEAD_DIM]
            parts[1, rows, at] = pair[:, HEAD_DIM:]
            parts[2, rows, at] = halves_out(dpack[4 * seq + head, 256:, :])
        for shift, part in enumerate((a0, a1, a2, a3)):
            columns[seq, uly ^ shift] = part[64 * seq : 64 * (seq + 1)]
    query, key, value = group_places(uly)
    for number in range(3):
        part = jnp.where(query == number, 0, jnp.where(key == number, 1, 2))
        grad_qkv[:, 192 * number : 192 * (number + 1)] = parts[part]
    finish(moves[0])
    grad = mul_t(grad_qkv[...], weight[...].reshape(WIDE, 640)[:, :576])
    result = in_bf16(grad).reshape(2, 4, 64, WIDE)
    for to in range(4):
        slots[to] = result[:, to]
    out_moves = copies(sems.at[pl.ds(4, 1)], (slots, grad_to))
    finish(moves[1])
    normal, unused = norm_stats(in_f32(rows_in[...].reshape(512, WIDE)))
    sums = jnp.concatenate(
        [
            jnp.sum(grad * normal, axis=0, keepdims=True),
            jnp.sum(grad, axis=0, keepdims=True),
            sums_two[0:2],
            jnp.zeros((60, WIDE), jnp.float32),
        ],
        axis=0,
    )
    finish(moves[2], moves[3])
    grad_weight = mul(normed[...].T, grad_qkv[...])
    grad_out_weight = mul(mixed[...].T, columns[...].reshape(512, 192))
    full[...] = in_bf16(jnp.concatenate([grad_weight, sums.T, grad_out_weight], axis=1)).reshape(8, 96, TAIL)
    for shift in range(4):
        keep[shift] = full[2 * (chip ^ shift) + core]
        send[shift] = full[2 * (chip ^ shift) + 1 - core]
    finish(*out_moves)


def join_ud_kernel(own, from_x, from_y, from_xy, up, down):
    total = own[...] + in_f32(from_x[...]) + in_f32(from_y[...]) + in_f32(from_xy[...])
    up[...] = total[0]
    for number in range(4):
        down[96 * number : 96 * (number + 1), :] = in_bf16(total[1, :, 192 * number : 192 * (number + 1)])


def join_tail_kernel(place, own, from_x, from_y, from_xy, kept, sums, w_out, to_one, to_two, to_three):
    even = lax.rem(place[1], 2) == 0
    total = own[...] + in_f32(from_x[...]) + in_f32(from_y[...]) + in_f32(from_xy[...])
    low = in_bf16(total)
    line = total[:, 512:640].T[64:72]
    kept[...] = total[:, :192]
    w_out[...] = total[:, 640:]
    sums[...] = line
    to_one[:, :192], to_one[:, 192:] = low[:, 192:384], low[:, 576:640]
    to_two[:, :192], to_two[:, 192:] = low[:, 384:576], low[:, 576:640]
    to_three[...] = line


def finish_tail_kernel(place, kept, sums, got_one, got_two, got_three, w_qkv, vectors):
    even = lax.rem(place[1], 2) == 0
    own, one, two = kept[...], in_f32(got_one[:, :192]), in_f32(got_two[:, :192])
    w_qkv[:, :192] = jnp.where(even, own, two)
    w_qkv[:, 192:384] = one
    w_qkv[:, 384:] = jnp.where(even, two, own)
    lines = in_f32(got_one[:, 128:256]) + in_f32(got_two[:, 128:256])
    vectors[...] = lines.T[64:72] + sums[...] + got_three[...]


def finish_rows_kernel(grads, inputs, grad_middle, vectors, grad_inputs):
    grad = in_f32(grads[0]) + in_f32(grads[1]) + in_f32(grads[2]) + in_f32(grads[3])
    normal, scale = norm_stats(in_f32(inputs[...].reshape(128, WIDE)))
    result = norm_back(grad.reshape(128, WIDE), normal, scale, vectors[0:1])
    grad_inputs[...] = grad_middle[...] + result.reshape(2, 64, WIDE)


def chip_sum_kernel(keep, got, own, to_x, to_y, to_xy):
    own[...] = in_f32(keep[0]) + in_f32(got[0])
    for shift, out in ((1, to_x), (2, to_y), (3, to_xy)):
        out[...] = in_bf16(in_f32(keep[shift]) + in_f32(got[shift]))


VMEM_SPEC = pl.BlockSpec(memory_space=pltpu.VMEM)


FAR_SPEC = pl.BlockSpec(memory_space=pltpu.HBM)


def on_core(kernel, outs, operands, scratch=(), grant=16, cost=0, place=False, far=(), far_outs=(), sems=0):
    shapes = [jax.ShapeDtypeStruct(shape, dtype) for shape, dtype in outs]
    specs = [FAR_SPEC if n in far else VMEM_SPEC for n in range(len(operands))]
    if place:
        specs[0] = pl.BlockSpec(memory_space=pltpu.SMEM)
    scratch = [pltpu.VMEM(shape, dtype) for shape, dtype in scratch]
    if sems:
        scratch.append(pltpu.SemaphoreType.DMA((sems,)))
    return pl.pallas_call(
        kernel,
        out_shape=shapes,
        in_specs=specs,
        out_specs=[FAR_SPEC if n in far_outs else VMEM_SPEC for n in range(len(shapes))],
        scratch_shapes=scratch,
        compiler_params=pltpu.CompilerParams(vmem_limit_bytes=(56 if far or far_outs else grant) * 2**20),
        cost_estimate=pl.CostEstimate(flops=int(cost * 10**9), bytes_accessed=0, transcendentals=0),
        name=kernel.__name__,
    )(*operands)


def swap_z(value, shift):
    return lax.ppermute(value, "uly", [(i, i ^ shift) for i in range(4)])


def swap_blk(value, mask):
    return lax.ppermute(value, "blk", [(i, i ^ mask) for i in range(8)])


def swap_parts(parts):
    return [parts[0]] + [swap_z(parts[shift], shift) for shift in (1, 2, 3)]


def sum_blk(keep, send):
    got = swap_blk(send, 1)
    shape = keep.shape[1:]
    own, to_x, to_y, to_xy = on_core(
        chip_sum_kernel, [(shape, jnp.float32)] + [(shape, jnp.bfloat16)] * 3, (keep, got)
    )
    return own, to_x, to_y, to_xy


def swap_sums(own, to_x, to_y, to_xy):
    return own, swap_blk(to_x, 2), swap_blk(to_y, 4), swap_blk(to_xy, 6)


def after(value, *others):
    return lax.optimization_barrier((value,) + others)[0]


DOWN_MOVES = [(b * 4 + u, (2 * (u ^ (b // 2)) + b % 2) * 4 + b // 2) for b in range(8) for u in range(4)]


def local_fast(
    inputs,
    doc_starts,
    out_grad,
    first_gain,
    first_bias,
    query_key_value_weight,
    attention_out_weight,
    second_gain,
    second_bias,
    up_weight,
    down_weight,
):
    bf16, f32 = jnp.bfloat16, jnp.float32
    blk, uly = lax.axis_index("blk"), lax.axis_index("uly")
    place = jnp.stack([blk, uly]).astype(jnp.int32)
    square = (WIDE, WIDE)

    to_one, to_two, shared = on_core(
        send_kernel,
        [((208, 192), bf16), ((208, 192), bf16), ((32, WIDE), bf16)],
        [place, query_key_value_weight, attention_out_weight, doc_starts],
        scratch=[((96, 576), bf16), ((96, 192), bf16), ((2, 64), jnp.int32)],
        place=True,
        far=(1, 2, 3),
        sems=3,
    )
    got_one, got_two = swap_z(to_one, 1), swap_z(to_two, 2)
    x_own = after(inputs, to_one, to_two)
    to_three = jnp.concatenate([x_own.reshape(128, WIDE), shared], axis=0)
    x_parts = [inputs, swap_z(x_own, 1), swap_z(x_own, 2), swap_z(to_three, 3)]
    (qkv_shard,) = on_core(
        shard_kernel,
        [((96, 640), bf16)],
        [place, query_key_value_weight, got_one, got_two]
        + [jnp.stack([first_gain, first_bias, second_gain, second_bias])],
        place=True,
    )
    w_qkv = lax.all_gather(qkv_shard, "blk", axis=0)
    down_shard = lax.ppermute(down_weight, ("blk", "uly"), DOWN_MOVES)
    x_parts[0], down_shard = lax.optimization_barrier((inputs, down_shard))

    pack, normed_one, rows, vectors = on_core(
        first_kernel,
        [((8, PACK, 128), bf16), ((512, WIDE), bf16), ((2, 4, 64, WIDE), bf16), ((8, WIDE), f32)],
        [place] + x_parts + [got_one, got_two, doc_starts, w_qkv],
        scratch=[((3, 512, 192), bf16)],
        place=True,
    )
    g_own = after(out_grad, normed_one)
    g_one, g_three = swap_z(g_own, 1), swap_z(g_own, 3)
    (weights,) = on_core(
        weights_kernel,
        [((96, 2 * WIDE), bf16)],
        [down_shard, attention_out_weight, after(got_one, pack), got_two, x_parts[3]],
    )
    ups = lax.all_gather(up_weight, "blk", axis=0)
    pack = lax.all_to_all(pack, "blk", 0, 0, tiled=True)
    pack, g_three = lax.optimization_barrier((pack, g_three))

    head_rows = ((FULL_TOK, HEAD_DIM), bf16)
    head_cols = ((HEAD_DIM, FULL_TOK), bf16)
    attn_pack, out_cols, log_row = on_core(
        attn_forward_kernel,
        [((8, 128, 128), bf16), ((HEAD_DIM, FULL_TOK), f32), ((1, FULL_TOK), f32)],
        [pack],
        scratch=[head_rows, head_rows, head_cols, ((2, TILES, TILE, TILE), f32), ((2, FULL_TOK, TILE), bf16)],
    )
    weights, g_own = lax.optimization_barrier((weights, out_grad, attn_pack))[:2]
    weights = lax.all_gather(weights, "blk", axis=0)
    attn_pack = lax.all_to_all(attn_pack, "blk", 0, 0, tiled=True)
    g_two = swap_z(g_own, 2)
    g_parts = [out_grad, g_one, g_two, g_three]

    tok_rows = ((512, WIDE), bf16)
    own_rows = ((2, 64, WIDE), bf16)
    attn_pack = lax.all_gather(attn_pack.reshape(2, 4, 128, 128)[:, :3], "uly", axis=0)
    *grad_norm, mixed, middle_own, normed_two, act, grad_pre, w_out, w_down, grad_branch = on_core(
        middle_kernel,
        [own_rows] * 4 + [tok_rows, ((2, 64, WIDE), f32)] + [tok_rows] * 3 + [(square, bf16)] * 2 + [tok_rows],
        [place, attn_pack, rows, weights, ups] + g_parts + [vectors],
        scratch=[
            ((4, 2, 64, WIDE), bf16),
            tok_rows,
            ((2, 4, 64, WIDE), bf16),
            ((2, 8, 96, WIDE), bf16),
            ((8, 96, WIDE), bf16),
            ((2, 4, 64, WIDE), bf16),
            ((2, 4, WIDE, 192), bf16),
            (square, bf16),
            (square, bf16),
            tok_rows,
            ((2, 64, WIDE), f32),
            tok_rows,
            tok_rows,
            tok_rows,
        ],
        cost=5,
        place=True,
        far=(2, 3, 4),
        far_outs=tuple(range(12)),
        sems=16,
    )
    grad_norm = swap_parts(grad_norm)
    feed, keep, send = on_core(
        feed_grads_kernel,
        [((2, 256, WIDE), bf16), ((4, 2, 96, WIDE), bf16), ((4, 2, 96, WIDE), bf16)],
        [place, normed_two, act, grad_pre, grad_branch, w_down],
        scratch=[((8, 96, WIDE), bf16), ((8, 96, WIDE), bf16), tok_rows, (square, bf16)],
        place=True,
        cost=4,
        far=(4, 5),
        sems=2,
    )
    grad_norm[0], keep, send = lax.optimization_barrier((grad_norm[0], keep, send))
    grad_middle, grad_pack, sums_two, *grad_cols = on_core(
        second_back_kernel,
        [((2, 64, WIDE), f32), ((8, 4, 32, 128), bf16), ((8, WIDE), f32)] + [((128, 192), bf16)] * 4,
        [place] + grad_norm + [middle_own, out_grad, w_out, vectors],
        scratch=[((4, 128, 192), bf16), ((2, 64, WIDE), f32), (square, bf16)],
        place=True,
        cost=2,
        far=(7,),
        far_outs=(0, 3, 4, 5, 6),
        sems=6,
    )
    grad_pack = lax.all_to_all(grad_pack.reshape(32, 32, 128), ("blk", "uly"), 0, 0, tiled=True)
    feed = in_f32(lax.psum_scatter(after(feed, grad_pack), "uly", scatter_dimension=1, tiled=True))
    output = in_bf16(middle_own + branch_scale * feed)
    sums = sum_blk(keep, send)
    grad_pack = after(grad_pack, *sums)
    sums = swap_sums(*sums)

    (dpack,) = on_core(
        attn_backward_kernel,
        [((8, 384, 128), bf16)],
        [pack, grad_pack, out_cols, log_row],
        scratch=[head_rows] * 4 + [head_cols] + [((1, FULL_TOK), f32)] * 2 + [((HEAD_DIM, FULL_TOK), f32)] + [((2, TILE, FULL_TOK), bf16)] * 2,
    )
    dpack, *sums = lax.optimization_barrier([dpack] + list(sums))
    g_w_up, g_w_down = on_core(join_ud_kernel, [((96, WIDE), f32), ((384, 192), bf16)], sums)
    grad_cols = swap_parts([after(part, dpack) for part in grad_cols])
    dpack = lax.all_to_all(dpack, "blk", 0, 0, tiled=True)
    grad_norm, keep, send = on_core(
        last_kernel,
        [((4, 2, 64, WIDE), bf16)] + [((4, 96, TAIL), bf16)] * 2,
        [place, dpack, w_qkv, rows, normed_one, sums_two, mixed] + grad_cols,
        scratch=[
            ((512, 576), bf16),
            ((3, 512, 192), bf16),
            ((4, 2, 64, WIDE), bf16),
            ((8, 96, TAIL), bf16),
            ((2, 4, 64, 192), bf16),
            ((8, 96, 640), bf16),
            ((2, 4, 64, WIDE), bf16),
            tok_rows,
            tok_rows,
        ],
        grant=24,
        place=True,
        far=(2, 3, 4, 6),
        far_outs=(0,),
        sems=5,
        cost=3,
    )
    grad_norm = lax.all_to_all(grad_norm, "uly", 0, 0, tiled=True)
    kept, sums, g_w_out, to_one, to_two, to_three = on_core(
        join_tail_kernel,
        [((96, 192), f32), ((8, 96), f32), ((96, 192), f32), ((96, 256), bf16), ((96, 256), bf16), ((8, 96), f32)],
        [place] + list(swap_sums(*sum_blk(keep, send))),
        place=True,
    )
    g_w_down = lax.ppermute(after(g_w_down, to_one), ("blk", "uly"), [(to, at) for at, to in DOWN_MOVES])
    g_w_qkv, d_vectors = on_core(
        finish_tail_kernel,
        [((96, 576), f32), ((8, 96), f32)],
        [place, kept, sums, swap_z(to_one, 1), swap_z(to_two, 2), swap_z(to_three, 3)],
        place=True,
    )
    (grad_inputs,) = on_core(
        finish_rows_kernel, [((2, 64, WIDE), f32)], [grad_norm, inputs, grad_middle, vectors]
    )
    return (
        output,
        grad_inputs,
        d_vectors[0],
        d_vectors[1],
        g_w_qkv,
        g_w_out,
        d_vectors[2],
        d_vectors[3],
        g_w_up,
        in_f32(g_w_down),
    )


def solution(mesh):
    local = local_fast if fits_fast(mesh) else local_general
    placed = (
        P(None, ("blk", "uly"), None),
        P(None, ("blk", "uly")),
        P(None, ("blk", "uly"), None),
        P("blk"),
        P("blk"),
        P("blk", "uly"),
        P("blk", "uly"),
        P("blk"),
        P("blk"),
        P("blk", "uly"),
        P("blk", "uly"),
    )
    return jax.shard_map(
        local,
        mesh=mesh,
        in_specs=placed,
        out_specs=(
            P(None, ("blk", "uly"), None),
            P(None, ("blk", "uly"), None),
            P("blk"),
            P("blk"),
            P("blk", "uly"),
            P("blk", "uly"),
            P("blk"),
            P("blk"),
            P("blk", "uly"),
            P("blk", "uly"),
        ),
        check_vma=False,
    )
```
